32 devices in a mesh: row: 8 (over z, y), col: 4 (over x, core).
Axes of the slice: x: 2, y: 2, z: 4, core: 2. Of those that a mesh axis runs over, the one named last changes fastest.
Arguments:
- coords: float32 [4, 3, 8, 4096], P(None, None, None, ('row', 'col')), may hold values from -6 to 6
- chrom_lengths: int32 [46], replicated, may hold values from 1 to 2048, 32768 in all
- band_counts: int32 [4, 8, 32, 32], P(None, None, ('row', 'col')), may hold values from 16 to 111
- inter_pairs: int32 [4, 1024, 2], replicated, may hold values from 0 to 255, as said below
- inter_counts: int32 [4, 1024], replicated, may hold values from 16 to 111
Outputs:
- grad: float32 [4, 3, 8, 4096], P(None, None, None, ('row', 'col'))
The draws below stay inside these ranges and needn't reach their ends.
Inputs may be any that keep to these rules, and one draw needn't show every extreme that they name: `inter_pairs`: every entry names two blocks of the structure. for every g in 0 to 7 and h in 0 to 3, at most 64 entries of one structure have (I mod 32) div 4 = g and J mod 4 = h, and one such (g, h) has exactly 64; the same holds with the roles of I and J exchanged.
All inputs are finite; a program needn't handle non-finite values.
Results may differ from the reference program's by a relative error of at most 0.0003.
Values sent between devices are 32-bit elements; how exact they have to be, the bound alone decides.
No kernel may reach another device: no remote copies, remote signals or barrier semaphores. Data moves between devices by JAX's collectives and lax.ppermute only.
A program may use at most 64 MiB of HBM per device.

```python
import math
import jax
import jax.numpy as jnp
import numpy as np
from jax import lax

STRUCTURES = 4
BLOCK = 128
BAND_BLOCKS = 31
SWEEPS = 8
CHROMOSOMES = 46
LIST_CAP = 64
GROUPS = 32
SWEEP_BEADS = 4096
BLOCKS = 256
BEADS = 32768
LISTED = 1024
N_COL = 4


def draw_inter_pairs(key, part):
    slot_count = GROUPS * LIST_CAP

    def owners(owner_key):
        key_order, key_favor = jax.random.split(owner_key)
        slot_order = jax.random.permutation(key_order, slot_count).astype(jnp.int32)
        favored = jax.random.randint(key_favor, (), 0, GROUPS)
        slot_score = slot_order + jnp.where(jnp.arange(slot_count) // LIST_CAP == favored, slot_count, 0).astype(jnp.int32)
        top_score, picked = lax.top_k(slot_score, LISTED)
        return (picked // LIST_CAP).astype(jnp.int32)

    def one_structure(member_key):
        key_first, key_second, key_mix, key_sweep_first, key_sweep_second = jax.random.split(member_key, 5)
        first_owner = owners(key_first)
        second_owner = jax.random.permutation(key_mix, owners(key_second))
        first_sweep = jax.random.randint(key_sweep_first, (LISTED,), 0, SWEEPS)
        second_sweep = jax.random.randint(key_sweep_second, (LISTED,), 0, SWEEPS)
        first_row = first_owner // N_COL
        first_col = first_owner % N_COL
        second_row = second_owner // N_COL
        second_col = second_owner % N_COL
        first_block = first_sweep * GROUPS + first_row * N_COL + second_col
        second_block = second_sweep * GROUPS + second_row * N_COL + first_col
        return jnp.stack([first_block, second_block], axis=-1)
    structure_keys = jax.random.split(jax.random.fold_in(key, 7), STRUCTURES)
    return jax.vmap(one_structure)(structure_keys).astype(jnp.int32)


def touch_ends(array, stream_key, low, largest):
    place = [jax.random.randint(jax.random.fold_in(stream_key, axis), (), 0, length) for axis, length in enumerate(array.shape)]
    widest = array.shape.index(max(array.shape))
    next_to = place[:widest] + [(place[widest] + 1) % array.shape[widest]] + place[widest + 1:]
    return array.at[tuple(place)].set(low).at[tuple(next_to)].set(largest)


def block_scale(rng, dims, cuts, low, largest):
    factor_of, own = 1.0, jax.random.fold_in(rng, 6)
    for position, parts in cuts:
        heights = jnp.exp(jax.random.uniform(jax.random.fold_in(own, position), (parts,), jnp.float32, low / len(cuts), largest / len(cuts)))
        factor_of = factor_of * jnp.repeat(heights, dims[position] // parts).reshape([-1 if axis == position else 1 for axis in range(len(dims))])
    return factor_of


def split_up(amount, total, bound, lean):
    loads = [(1 << 20) // math.isqrt(grade ** lean) + 1 for grade in range(2, amount + 1)]
    spare, counts = total - bound - (amount - 1), [1] * (amount - 1)
    while spare > 0:
        movable = [i for i in range(amount - 1) if counts[i] < bound]
        mass, left = sum([loads[i] for i in movable]), spare
        for i in movable:
            more = min(bound - counts[i], max(1, left * loads[i] // mass), spare)
            counts[i] = counts[i] + more
            spare = spare - more
    return np.array([bound] + counts)


def ragged_sizes(own_key, count, total, bound, lean):
    if count == 2:
        one = jax.random.randint(own_key, (), max(1, total - bound), min(bound, total - 1) + 1)
        return jnp.stack([one, total - one])
    sizes = jnp.asarray(split_up(count, total, bound, lean), jnp.int32)
    couples = (count - 1) // 2
    source_of, sink = sizes[1:1 + 2 * couples:2], sizes[2:2 + 2 * couples:2]
    margin = jnp.minimum(source_of - 1, bound - sink)
    moved = jax.random.randint(jax.random.fold_in(own_key, 1), (couples,), 0, 1 << 20) % (margin + 1)
    sizes = sizes.at[1:1 + 2 * couples:2].set(source_of - moved).at[2:2 + 2 * couples:2].set(sink + moved)
    return sizes[jax.random.permutation(jax.random.fold_in(own_key, 2), count)]


def gaussian(rng, dims, width, bound, cuts=(), held_as=jnp.bfloat16):
    drawn = width * jax.random.normal(rng, dims, jnp.float32)
    if cuts:
        drawn = drawn * block_scale(rng, dims, cuts, -0.22, 0.18)
    return jnp.clip(drawn, -bound, bound).astype(held_as)


def setup_inputs(seed: int = 0) -> dict:
    arg_keys = jax.random.split(jax.random.key(seed), 6)
    return {
        "coords": gaussian(arg_keys[0], (STRUCTURES, 3, SWEEPS, SWEEP_BEADS), 1.0, 6.0, ((3, 32),), jnp.float32),
        "chrom_lengths": ragged_sizes(arg_keys[1], CHROMOSOMES, BEADS, BEADS // 16, 2).astype(jnp.int32),
        "band_counts": touch_ends(jax.random.randint(arg_keys[2], (STRUCTURES, SWEEPS, GROUPS, BAND_BLOCKS + 1), 16, 112), jax.random.fold_in(arg_keys[2], 1), 16, 111).astype(jnp.int32),
        "inter_pairs": draw_inter_pairs(jax.random.fold_in(arg_keys[5], 71), 0),
        "inter_counts": touch_ends(jax.random.randint(arg_keys[4], (STRUCTURES, LISTED), 16, 112), jax.random.fold_in(arg_keys[4], 1), 16, 111).astype(jnp.int32),
    }


CONTACT_SHIFT = 3.0
CONTACT_SLOPE = 0.5
BACKGROUND = 0.5

def chromosome(beads, chrom_ends):
    return lax.optimization_barrier(jnp.sum((chrom_ends <= beads[..., None]).astype(jnp.int32), axis=-1)).astype(jnp.int32)

def pair_terms(first_points, second_points, pair_mask, tile_counts, tile_number):
    rows_here = first_points.shape[1]
    difference = first_points[:, :, None] - second_points[:, None, :]
    distance = lax.optimization_barrier(jnp.sum(difference * difference, axis=0))
    chance = jax.nn.sigmoid(CONTACT_SHIFT - CONTACT_SLOPE * distance)
    masked = chance * pair_mask
    expect = BACKGROUND + lax.optimization_barrier(jnp.sum(masked.reshape(rows_here, tile_number, BLOCK), axis=(0, 2))) / BLOCK
    weight = 1.0 - tile_counts.astype(jnp.float32) / expect
    factor = -2.0 * CONTACT_SLOPE / BLOCK * (masked * (1.0 - chance)).reshape(rows_here, tile_number, BLOCK) * weight[None, :, None]
    factor = factor.reshape(rows_here, tile_number * BLOCK)
    pair_force = factor[None] * difference
    return (lax.optimization_barrier(jnp.sum(pair_force, axis=2)), -lax.optimization_barrier(jnp.sum(pair_force, axis=1)))

def add_at(grad_total, block_start, addition):
    current = lax.dynamic_slice_in_dim(grad_total, block_start, addition.shape[1], 1)
    return lax.dynamic_update_slice_in_dim(grad_total, current + addition, block_start, 1)

def structure_grad(positions, labels, band, pair_ids, listed):
    band_span = (BAND_BLOCKS + 1) * BLOCK
    pad_extra = BAND_BLOCKS * BLOCK
    padded = jnp.concatenate([positions, jnp.zeros((3, pad_extra), jnp.float32)], axis=1)
    padded_labels = jnp.concatenate([labels, jnp.full((pad_extra,), -1, jnp.int32)])
    later_pair = jnp.arange(band_span)[None, :] > jnp.arange(BLOCK)[:, None]

    def band_step(grad_total, block_id):
        block_start = (block_id * BLOCK).astype(jnp.int32)
        first_points = lax.dynamic_slice_in_dim(padded, block_start, BLOCK, 1)
        second_points = lax.dynamic_slice_in_dim(padded, block_start, band_span, 1)
        left_chrom = lax.dynamic_slice_in_dim(padded_labels, block_start, BLOCK, 0)
        right_chrom = lax.dynamic_slice_in_dim(padded_labels, block_start, band_span, 0)
        pair_mask = ((left_chrom[:, None] == right_chrom[None, :]) & later_pair).astype(jnp.float32)
        gain_first, gain_second = pair_terms(first_points, second_points, pair_mask, band[block_id], BAND_BLOCKS + 1)
        grad_total = add_at(grad_total, block_start, gain_second)
        grad_total = add_at(grad_total, block_start, gain_first)
        return (grad_total, None)
    grad_total = jnp.zeros((3, BEADS + pad_extra), jnp.float32)
    grad_total, _ = lax.scan(band_step, grad_total, jnp.arange(BLOCKS, dtype=jnp.int32))
    grad_total = grad_total[:, :BEADS]

    def inter_step(grad_total, list_entry):
        block_pair, tile_count = list_entry
        first_start = (block_pair[0] * BLOCK).astype(jnp.int32)
        second_start = (block_pair[1] * BLOCK).astype(jnp.int32)
        first_points = lax.dynamic_slice_in_dim(positions, first_start, BLOCK, 1)
        second_points = lax.dynamic_slice_in_dim(positions, second_start, BLOCK, 1)
        left_chrom = lax.dynamic_slice_in_dim(labels, first_start, BLOCK, 0)
        right_chrom = lax.dynamic_slice_in_dim(labels, second_start, BLOCK, 0)
        pair_mask = (left_chrom[:, None] != right_chrom[None, :]).astype(jnp.float32)
        gain_first, gain_second = pair_terms(first_points, second_points, pair_mask, tile_count[None], 1)
        grad_total = add_at(grad_total, first_start, gain_first)
        grad_total = add_at(grad_total, second_start, gain_second)
        return (grad_total, None)
    grad_total, _ = lax.scan(inter_step, grad_total, (pair_ids, listed))
    return grad_total

def reference(coords, chrom_lengths, band_counts, inter_pairs, inter_counts):
    chrom_ends = jnp.cumsum(chrom_lengths).astype(jnp.int32)
    labels = chromosome(jnp.arange(BEADS, dtype=jnp.int32), chrom_ends)
    results = []
    for member in range(STRUCTURES):
        positions = coords[member].reshape(3, BEADS)
        band = band_counts[member].reshape(BLOCKS, BAND_BLOCKS + 1)
        member_grad = structure_grad(positions, labels, band, inter_pairs[member], inter_counts[member])
        results.append(member_grad.reshape(3, SWEEPS, SWEEP_BEADS))
    return jnp.stack(results)
```

```python
import functools

import jax
import jax.numpy as jnp
from jax import lax
from jax.experimental import pallas as pl
from jax.experimental.pallas import tpu as pltpu
from jax.sharding import PartitionSpec as P

CONTACT_SHIFT = 3.0
CONTACT_SLOPE = 0.5
BACKGROUND = 0.5
FAR = 32.0
UNIT = 8
POINT_ROWS = 16
VMEM = pl.BlockSpec(memory_space=pltpu.VMEM)
SMEM = pl.BlockSpec(memory_space=pltpu.SMEM)


def split(value):
    high = value.astype(jnp.bfloat16).astype(jnp.float32)
    return high, (value - high).astype(jnp.bfloat16).astype(jnp.float32)


def pack_kernel(n_col, coords_ref, counts_ref, *out_refs):
    structures = coords_ref.shape[0]
    width = counts_ref.shape[3]
    column_here = lax.axis_index("col")
    for k, out_ref in enumerate(out_refs):
        member = lax.rem(lax.rem(column_here + k, n_col), structures)
        out_ref[0:3] = coords_ref[member]
        out_ref[3] = jnp.zeros(out_ref.shape[1:], jnp.float32)
        out_ref[3, :, 0:width] = counts_ref[member][:, 0, :].astype(jnp.float32)


def list_kernel(sizes, reach_ref, pairs_ref, code_ref, place_ref, number_ref):
    n_row, n_col, structures, sweeps = sizes
    groups = n_row * n_col
    blocks = groups * sweeps
    slots = structures * sweeps
    family = lax.axis_index("row") * (n_col // structures) + lax.axis_index("col") // structures
    base = family * structures

    def at(block):
        return lax.rem(block, groups) * sweeps + lax.div(block, groups)

    def idle(position, carry):
        code_ref[position] = slots * (1 << 19)
        place_ref[position] = 0
        return carry

    lax.fori_loop(0, UNIT, idle, 0)

    def band(slot, number):
        block = lax.rem(slot, sweeps) * groups + base + lax.div(slot, sweeps)
        low = reach_ref[0, slot]
        high = reach_ref[1, slot]

        def add(other, number):
            first = jnp.minimum(block, other)
            code_ref[number] = at(other) + slot * (1 << 12) + slot * (1 << 19)
            place_ref[number] = at(first) * 128 + jnp.abs(block - other)
            return number + 1

        return lax.fori_loop(low, high + 1, add, number)

    number = lax.fori_loop(0, slots, band, jnp.int32(UNIT))

    def listed(step, number):
        for inner in range(8):
            entry = step * 8 + inner
            first = pairs_ref[0, entry]
            second = pairs_ref[1, entry]
            for block, other in ((first, second), (second, first)):
                slot = lax.rem(block, structures) * sweeps + lax.div(block, groups)
                code_ref[number] = at(other) + (slots + slot) * (1 << 12) + slot * (1 << 19)
                place_ref[number] = blocks * 128 + entry
                mine = lax.div(lax.rem(block, groups), structures) == family
                number = number + mine.astype(jnp.int32)
        return number

    number = lax.fori_loop(0, pairs_ref.shape[1] // 8, listed, number)
    lax.fori_loop(number, number + 2 * UNIT, idle, 0)
    number_ref[0] = lax.div(number - 1, UNIT)


def tile_kernel(
    sizes,
    code_ref,
    place_ref,
    number_ref,
    starts_ref,
    ends_ref,
    listed_ref,
    *refs,
):
    n_row, n_col, structures, sweeps = sizes
    groups = n_row * n_col
    blocks = groups * sweeps
    slots = structures * sweeps
    piece_refs = refs[:n_row]
    out_refs = refs[n_row : n_row + structures]
    second_ref, first_ref, counts_ref, rows_ref, own_ref, held_ref, sums_ref, picks_ref, diag_ref, total_ref = refs[
        n_row + structures :
    ]
    labels = starts_ref.shape[0]
    depth = 2 * POINT_ROWS + labels
    row_here = lax.axis_index("row")
    column_here = lax.axis_index("col")
    share = lax.div(column_here, structures)
    place_here = lax.rem(column_here, structures)
    lane = lax.broadcasted_iota(jnp.int32, (1, 128), 1)

    def member(block):
        bead = block * 128 + lane
        inside = (bead >= starts_ref[...]) & (bead < ends_ref[...])
        return inside.astype(jnp.float32)

    def points(piece_ref, turn):
        parts = [split(piece_ref[turn, k]) for k in range(3)]
        near = [high + low for high, low in parts]
        norm = -0.5 * CONTACT_SLOPE * (near[0] * near[0] + near[1] * near[1] + near[2] * near[2])
        return parts, norm

    row = lax.broadcasted_iota(jnp.int32, (POINT_ROWS, 128), 0)
    fixed = jnp.where((row == 4) | (row == 5), 1.0, 0.0)
    for u in range(sweeps):
        rows_ref[u * POINT_ROWS : (u + 1) * POINT_ROWS] = fixed
    for k in range(n_row):
        origin = lax.rem(row_here + (n_row - k), n_row)

        def prepare(turn, carry, k=k, origin=origin):
            column = lax.rem(column_here + (n_col - turn), n_col)
            group = origin * n_col + column
            parts, norm = points(piece_refs[k], turn)
            for place, (high, low) in enumerate(parts + [split(norm)]):
                rows_ref[pl.ds(place, sweeps, stride=POINT_ROWS), :] = high
                rows_ref[pl.ds(place + 8, sweeps, stride=POINT_ROWS), :] = low
            counts_ref[pl.ds(pl.multiple_of(group * sweeps, sweeps), sweeps), :] = piece_refs[k][turn, 3]
            for u in range(sweeps):
                features = rows_ref[u * POINT_ROWS : (u + 1) * POINT_ROWS].astype(jnp.bfloat16)
                at = group * sweeps + u
                second_ref[at, 0:POINT_ROWS] = features
                second_ref[at, POINT_ROWS : 2 * POINT_ROWS] = features
                second_ref[at, 2 * POINT_ROWS : depth] = member(u * groups + group).astype(jnp.bfloat16)
            return carry

        lax.fori_loop(0, n_col, prepare, 0)
    counts_ref[blocks : blocks + listed_ref.shape[0]] = listed_ref[...].astype(jnp.float32)

    row = lax.broadcasted_iota(jnp.int32, (2 * POINT_ROWS, 128), 0)
    fixed = jnp.where((row == 3) | (row == 11), 1.0, jnp.where(row == 5, -FAR, 0.0))
    for u in range(sweeps):
        own_ref[u * 2 * POINT_ROWS : (u + 1) * 2 * POINT_ROWS] = fixed
    turned = jnp.where(lane == 5, 0.0, jnp.where(lane >= 2 * POINT_ROWS, -1.0, 1.0))

    def own(near_column, carry):
        column = share * structures + near_column
        turn = lax.rem(column_here - column + n_col, n_col)
        parts, norm = points(piece_refs[0], turn)
        for place, (high, low) in enumerate(parts):
            for at, value in ((place, high), (place + 8, high), (place + 16, low), (place + 24, low)):
                own_ref[pl.ds(at, sweeps, stride=2 * POINT_ROWS), :] = CONTACT_SLOPE * value
        high, low = split(norm + 0.5 * CONTACT_SHIFT)
        own_ref[pl.ds(4, sweeps, stride=2 * POINT_ROWS), :] = high
        own_ref[pl.ds(20, sweeps, stride=2 * POINT_ROWS), :] = low
        for u in range(sweeps):
            block = u * groups + row_here * n_col + column
            features = jnp.concatenate(
                [
                    own_ref[u * 2 * POINT_ROWS : (u + 1) * 2 * POINT_ROWS],
                    FAR * member(block),
                    jnp.zeros((128 - depth, 128), jnp.float32),
                ],
                axis=0,
            )
            features = jnp.transpose(features)
            slot = near_column * sweeps + u
            first_ref[slot] = features[:, :depth].astype(jnp.bfloat16)
            first_ref[slots + slot] = (features * turned)[:, :depth].astype(jnp.bfloat16)
        return carry

    lax.fori_loop(0, structures, own, 0)

    total_ref[...] = jnp.zeros_like(total_ref)
    spare = 1.0 / (1.0 + jnp.exp(jnp.float32(-CONTACT_SHIFT)))

    def step(turn, carry):
        start = turn * UNIT
        codes = [code_ref[start + t] for t in range(UNIT)]
        sums = sums_ref[pl.ds(0, UNIT, stride=8), :]
        for k in range(1, 8):
            sums = sums + sums_ref[pl.ds(k, UNIT, stride=8), :]
        chance = 64.0 * 128.0 + 0.5 * jnp.sum(sums, axis=1, keepdims=True)
        count = jnp.sum(picks_ref[...], axis=1, keepdims=True)
        chance = jnp.where(diag_ref[...] > 0.5, 0.5 * (chance - 128.0 * spare), chance)
        weight = 1.0 - count / (BACKGROUND + chance / 128.0)
        for t in range(0, UNIT, 2):
            left, right = (second_ref[codes[t + i] & 4095, 0:POINT_ROWS] for i in range(2))
            product = lax.dot_general(
                jnp.concatenate([left, right], axis=0),
                held_ref[t * 128 : (t + 2) * 128],
                (((1,), (1,)), ((), ())),
                preferred_element_type=jnp.float32,
            )
            for i in range(2):
                gain = product[i * POINT_ROWS : (i + 1) * POINT_ROWS, i * 128 : (i + 1) * 128]
                at = pl.multiple_of((codes[t + i] >> 19) * POINT_ROWS, POINT_ROWS)
                total_ref[pl.ds(at, POINT_ROWS), :] += weight[t + i : t + i + 1] * gain
        for t in range(UNIT):
            code = code_ref[start + UNIT + t]
            place = place_ref[start + UNIT + t]
            logit = jnp.dot(
                first_ref[(code >> 12) & 127],
                second_ref[code & 4095],
                preferred_element_type=jnp.float32,
            )
            bend = jnp.tanh(logit)
            sums_ref[t * 8 : (t + 1) * 8] = jnp.sum(bend.reshape(16, 8, 128), axis=0)
            held_ref[t * 128 : (t + 1) * 128] = (1.0 - bend * bend).astype(jnp.bfloat16)
            picked = counts_ref[pl.ds(place >> 7, 1), :]
            picks_ref[t : t + 1] = jnp.where(lane == (place & 127), picked, 0.0)
            band = ((code >> 12) & 127) < slots
            diagonal = band & ((place & 127) == 0)
            diag_ref[t : t + 1] = jnp.full((1, 128), diagonal.astype(jnp.float32))
        return carry

    lax.fori_loop(0, number_ref[0] + 1, step, 0)

    scale = -2.0 * CONTACT_SLOPE / 128.0 / 4.0
    for k in range(structures):
        near_column = lax.rem(place_here + k, structures)
        turn = lax.rem(place_here - near_column + n_col, n_col)
        first = near_column * sweeps * POINT_ROWS
        mass = total_ref[pl.ds(first + 4, sweeps, stride=POINT_ROWS), :]
        for place in range(3):
            high, low = split(piece_refs[0][turn, place])
            pull = (
                total_ref[pl.ds(first + place, sweeps, stride=POINT_ROWS), :]
                + total_ref[pl.ds(first + place + 8, sweeps, stride=POINT_ROWS), :]
            )
            out_refs[k][place] = scale * ((high + low) * mass - pull)


def on_device(n_row, n_col, coords, chrom_lengths, band_counts, inter_pairs, inter_counts):
    structures, _, sweeps, block_size = coords.shape
    band_reach = band_counts.shape[3] - 1
    listed = inter_pairs.shape[1]
    groups = n_row * n_col
    blocks = groups * sweeps
    slots = structures * sweeps
    sizes = (n_row, n_col, structures, sweeps)
    row_here = lax.axis_index("row")
    column_here = lax.axis_index("col")
    member = column_here % structures

    messages = pl.pallas_call(
        functools.partial(pack_kernel, n_col),
        out_shape=[jax.ShapeDtypeStruct((4, sweeps, block_size), jnp.float32)] * n_col,
        in_specs=[VMEM, VMEM],
        out_specs=[VMEM] * n_col,
        name="pack",
    )(coords, band_counts)
    received = [messages[0]]
    for k in range(1, n_col):
        received.append(lax.ppermute(messages[k], "col", [(i, (i + k) % n_col) for i in range(n_col)]))
    own_row = jnp.stack(received)
    pieces = [own_row]
    for k in range(1, n_row):
        pieces.append(lax.ppermute(own_row, "row", [(i, (i + k) % n_row) for i in range(n_row)]))

    chromosomes = chrom_lengths.shape[0]
    numbers = jnp.arange(chromosomes)
    ends = jnp.sum(jnp.where(numbers[None, :] <= numbers[:, None], chrom_lengths[None, :], 0), axis=1)
    starts = ends - chrom_lengths
    slot = jnp.arange(slots)
    block = (
        slot % sweeps * groups
        + row_here * n_col
        + column_here // structures * structures
        + slot // sweeps
    )
    first_bead = block * block_size
    last_bead = first_bead + block_size - 1
    low = jnp.max(jnp.where(starts[None, :] <= first_bead[:, None], starts[None, :], 0), axis=1)
    high = jnp.min(
        jnp.where(ends[None, :] > last_bead[:, None], ends[None, :], blocks * block_size), axis=1
    )
    low = jnp.maximum(low // block_size, block - band_reach)
    high = jnp.minimum(jnp.minimum((high - 1) // block_size, block + band_reach), blocks - 1)
    reach = jnp.stack([low, high]).astype(jnp.int32)
    pairs = jnp.transpose(lax.dynamic_index_in_dim(inter_pairs, member, 0, keepdims=False))
    capacity = slots * (2 * band_reach + 1) + 2 * listed + 4 * UNIT
    code, place, number = pl.pallas_call(
        functools.partial(list_kernel, sizes),
        out_shape=[
            jax.ShapeDtypeStruct((capacity,), jnp.int32),
            jax.ShapeDtypeStruct((capacity,), jnp.int32),
            jax.ShapeDtypeStruct((1,), jnp.int32),
        ],
        in_specs=[SMEM, SMEM],
        out_specs=[SMEM] * 3,
        name="list_tiles",
    )(reach, pairs)

    labels = -(-chromosomes // 16) * 16
    spread = [
        jnp.broadcast_to(jnp.pad(edge, (0, labels - chromosomes))[:, None], (labels, block_size))
        for edge in (starts, ends)
    ]
    counts = lax.dynamic_index_in_dim(inter_counts, member, 0, keepdims=False)
    counts = counts.reshape(listed // block_size, block_size)
    depth = 2 * POINT_ROWS + labels
    gains = pl.pallas_call(
        functools.partial(tile_kernel, sizes),
        out_shape=[jax.ShapeDtypeStruct((3, sweeps, block_size), jnp.float32)] * structures,
        in_specs=[SMEM] * 3 + [VMEM] * (3 + n_row),
        out_specs=[VMEM] * structures,
        scratch_shapes=[
            pltpu.VMEM((blocks, depth, block_size), jnp.bfloat16),
            pltpu.VMEM((2 * slots, block_size, depth), jnp.bfloat16),
            pltpu.VMEM((blocks + listed // block_size, block_size), jnp.float32),
            pltpu.VMEM((sweeps * POINT_ROWS, block_size), jnp.float32),
            pltpu.VMEM((sweeps * 2 * POINT_ROWS, block_size), jnp.float32),
            pltpu.VMEM((UNIT * block_size, block_size), jnp.bfloat16),
            pltpu.VMEM((UNIT * 8, block_size), jnp.float32),
            pltpu.VMEM((UNIT, block_size), jnp.float32),
            pltpu.VMEM((UNIT, block_size), jnp.float32),
            pltpu.VMEM(((slots + 1) * POINT_ROWS, block_size), jnp.float32),
        ],
        compiler_params=pltpu.CompilerParams(vmem_limit_bytes=50 * 1024 * 1024),
        name="tiles",
    )(code, place, number, *spread, counts, *pieces)

    arrived = [gains[0]]
    for k in range(1, structures):
        moves = [
            (base + i, base + (i + k) % structures)
            for base in range(0, n_col, structures)
            for i in range(structures)
        ]
        arrived.append(lax.ppermute(gains[k], "col", moves))
    stacked = jnp.stack(arrived)
    order = (member - jnp.arange(structures)) % structures
    return jnp.take(stacked, order, axis=0)


def solution(mesh):
    placed = (
        P(None, None, None, ("row", "col")),
        P(),
        P(None, None, ("row", "col"), None),
        P(),
        P(),
    )
    return jax.shard_map(
        functools.partial(on_device, mesh.shape["row"], mesh.shape["col"]),
        mesh=mesh,
        in_specs=placed,
        out_specs=P(None, None, None, ("row", "col")),
        check_vma=False,
    )
```

```python
import functools

import jax
import jax.numpy as jnp
from jax import lax
from jax.experimental import pallas as pl
from jax.experimental.pallas import tpu as pltpu
from jax.sharding import PartitionSpec as P

CONTACT_SHIFT = 3.0
CONTACT_SLOPE = 0.5
BACKGROUND = 0.5
FAR = 32.0
UNIT = 8
POINT_ROWS = 16
AXES = ("row", "col")
VMEM = pl.BlockSpec(memory_space=pltpu.VMEM)
SMEM = pl.BlockSpec(memory_space=pltpu.SMEM)
ANY = pl.BlockSpec(memory_space=pl.ANY)


def rounded(value):
    return value.astype(jnp.bfloat16).astype(jnp.float32)


def divide(value, by):
    return value >> (by.bit_length() - 1) if by & (by - 1) == 0 else lax.div(value, by)


def modulo(value, by):
    return value & (by - 1) if by & (by - 1) == 0 else lax.rem(value, by)


class Sizes:
    def __init__(self, n_row, n_col, structures, sweeps, width):
        self.n_row, self.n_col, self.structures, self.sweeps = n_row, n_col, structures, sweeps
        self.width = width
        self.share = n_row // structures
        self.plane = self.share * n_col
        self.chips = self.plane // 2
        self.half = n_col // 2
        self.groups = n_row * n_col
        self.blocks = self.groups * sweeps
        self.slots = structures * sweeps
        self.rows = self.slots * 4 + sweeps

    def at(self, block):
        return modulo(block, self.groups) * self.sweeps + divide(block, self.groups)


def pack_kernel(sizes, coords_ref, counts_ref, *out_refs):
    sweeps, width = sizes.sweeps, sizes.width
    family = lax.div(lax.axis_index("row"), sizes.share)
    lane = lax.broadcasted_iota(jnp.int32, (width, 128), 1)
    place = lax.broadcasted_iota(jnp.int32, (width, 128), 0) + family * width
    spread = (lane == place).astype(jnp.float32)
    for k, out_ref in enumerate(out_refs):
        member = lax.rem(family + k, sizes.structures)
        norm = jnp.zeros((sweeps, 128), jnp.float32)
        for place in range(3):
            point = coords_ref[member, place]
            out_ref[pl.ds(place, sweeps, stride=4), :] = point
            high = rounded(point)
            near = high + rounded(point - high)
            norm = norm - 0.5 * CONTACT_SLOPE * near * near
        out_ref[pl.ds(3, sweeps, stride=4), :] = norm
        counts = counts_ref[member][:, 0, :].astype(jnp.float32)
        out_ref[4 * sweeps : 5 * sweeps] = jnp.dot(counts, spread, preferred_element_type=jnp.float32)


def merge_kernel(points, *refs):
    counts = refs[0][points:]
    for k, ref in enumerate(refs[:-1]):
        refs[-1][k * points : (k + 1) * points] = ref[:points]
        counts = counts + ref[points:] if k else counts
    refs[-1][(len(refs) - 1) * points :] = counts


def join_kernel(*refs):
    rows = refs[0].shape[0]
    for k, ref in enumerate(refs[:-1]):
        refs[-1][k * rows : (k + 1) * rows] = ref[...]


def list_kernel(sizes, bits, reach_ref, keys_ref, mine_ref, after_ref, code_ref, place_ref, number_ref):
    slots, sweeps, groups = sizes.slots, sizes.sweeps, sizes.groups
    entry_bits, block_bits = bits
    here = lax.rem(lax.axis_index("row"), sizes.share) * sizes.n_col + lax.axis_index("col")

    def idle(position, carry):
        code_ref[position] = slots << 19
        place_ref[position] = 0
        return carry

    lax.fori_loop(0, UNIT, idle, 0)

    def band(slot, number):
        block = modulo(slot, sweeps) * groups + divide(slot, sweeps) * sizes.plane + here

        def add(other, number):
            first = jnp.minimum(block, other)
            group = modulo(first, groups)
            row = modulo(group, sizes.plane) * sweeps + divide(first, groups)
            code_ref[number] = sizes.at(other) + (slot << 12) + (slot << 19)
            place_ref[number] = (
                row * 128 + divide(group, sizes.plane) * sizes.width + jnp.abs(block - other)
            )
            return number + 1

        return lax.fori_loop(reach_ref[0, slot], reach_ref[1, slot] + 1, add, number)

    number = lax.fori_loop(0, slots, band, jnp.int32(UNIT))
    base = sizes.plane * sweeps * 128
    for side in range(2):

        def add(entry, number, side=side):
            key = keys_ref[side, entry]
            slot = key >> (entry_bits + block_bits)
            other = (key >> entry_bits) & ((1 << block_bits) - 1)
            code_ref[number] = other + ((slots + slot) << 12) + (slot << 19)
            place_ref[number] = base + (key & ((1 << entry_bits) - 1))
            return number + 1

        number = lax.fori_loop(0, mine_ref[side], add, number)
    lax.fori_loop(number, number + 2 * UNIT, idle, 0)
    number_ref[0] = lax.div(number - 1, UNIT)


def marks_kernel(sizes, starts_ref, ends_ref, out_ref):
    lane = lax.broadcasted_iota(jnp.int32, (1, 128), 1)

    def mark(group, carry):
        for u in range(sizes.sweeps):
            bead = (u * sizes.groups + group) * 128 + lane
            inside = (bead >= starts_ref[...]) & (bead < ends_ref[...])
            out_ref[group * sizes.sweeps + u] = inside.astype(jnp.float32).astype(jnp.bfloat16)
        return carry

    lax.fori_loop(0, sizes.groups, mark, 0)


def own_kernel(sizes, own_ref, starts_ref, ends_ref, out_ref):
    slots, sweeps = sizes.slots, sizes.sweeps
    family = lax.div(lax.axis_index("row"), sizes.share)
    here = lax.rem(lax.axis_index("row"), sizes.share) * sizes.n_col + lax.axis_index("col")
    lane = lax.broadcasted_iota(jnp.int32, (1, 128), 1)
    row = lax.broadcasted_iota(jnp.int32, (8, 128), 0)
    labels = starts_ref.shape[0]
    depth = POINT_ROWS + labels

    def fill(turn, carry):
        origin = lax.rem(family + (sizes.structures - turn), sizes.structures)
        for pair in range(sweeps // 2):
            value = own_ref[pl.ds(pl.multiple_of(turn * sweeps * 4 + pair * 8, 8), 8), :]
            for odd in range(2):
                value = pltpu.roll(value, 4, 0) if odd else value
                high = rounded(value)
                low = rounded(value - high)
                shifted = value + 0.5 * CONTACT_SHIFT
                shifted_high = rounded(shifted)
                shifted_low = rounded(shifted - shifted_high)
                both = jnp.where(row < 4, high, pltpu.roll(high, 4, 0))
                near = jnp.where((row & 3) == 3, 1.0, CONTACT_SLOPE * both)
                rest = jnp.where(row == 4, pltpu.roll(shifted_low, 1, 0), 0.0)
                rest = jnp.where(row == 3, shifted_high, rest)
                rest = jnp.where(row < 3, CONTACT_SLOPE * low, rest)
                u = 2 * pair + odd
                bead = (u * sizes.groups + origin * sizes.plane + here) * 128 + lane
                inside = (bead >= starts_ref[...]) & (bead < ends_ref[...])
                apart = jnp.where(inside, 0.0, -FAR)
                blank = jnp.zeros((128 - depth, 128), jnp.float32)
                turned = jnp.transpose(jnp.concatenate([near, rest, apart, blank], axis=0))
                slot = origin * sweeps + u
                out_ref[slot] = turned[:, :depth].astype(jnp.bfloat16)
                other = jnp.where(lane < POINT_ROWS, turned, -FAR - turned)
                out_ref[slots + slot] = other[:, :depth].astype(jnp.bfloat16)
        return carry

    lax.fori_loop(0, sizes.structures, fill, 0)


def tile_kernel(
    sizes,
    code_ref,
    place_ref,
    number_ref,
    listed_ref,
    first_ref,
    marks_ref,
    same_ref,
    across_ref,
    *refs,
):
    structures, sweeps, slots = sizes.structures, sizes.sweeps, sizes.slots
    out_refs = refs[:structures]
    second_ref, counts_ref, held_ref, sums_ref, picks_ref, diag_ref, total_ref = refs[structures:]
    row_here = lax.axis_index("row")
    column_here = lax.axis_index("col")
    family = lax.div(row_here, sizes.share)
    chip_here = lax.rem(row_here, sizes.share) * sizes.half + lax.div(column_here, 2)
    core_here = lax.rem(column_here, 2)
    lane = lax.broadcasted_iota(jnp.int32, (1, 128), 1)
    row = lax.broadcasted_iota(jnp.int32, (8, 128), 0)
    ones = jnp.where((row == 3) | (row == 4), 1.0, 0.0)

    for core, piece_ref in ((core_here, same_ref), (1 - core_here, across_ref)):
        for k in range(sizes.chips):
            chip = lax.rem(chip_here + (sizes.chips - k), sizes.chips)
            device = chip * 2 + core
            base = k * sizes.rows
            counts_ref[pl.ds(pl.multiple_of(device * sweeps, sweeps), sweeps), :] = piece_ref[
                base + slots * 4 : base + slots * 4 + sweeps
            ]
            for turn in range(structures):
                origin = lax.rem(family + (structures - turn), structures)
                at = (origin * sizes.plane + device) * sweeps
                for pair in range(sweeps // 2):
                    start = base + turn * sweeps * 4 + pair * 8
                    value = piece_ref[start : start + 8]
                    high = rounded(value)
                    low = value - high
                    high_turned = pltpu.roll(high, 4, 0)
                    even = jnp.concatenate(
                        [jnp.where(row < 4, high, pltpu.roll(low, 4, 0)), jnp.where(row < 3, high, ones)],
                        axis=0,
                    )
                    odd = jnp.concatenate(
                        [jnp.where(row < 4, high_turned, low), jnp.where(row < 3, high_turned, ones)],
                        axis=0,
                    )
                    second_ref[at + 2 * pair] = even.astype(jnp.bfloat16)
                    second_ref[at + 2 * pair + 1] = odd.astype(jnp.bfloat16)
    listed_base = sizes.plane * sweeps
    counts_ref[listed_base : listed_base + listed_ref.shape[0]] = listed_ref[...].astype(jnp.float32)

    total_ref[...] = jnp.zeros_like(total_ref)
    spare = 1.0 / (1.0 + jnp.exp(jnp.float32(-CONTACT_SHIFT)))

    def step(turn, carry):
        start = turn * UNIT
        codes = [code_ref[start + t] for t in range(UNIT)]
        sums = sums_ref[pl.ds(0, UNIT, stride=8), :]
        for k in range(1, 8):
            sums = sums + sums_ref[pl.ds(k, UNIT, stride=8), :]
        chance = 64.0 * 128.0 + 0.5 * jnp.sum(sums, axis=1, keepdims=True)
        count = jnp.sum(picks_ref[...], axis=1, keepdims=True)
        chance = jnp.where(diag_ref[...] > 0.5, 0.5 * (chance - 128.0 * spare), chance)
        weight = 1.0 - count / (BACKGROUND + chance / 128.0)
        for t in range(0, UNIT, 2):
            left, right = (second_ref[codes[t + i] & 4095] for i in range(2))
            product = lax.dot_general(
                jnp.concatenate([left, right], axis=0),
                held_ref[t * 128 : (t + 2) * 128],
                (((1,), (1,)), ((), ())),
                preferred_element_type=jnp.float32,
            )
            for i in range(2):
                gain = product[i * POINT_ROWS : (i + 1) * POINT_ROWS, i * 128 : (i + 1) * 128]
                at = pl.multiple_of((codes[t + i] >> 19) * POINT_ROWS, POINT_ROWS)
                total_ref[pl.ds(at, POINT_ROWS), :] += weight[t + i : t + i + 1] * gain
        for t in range(UNIT):
            code = code_ref[start + UNIT + t]
            place = place_ref[start + UNIT + t]
            second = code & 4095
            logit = jnp.dot(
                first_ref[(code >> 12) & 127],
                jnp.concatenate([second_ref[second], marks_ref[second]], axis=0),
                preferred_element_type=jnp.float32,
            )
            bend = jnp.tanh(logit)
            sums_ref[t * 8 : (t + 1) * 8] = jnp.sum(bend.reshape(16, 8, 128), axis=0)
            held_ref[t * 128 : (t + 1) * 128] = (1.0 - bend * bend).astype(jnp.bfloat16)
            picked = counts_ref[pl.ds(place >> 7, 1), :]
            picks_ref[t : t + 1] = jnp.where(lane == (place & 127), picked, 0.0)
            band = ((code >> 12) & 127) < slots
            diagonal = band & ((place & (sizes.width - 1)) == 0)
            diag_ref[t : t + 1] = jnp.full((1, 128), diagonal.astype(jnp.float32))
        return carry

    lax.fori_loop(0, number_ref[0] + 1, step, 0)

    scale = -2.0 * CONTACT_SLOPE / 128.0 / 4.0
    for k in range(structures):
        origin = lax.rem(family + k, structures)
        turn = (structures - k) % structures
        first = origin * sweeps * POINT_ROWS
        mass = total_ref[pl.ds(first + 11, sweeps, stride=POINT_ROWS), :]
        for place in range(3):
            point = same_ref[pl.ds(turn * sweeps * 4 + place, sweeps, stride=4), :]
            high = rounded(point)
            near = high + rounded(point - high)
            pull = (
                total_ref[pl.ds(first + place, sweeps, stride=POINT_ROWS), :]
                + total_ref[pl.ds(first + place + 4, sweeps, stride=POINT_ROWS), :]
            )
            out_refs[k][place] = scale * (near * mass - pull)


def place_kernel(sizes, *refs):
    family = lax.div(lax.axis_index("row"), sizes.share)
    for k, ref in enumerate(refs[:-1]):
        refs[-1][lax.rem(family + (sizes.structures - k), sizes.structures)] = ref[...]


def on_device(n_row, n_col, coords, chrom_lengths, band_counts, inter_pairs, inter_counts):
    structures, _, sweeps, block_size = coords.shape
    width = band_counts.shape[3]
    band_reach = width - 1
    listed = inter_pairs.shape[1]
    sizes = Sizes(n_row, n_col, structures, sweeps, width)
    share, groups, slots, blocks = sizes.share, sizes.groups, sizes.slots, sizes.blocks
    row_here = lax.axis_index("row")
    column_here = lax.axis_index("col")
    member = row_here // share
    here = row_here % share * n_col + column_here

    messages = pl.pallas_call(
        functools.partial(pack_kernel, sizes),
        out_shape=[jax.ShapeDtypeStruct((5 * sweeps, block_size), jnp.float32)] * structures,
        in_specs=[VMEM, VMEM],
        out_specs=[VMEM] * structures,
        name="pack",
    )(coords, band_counts)
    deal = [
        [(i, (i // share + k) % structures * share + i % share) for i in range(n_row)]
        for k in range(structures)
    ]
    received = [messages[0]]
    for k in range(1, structures):
        received.append(lax.ppermute(messages[k], "row", deal[k]))
    own_row = pl.pallas_call(
        functools.partial(merge_kernel, 4 * sweeps),
        out_shape=jax.ShapeDtypeStruct((sizes.rows, block_size), jnp.float32),
        in_specs=[VMEM] * structures,
        out_specs=VMEM,
        name="merge",
    )(*received)

    def device(family, chip, core):
        row = family * share + chip // sizes.half
        return row * n_col + chip % sizes.half * 2 + core

    pieces = [own_row]
    for k in range(1, sizes.chips):
        moves = [
            (device(f, i, core), device(f, (i + k) % sizes.chips, core))
            for f in range(structures)
            for i in range(sizes.chips)
            for core in range(2)
        ]
        pieces.append(lax.ppermute(own_row, AXES, moves))
    same = pl.pallas_call(
        join_kernel,
        out_shape=jax.ShapeDtypeStruct((sizes.chips * sizes.rows, block_size), jnp.float32),
        in_specs=[VMEM] * sizes.chips,
        out_specs=VMEM,
        name="join",
    )(*pieces)
    across = lax.ppermute(same, "col", [(i, i ^ 1) for i in range(n_col)])

    chromosomes = chrom_lengths.shape[0]
    numbers = jnp.arange(chromosomes)
    ends = jnp.sum(jnp.where(numbers[None, :] <= numbers[:, None], chrom_lengths[None, :], 0), axis=1)
    starts = ends - chrom_lengths
    slot = jnp.arange(slots)
    block = slot % sweeps * groups + slot // sweeps * sizes.plane + here
    first_bead = block * block_size
    last_bead = first_bead + block_size - 1
    low = jnp.max(jnp.where(starts[None, :] <= first_bead[:, None], starts[None, :], 0), axis=1)
    high = jnp.min(
        jnp.where(ends[None, :] > last_bead[:, None], ends[None, :], blocks * block_size), axis=1
    )
    low = jnp.maximum(low // block_size, block - band_reach)
    high = jnp.minimum(jnp.minimum((high - 1) // block_size, block + band_reach), blocks - 1)
    reach = jnp.stack([low, high]).astype(jnp.int32)
    pairs = jnp.transpose(lax.dynamic_index_in_dim(inter_pairs, member, 0, keepdims=False))
    others = pairs[::-1]
    entry_bits = (listed - 1).bit_length()
    block_bits = (blocks - 1).bit_length()
    group = modulo(pairs, groups)
    mine = modulo(group, sizes.plane) == here
    pair_slot = divide(group, sizes.plane) * sweeps + divide(pairs, groups)
    keys = (
        (pair_slot << (entry_bits + block_bits))
        + (sizes.at(others) << entry_bits)
        + jnp.arange(listed, dtype=jnp.int32)[None, :]
    )
    keys = lax.sort(jnp.where(mine, keys, jnp.int32((1 << 31) - 1)), dimension=1, is_stable=False)
    mine = jnp.sum(mine.astype(jnp.int32), axis=1)
    capacity = slots * (2 * band_reach + 1) + 2 * listed + 4 * UNIT
    code, place, number = pl.pallas_call(
        functools.partial(list_kernel, sizes, (entry_bits, block_bits)),
        out_shape=[
            jax.ShapeDtypeStruct((capacity,), jnp.int32),
            jax.ShapeDtypeStruct((capacity,), jnp.int32),
            jax.ShapeDtypeStruct((1,), jnp.int32),
        ],
        in_specs=[SMEM, SMEM, SMEM, ANY],
        out_specs=[SMEM] * 3,
        cost_estimate=pl.CostEstimate(flops=1 << 30, bytes_accessed=1 << 23, transcendentals=0),
        name="list_tiles",
    )(reach, keys, mine, own_row)

    labels = -(-chromosomes // 16) * 16
    depth = POINT_ROWS + labels
    spread = [
        jnp.broadcast_to(jnp.pad(edge, (0, labels - chromosomes))[:, None], (labels, block_size))
        for edge in (starts, ends)
    ]
    marks = pl.pallas_call(
        functools.partial(marks_kernel, sizes),
        out_shape=jax.ShapeDtypeStruct((blocks, labels, block_size), jnp.bfloat16),
        in_specs=[VMEM] * 2,
        out_specs=VMEM,
        cost_estimate=pl.CostEstimate(flops=1 << 30, bytes_accessed=1 << 23, transcendentals=0),
        compiler_params=pltpu.CompilerParams(vmem_limit_bytes=24 * 1024 * 1024),
        name="marks",
    )(*spread)
    own = pl.pallas_call(
        functools.partial(own_kernel, sizes),
        out_shape=jax.ShapeDtypeStruct((2 * slots, block_size, depth), jnp.bfloat16),
        in_specs=[VMEM] * 3,
        out_specs=VMEM,
        cost_estimate=pl.CostEstimate(flops=1 << 30, bytes_accessed=1 << 23, transcendentals=0),
        compiler_params=pltpu.CompilerParams(vmem_limit_bytes=24 * 1024 * 1024),
        name="own_features",
    )(own_row, *spread)

    counts = lax.dynamic_index_in_dim(inter_counts, member, 0, keepdims=False)
    counts = counts.reshape(listed // block_size, block_size)
    gains = pl.pallas_call(
        functools.partial(tile_kernel, sizes),
        out_shape=[jax.ShapeDtypeStruct((3, sweeps, block_size), jnp.float32)] * structures,
        in_specs=[SMEM] * 3 + [VMEM] * 5,
        out_specs=[VMEM] * structures,
        scratch_shapes=[
            pltpu.VMEM((blocks, POINT_ROWS, block_size), jnp.bfloat16),
            pltpu.VMEM((sizes.plane * sweeps + listed // block_size, block_size), jnp.float32),
            pltpu.VMEM((UNIT * block_size, block_size), jnp.bfloat16),
            pltpu.VMEM((UNIT * 8, block_size), jnp.float32),
            pltpu.VMEM((UNIT, block_size), jnp.float32),
            pltpu.VMEM((UNIT, block_size), jnp.float32),
            pltpu.VMEM(((slots + 1) * POINT_ROWS, block_size), jnp.float32),
        ],
        compiler_params=pltpu.CompilerParams(vmem_limit_bytes=40 * 1024 * 1024),
        name="tiles",
    )(code, place, number, counts, own, marks, same, across)

    arrived = [gains[0]]
    for k in range(1, structures):
        arrived.append(lax.ppermute(gains[k], "row", deal[k]))
    return pl.pallas_call(
        functools.partial(place_kernel, sizes),
        out_shape=jax.ShapeDtypeStruct(coords.shape, jnp.float32),
        in_specs=[VMEM] * structures,
        out_specs=VMEM,
        name="place",
    )(*arrived)


def solution(mesh):
    placed = (
        P(None, None, None, ("row", "col")),
        P(),
        P(None, None, ("row", "col"), None),
        P(),
        P(),
    )
    return jax.shard_map(
        functools.partial(on_device, mesh.shape["row"], mesh.shape["col"]),
        mesh=mesh,
        in_specs=placed,
        out_specs=P(None, None, None, ("row", "col")),
        check_vma=False,
    )
```

```python
import functools

import jax
import jax.numpy as jnp
from jax import lax
from jax.experimental import pallas as pl
from jax.experimental.pallas import tpu as pltpu
from jax.sharding import PartitionSpec as P

CONTACT_SHIFT = 3.0
CONTACT_SLOPE = 0.5
BACKGROUND = 0.5
FAR = 32.0
UNIT = 8
POINT_ROWS = 16
AXES = ("row", "col")
VMEM = pl.BlockSpec(memory_space=pltpu.VMEM)
SMEM = pl.BlockSpec(memory_space=pltpu.SMEM)


def rounded(value):
    return value.astype(jnp.bfloat16).astype(jnp.float32)


def divide(value, by):
    return value >> (by.bit_length() - 1) if by & (by - 1) == 0 else lax.div(value, by)


def modulo(value, by):
    return value & (by - 1) if by & (by - 1) == 0 else lax.rem(value, by)


class Sizes:
    def __init__(self, n_row, n_col, structures, sweeps, width):
        self.n_row, self.n_col, self.structures, self.sweeps = n_row, n_col, structures, sweeps
        self.width = width
        self.share = n_row // structures
        self.plane = self.share * n_col
        self.chips = self.plane // 2
        self.half = n_col // 2
        self.groups = n_row * n_col
        self.blocks = self.groups * sweeps
        self.slots = structures * sweeps
        self.rows = self.slots * 4 + sweeps

    def at(self, block):
        return modulo(block, self.groups) * self.sweeps + divide(block, self.groups)


def pack_kernel(sizes, coords_ref, counts_ref, *out_refs):
    sweeps, width = sizes.sweeps, sizes.width
    family = lax.div(lax.axis_index("row"), sizes.share)
    lane = lax.broadcasted_iota(jnp.int32, (width, 128), 1)
    place = lax.broadcasted_iota(jnp.int32, (width, 128), 0) + family * width
    spread = (lane == place).astype(jnp.float32)
    for k, out_ref in enumerate(out_refs):
        member = lax.rem(family + k, sizes.structures)
        norm = jnp.zeros((sweeps, 128), jnp.float32)
        for place in range(3):
            point = coords_ref[member, place]
            out_ref[pl.ds(place, sweeps, stride=4), :] = point
            high = rounded(point)
            near = high + rounded(point - high)
            norm = norm - 0.5 * CONTACT_SLOPE * near * near
        out_ref[pl.ds(3, sweeps, stride=4), :] = norm
        counts = counts_ref[member][:, 0, :].astype(jnp.float32)
        out_ref[4 * sweeps : 5 * sweeps] = jnp.dot(counts, spread, preferred_element_type=jnp.float32)


def merge_kernel(points, *refs):
    counts = refs[0][points:]
    for k, ref in enumerate(refs[:-1]):
        refs[-1][k * points : (k + 1) * points] = ref[:points]
        counts = counts + ref[points:] if k else counts
    refs[-1][(len(refs) - 1) * points :] = counts


def join_kernel(*refs):
    rows = refs[0].shape[0]
    for k, ref in enumerate(refs[:-1]):
        refs[-1][k * rows : (k + 1) * rows] = ref[...]


def prepare_kernel(sizes, lengths_ref, pairs_ref, own_ref, first_ref, marks_ref, list_ref, starts_ref, ends_ref, digits_ref):
    slots, sweeps, groups = sizes.slots, sizes.sweeps, sizes.groups
    family = lax.div(lax.axis_index("row"), sizes.share)
    here = lax.rem(lax.axis_index("row"), sizes.share) * sizes.n_col + lax.axis_index("col")
    lane = lax.broadcasted_iota(jnp.int32, (1, 128), 1)
    row = lax.broadcasted_iota(jnp.int32, (8, 128), 0)
    labels = starts_ref.shape[0]
    depth = POINT_ROWS + labels

    starts_ref[...] = jnp.zeros_like(starts_ref)
    ends_ref[...] = jnp.zeros_like(ends_ref)
    end = jnp.int32(0)
    for k in range(lengths_ref.shape[0]):
        starts_ref[k : k + 1] = jnp.full((1, 128), end)
        end = end + lengths_ref[k]
        ends_ref[k : k + 1] = jnp.full((1, 128), end)

    def mark(group, carry):
        for u in range(sweeps):
            bead = (u * groups + group) * 128 + lane
            inside = (bead >= starts_ref[...]) & (bead < ends_ref[...])
            marks_ref[group * sweeps + u] = inside.astype(jnp.float32).astype(jnp.bfloat16)
        return carry

    lax.fori_loop(0, groups, mark, 0)

    def fill(turn, carry):
        origin = lax.rem(family + (sizes.structures - turn), sizes.structures)
        for pair in range(sweeps // 2):
            value = own_ref[pl.ds(pl.multiple_of(turn * sweeps * 4 + pair * 8, 8), 8), :]
            for odd in range(2):
                value = pltpu.roll(value, 4, 0) if odd else value
                high = rounded(value)
                low = rounded(value - high)
                shifted = value + 0.5 * CONTACT_SHIFT
                shifted_high = rounded(shifted)
                shifted_low = rounded(shifted - shifted_high)
                both = jnp.where(row < 4, high, pltpu.roll(high, 4, 0))
                near = jnp.where((row & 3) == 3, 1.0, CONTACT_SLOPE * both)
                rest = jnp.where(row == 4, pltpu.roll(shifted_low, 1, 0), 0.0)
                rest = jnp.where(row == 3, shifted_high, rest)
                rest = jnp.where(row < 3, CONTACT_SLOPE * low, rest)
                u = 2 * pair + odd
                bead = (u * groups + origin * sizes.plane + here) * 128 + lane
                inside = (bead >= starts_ref[...]) & (bead < ends_ref[...])
                apart = jnp.where(inside, 0.0, -FAR)
                blank = jnp.zeros((128 - depth, 128), jnp.float32)
                turned = jnp.transpose(jnp.concatenate([near, rest, apart, blank], axis=0))
                slot = origin * sweeps + u
                first_ref[slot] = turned[:, :depth].astype(jnp.bfloat16)
                other = jnp.where(lane < POINT_ROWS, turned, -FAR - turned)
                first_ref[slots + slot] = other[:, :depth].astype(jnp.bfloat16)
        return carry

    lax.fori_loop(0, sizes.structures, fill, 0)

    lines = pairs_ref.shape[0]
    half = lines // 2
    pairs = pairs_ref[...]
    group = modulo(pairs, groups)
    mine = modulo(group, sizes.plane) == here
    slot = jnp.where(mine, divide(group, sizes.plane) * sweeps + divide(pairs, groups), -1)
    other = sizes.at(pairs)
    slot_row = lax.broadcasted_iota(jnp.int32, (slots, 128), 0)
    before = lax.broadcasted_iota(jnp.int32, (128, 256), 0)
    after = lax.broadcasted_iota(jnp.int32, (128, 256), 1)
    count = (before <= after).astype(jnp.float32).astype(jnp.bfloat16)
    running = jnp.zeros((slots, 128), jnp.float32)
    picked = []
    for line in range(lines):
        chosen = (slot[line : line + 1] == slot_row).astype(jnp.float32)
        counted = jnp.dot(chosen.astype(jnp.bfloat16), count, preferred_element_type=jnp.float32)
        inner = jnp.sum(chosen * (counted[:, :128] - 1.0 + running), axis=0, keepdims=True)
        picked.append((chosen, inner))
        running = running + counted[:, 128:]
    doubled = 2.0 * jnp.floor(0.5 * (running + 1.0))
    lower = (
        lax.broadcasted_iota(jnp.int32, (slots, slots), 0) > lax.broadcasted_iota(jnp.int32, (slots, slots), 1)
    ).astype(jnp.float32)
    base = jnp.dot(lower, doubled, precision=lax.Precision.HIGHEST, preferred_element_type=jnp.float32)
    number = jnp.max(base + doubled).astype(jnp.int32)
    digit_row = lax.broadcasted_iota(jnp.int32, (POINT_ROWS, 128), 0)
    ranks = []
    for line in range(lines):
        chosen, inner = picked[line]
        rank = inner + jnp.sum(chosen * base, axis=0, keepdims=True)
        ranks.append(jnp.where(slot[line : line + 1] >= 0, rank.astype(jnp.int32), -1))
        opposite = (line + half) % lines
        partner = other[opposite : opposite + 1]
        digits = jnp.zeros((POINT_ROWS, 128), jnp.int32)
        for place, digit in enumerate(
            (partner & 31, partner >> 5, slot[line : line + 1], lane, line % half + 0 * lane, 1 + 0 * lane)
        ):
            digits = jnp.where(digit_row == place, digit, digits)
        digits_ref[line] = digits.astype(jnp.float32).astype(jnp.bfloat16)
    chunks = (list_ref.shape[0] - 8) // 2
    spot = lax.broadcasted_iota(jnp.int32, (128, 128), 0)

    def compact(chunk, carry):
        found = jnp.zeros((POINT_ROWS, 128), jnp.float32)
        for line in range(0, lines, 2):
            there = jnp.concatenate(
                [(ranks[line + i] == spot + chunk * 128).astype(jnp.float32).astype(jnp.bfloat16) for i in range(2)],
                axis=1,
            )
            found = found + lax.dot_general(
                jnp.concatenate([digits_ref[line], digits_ref[line + 1]], axis=1),
                there,
                (((1,), (1,)), ((), ())),
                preferred_element_type=jnp.float32,
            )
        found = found.astype(jnp.int32)
        at = found[2:3]
        code = found[0:1] + (found[1:2] << 5) + ((slots + at) << 12) + (at << 19)
        list_ref[pl.ds(chunk, 1), :] = jnp.where(found[5:6] > 0, code, slots << 19)
        list_ref[pl.ds(chunks + chunk, 1), :] = (
            sizes.plane * sweeps * 128 + found[3:4] + found[4:5] * 128
        )
        return carry

    lax.fori_loop(0, lax.div(number + 2 * UNIT - 1, 128) + 1, compact, 0)
    list_ref[2 * chunks : 2 * chunks + 8] = jnp.full((8, 128), number)


def tile_kernel(sizes, reach_ref, list_ref, listed_ref, first_ref, marks_ref, same_ref, across_ref, *refs):
    structures, sweeps, slots = sizes.structures, sizes.sweeps, sizes.slots
    out_refs = refs[:structures]
    second_ref, counts_ref, held_ref, sums_ref, picks_ref, diag_ref, total_ref = refs[structures:]
    row_here = lax.axis_index("row")
    column_here = lax.axis_index("col")
    family = lax.div(row_here, sizes.share)
    chip_here = lax.rem(row_here, sizes.share) * sizes.half + lax.div(column_here, 2)
    core_here = lax.rem(column_here, 2)
    lane = lax.broadcasted_iota(jnp.int32, (1, 128), 1)
    row = lax.broadcasted_iota(jnp.int32, (8, 128), 0)
    ones = jnp.where((row == 3) | (row == 4), 1.0, 0.0)

    for core, piece_ref in ((core_here, same_ref), (1 - core_here, across_ref)):
        for k in range(sizes.chips):
            chip = lax.rem(chip_here + (sizes.chips - k), sizes.chips)
            device = chip * 2 + core
            base = k * sizes.rows
            counts_ref[pl.ds(pl.multiple_of(device * sweeps, sweeps), sweeps), :] = piece_ref[
                base + slots * 4 : base + slots * 4 + sweeps
            ]
            for turn in range(structures):
                origin = lax.rem(family + (structures - turn), structures)
                at = (origin * sizes.plane + device) * sweeps
                for pair in range(sweeps // 2):
                    start = base + turn * sweeps * 4 + pair * 8
                    value = piece_ref[start : start + 8]
                    high = rounded(value)
                    low = value - high
                    high_turned = pltpu.roll(high, 4, 0)
                    even = jnp.concatenate(
                        [jnp.where(row < 4, high, pltpu.roll(low, 4, 0)), jnp.where(row < 3, high, ones)],
                        axis=0,
                    )
                    odd = jnp.concatenate(
                        [jnp.where(row < 4, high_turned, low), jnp.where(row < 3, high_turned, ones)],
                        axis=0,
                    )
                    second_ref[at + 2 * pair] = even.astype(jnp.bfloat16)
                    second_ref[at + 2 * pair + 1] = odd.astype(jnp.bfloat16)
    listed_base = sizes.plane * sweeps
    counts_ref[listed_base : listed_base + listed_ref.shape[0]] = listed_ref[...].astype(jnp.float32)

    total_ref[...] = jnp.zeros_like(total_ref)
    spare = 1.0 / (1.0 + jnp.exp(jnp.float32(-CONTACT_SHIFT)))

    here = lax.rem(row_here, sizes.share) * sizes.n_col + column_here
    groups = sizes.groups

    def step(ending, beginning):
        sums = sums_ref[pl.ds(0, UNIT, stride=8), :]
        for k in range(1, 8):
            sums = sums + sums_ref[pl.ds(k, UNIT, stride=8), :]
        chance = 64.0 * 128.0 + 0.5 * jnp.sum(sums, axis=1, keepdims=True)
        count = jnp.sum(picks_ref[...], axis=1, keepdims=True)
        chance = jnp.where(diag_ref[...] > 0.5, 0.5 * (chance - 128.0 * spare), chance)
        weight = 1.0 - count / (BACKGROUND + chance / 128.0)
        for t in range(0, UNIT, 2):
            left, right = (second_ref[ending[t + i] & 4095] for i in range(2))
            product = lax.dot_general(
                jnp.concatenate([left, right], axis=0),
                held_ref[t * 128 : (t + 2) * 128],
                (((1,), (1,)), ((), ())),
                preferred_element_type=jnp.float32,
            )
            for i in range(2):
                gain = product[i * POINT_ROWS : (i + 1) * POINT_ROWS, i * 128 : (i + 1) * 128]
                at = pl.multiple_of((ending[t + i] >> 19) * POINT_ROWS, POINT_ROWS)
                total_ref[pl.ds(at, POINT_ROWS), :] += weight[t + i : t + i + 1] * gain
        for t in range(0, UNIT, 2):
            seconds = [beginning[t + i][0] & 4095 for i in range(2)]
            logit = jnp.dot(
                first_ref[(beginning[t][0] >> 12) & 127],
                jnp.concatenate(
                    [jnp.concatenate([second_ref[at], marks_ref[at]], axis=0) for at in seconds], axis=1
                ),
                preferred_element_type=jnp.float32,
            )
            bend = jnp.tanh(logit)
            rest = 1.0 - bend * bend
            for i in range(2):
                part = bend[:, i * 128 : (i + 1) * 128]
                sums_ref[(t + i) * 8 : (t + i + 1) * 8] = jnp.sum(part.reshape(16, 8, 128), axis=0)
                held_ref[(t + i) * 128 : (t + i + 1) * 128] = rest[:, i * 128 : (i + 1) * 128].astype(
                    jnp.bfloat16
                )
                code, place, diagonal = beginning[t + i]
                picked = counts_ref[pl.ds(place >> 7, 1), :]
                picks_ref[t + i : t + i + 1] = jnp.where(lane == (place & 127), picked, 0.0)
                diag_ref[t + i : t + i + 1] = jnp.full((1, 128), diagonal)
        return tuple(code for code, _, _ in beginning)

    def band_step(turn, carry):
        slot, other, ending = carry
        beginning = []
        for _ in range(UNIT // 2):
            block = modulo(slot, sweeps) * groups + divide(slot, sweeps) * sizes.plane + here
            high = reach_ref[1, slot]
            for i in range(2):
                second = jnp.minimum(other + i, high)
                first = jnp.minimum(block, second)
                group = modulo(first, groups)
                line = modulo(group, sizes.plane) * sweeps + divide(first, groups)
                apart = jnp.abs(block - second)
                place = line * 128 + divide(group, sizes.plane) * sizes.width + apart
                total = jnp.where(other + i <= high, slot, slots)
                code = sizes.at(second) + (jnp.minimum(slot, slots - 1) << 12) + (total << 19)
                beginning.append((code, place, (apart == 0).astype(jnp.float32)))
            over = other + 2 > high
            slot = jnp.minimum(slot + over.astype(jnp.int32), slots)
            other = jnp.where(over, reach_ref[0, slot], other + 2)
        return slot, other, step(ending, beginning)

    def listed_step(turn, ending):
        beginning = []
        for t in range(UNIT):
            at = turn * UNIT + t
            beginning.append(
                (list_ref[at >> 7, at & 127], list_ref[chunks + (at >> 7), at & 127], jnp.float32(0.0))
            )
        return step(ending, beginning)

    chunks = (list_ref.shape[0] - 8) // 2
    idle = (jnp.int32(slots << 19),) * UNIT
    sums_ref[...] = jnp.zeros_like(sums_ref)
    carry = (jnp.int32(0), reach_ref[0, 0], idle)
    ending = lax.fori_loop(0, reach_ref[0, slots + 1], band_step, carry)[2]
    listed_steps = lax.div(list_ref[2 * chunks, 0] + UNIT - 1, UNIT)
    lax.fori_loop(0, listed_steps + 1, listed_step, ending)

    scale = -2.0 * CONTACT_SLOPE / 128.0 / 4.0
    for k in range(structures):
        origin = lax.rem(family + k, structures)
        turn = (structures - k) % structures
        first = origin * sweeps * POINT_ROWS
        mass = total_ref[pl.ds(first + 11, sweeps, stride=POINT_ROWS), :]
        for place in range(3):
            point = same_ref[pl.ds(turn * sweeps * 4 + place, sweeps, stride=4), :]
            high = rounded(point)
            near = high + rounded(point - high)
            pull = (
                total_ref[pl.ds(first + place, sweeps, stride=POINT_ROWS), :]
                + total_ref[pl.ds(first + place + 4, sweeps, stride=POINT_ROWS), :]
            )
            out_refs[k][place] = scale * (near * mass - pull)


def place_kernel(sizes, *refs):
    family = lax.div(lax.axis_index("row"), sizes.share)
    for k, ref in enumerate(refs[:-1]):
        refs[-1][lax.rem(family + (sizes.structures - k), sizes.structures)] = ref[...]


def on_device(n_row, n_col, coords, chrom_lengths, band_counts, inter_pairs, inter_counts):
    structures, _, sweeps, block_size = coords.shape
    width = band_counts.shape[3]
    band_reach = width - 1
    listed = inter_pairs.shape[1]
    sizes = Sizes(n_row, n_col, structures, sweeps, width)
    share, groups, slots, blocks = sizes.share, sizes.groups, sizes.slots, sizes.blocks
    row_here = lax.axis_index("row")
    column_here = lax.axis_index("col")
    member = row_here // share
    here = row_here % share * n_col + column_here

    messages = pl.pallas_call(
        functools.partial(pack_kernel, sizes),
        out_shape=[jax.ShapeDtypeStruct((5 * sweeps, block_size), jnp.float32)] * structures,
        in_specs=[VMEM, VMEM],
        out_specs=[VMEM] * structures,
        name="pack",
    )(coords, band_counts)
    deal = [
        [(i, (i // share + k) % structures * share + i % share) for i in range(n_row)]
        for k in range(structures)
    ]
    received = [messages[0]]
    for k in range(1, structures):
        received.append(lax.ppermute(messages[k], "row", deal[k]))
    own_row = pl.pallas_call(
        functools.partial(merge_kernel, 4 * sweeps),
        out_shape=jax.ShapeDtypeStruct((sizes.rows, block_size), jnp.float32),
        in_specs=[VMEM] * structures,
        out_specs=VMEM,
        name="merge",
    )(*received)

    def device(family, chip, core):
        row = family * share + chip // sizes.half
        return row * n_col + chip % sizes.half * 2 + core

    pieces = [own_row]
    for k in range(1, sizes.chips):
        moves = [
            (device(f, i, core), device(f, (i + k) % sizes.chips, core))
            for f in range(structures)
            for i in range(sizes.chips)
            for core in range(2)
        ]
        pieces.append(lax.ppermute(own_row, AXES, moves))
    same = pl.pallas_call(
        join_kernel,
        out_shape=jax.ShapeDtypeStruct((sizes.chips * sizes.rows, block_size), jnp.float32),
        in_specs=[VMEM] * sizes.chips,
        out_specs=VMEM,
        name="join",
    )(*pieces)
    across = lax.ppermute(same, "col", [(i, i ^ 1) for i in range(n_col)])

    chromosomes = chrom_lengths.shape[0]
    numbers = jnp.arange(chromosomes)
    ends = jnp.sum(jnp.where(numbers[None, :] <= numbers[:, None], chrom_lengths[None, :], 0), axis=1)
    starts = ends - chrom_lengths
    slot = jnp.arange(slots)
    block = slot % sweeps * groups + slot // sweeps * sizes.plane + here
    first_bead = block * block_size
    last_bead = first_bead + block_size - 1
    low = jnp.max(jnp.where(starts[None, :] <= first_bead[:, None], starts[None, :], 0), axis=1)
    high = jnp.min(
        jnp.where(ends[None, :] > last_bead[:, None], ends[None, :], blocks * block_size), axis=1
    )
    low = jnp.maximum(low // block_size, block - band_reach)
    high = jnp.minimum(jnp.minimum((high - 1) // block_size, block + band_reach), blocks - 1)
    steps = (jnp.sum((high - low + 2) // 2) + UNIT // 2 - 1) // (UNIT // 2)
    reach = jnp.stack(
        [
            jnp.concatenate([low, jnp.stack([jnp.zeros_like(steps), steps])]),
            jnp.concatenate([high, jnp.stack([jnp.zeros_like(steps), steps])]),
        ]
    ).astype(jnp.int32)
    pairs = jnp.transpose(lax.dynamic_index_in_dim(inter_pairs, member, 0, keepdims=False))
    pairs = pairs.reshape(2 * listed // block_size, block_size)
    labels = -(-chromosomes // 16) * 16
    depth = POINT_ROWS + labels
    chunks = -(-(2 * listed + slots + 2 * UNIT) // block_size)
    own, marks, tiles = pl.pallas_call(
        functools.partial(prepare_kernel, sizes),
        out_shape=[
            jax.ShapeDtypeStruct((2 * slots, block_size, depth), jnp.bfloat16),
            jax.ShapeDtypeStruct((blocks, labels, block_size), jnp.bfloat16),
            jax.ShapeDtypeStruct((2 * chunks + 8, block_size), jnp.int32),
        ],
        in_specs=[SMEM, VMEM, VMEM],
        out_specs=[VMEM] * 3,
        scratch_shapes=[
            pltpu.VMEM((labels, block_size), jnp.int32),
            pltpu.VMEM((labels, block_size), jnp.int32),
            pltpu.VMEM((2 * listed // block_size, POINT_ROWS, block_size), jnp.bfloat16),
        ],
        cost_estimate=pl.CostEstimate(flops=1 << 30, bytes_accessed=1 << 23, transcendentals=0),
        compiler_params=pltpu.CompilerParams(vmem_limit_bytes=24 * 1024 * 1024),
        name="prepare",
    )(chrom_lengths, pairs, own_row)

    counts = lax.dynamic_index_in_dim(inter_counts, member, 0, keepdims=False)
    counts = counts.reshape(listed // block_size, block_size)
    gains = pl.pallas_call(
        functools.partial(tile_kernel, sizes),
        out_shape=[jax.ShapeDtypeStruct((3, sweeps, block_size), jnp.float32)] * structures,
        in_specs=[SMEM] * 2 + [VMEM] * 5,
        out_specs=[VMEM] * structures,
        scratch_shapes=[
            pltpu.VMEM((blocks, POINT_ROWS, block_size), jnp.bfloat16),
            pltpu.VMEM((sizes.plane * sweeps + listed // block_size, block_size), jnp.float32),
            pltpu.VMEM((UNIT * block_size, block_size), jnp.bfloat16),
            pltpu.VMEM((UNIT * 8, block_size), jnp.float32),
            pltpu.VMEM((UNIT, block_size), jnp.float32),
            pltpu.VMEM((UNIT, block_size), jnp.float32),
            pltpu.VMEM(((slots + 1) * POINT_ROWS, block_size), jnp.float32),
        ],
        compiler_params=pltpu.CompilerParams(vmem_limit_bytes=40 * 1024 * 1024),
        name="tiles",
    )(reach, tiles, counts, own, marks, same, across)

    arrived = [gains[0]]
    for k in range(1, structures):
        arrived.append(lax.ppermute(gains[k], "row", deal[k]))
    return pl.pallas_call(
        functools.partial(place_kernel, sizes),
        out_shape=jax.ShapeDtypeStruct(coords.shape, jnp.float32),
        in_specs=[VMEM] * structures,
        out_specs=VMEM,
        name="place",
    )(*arrived)


def solution(mesh):
    placed = (
        P(None, None, None, ("row", "col")),
        P(),
        P(None, None, ("row", "col"), None),
        P(),
        P(),
    )
    return jax.shard_map(
        functools.partial(on_device, mesh.shape["row"], mesh.shape["col"]),
        mesh=mesh,
        in_specs=placed,
        out_specs=P(None, None, None, ("row", "col")),
        check_vma=False,
    )
```

```python
import functools

import jax
import jax.numpy as jnp
from jax import lax
from jax.experimental import pallas as pl
from jax.experimental.pallas import tpu as pltpu
from jax.sharding import PartitionSpec as P

CONTACT_SHIFT = 3.0
CONTACT_SLOPE = 0.5
BACKGROUND = 0.5
FAR = 32.0
UNIT = 16
POINT_ROWS = 16
AXES = ("row", "col")
VMEM = pl.BlockSpec(memory_space=pltpu.VMEM)
SMEM = pl.BlockSpec(memory_space=pltpu.SMEM)


def rounded(value):
    return value.astype(jnp.bfloat16).astype(jnp.float32)


def divide(value, by):
    return value >> (by.bit_length() - 1) if by & (by - 1) == 0 else lax.div(value, by)


def modulo(value, by):
    return value & (by - 1) if by & (by - 1) == 0 else lax.rem(value, by)


class Sizes:
    def __init__(self, n_row, n_col, structures, sweeps, width):
        self.n_row, self.n_col, self.structures, self.sweeps = n_row, n_col, structures, sweeps
        self.width = width
        self.share = n_row // structures
        self.plane = self.share * n_col
        self.chips = self.plane // 2
        self.half = n_col // 2
        self.groups = n_row * n_col
        self.blocks = self.groups * sweeps
        self.slots = structures * sweeps
        self.rows = self.slots * 4 + sweeps

    def at(self, block):
        return modulo(block, self.groups) * self.sweeps + divide(block, self.groups)


def pack_kernel(sizes, coords_ref, counts_ref, *out_refs):
    sweeps, width = sizes.sweeps, sizes.width
    family = lax.div(lax.axis_index("row"), sizes.share)
    lane = lax.broadcasted_iota(jnp.int32, (width, 128), 1)
    place = lax.broadcasted_iota(jnp.int32, (width, 128), 0) + family * width
    spread = (lane == place).astype(jnp.float32)
    for k, out_ref in enumerate(out_refs):
        member = lax.rem(family + k, sizes.structures)
        norm = jnp.zeros((sweeps, 128), jnp.float32)
        for place in range(3):
            point = coords_ref[member, place]
            out_ref[pl.ds(place, sweeps, stride=4), :] = point
            high = rounded(point)
            near = high + rounded(point - high)
            norm = norm - 0.5 * CONTACT_SLOPE * near * near
        out_ref[pl.ds(3, sweeps, stride=4), :] = norm
        counts = counts_ref[member][:, 0, :].astype(jnp.float32)
        out_ref[4 * sweeps : 5 * sweeps] = jnp.dot(counts, spread, preferred_element_type=jnp.float32)


def merge_kernel(points, *refs):
    counts = refs[0][points:]
    for k, ref in enumerate(refs[:-1]):
        refs[-1][k * points : (k + 1) * points] = ref[:points]
        counts = counts + ref[points:] if k else counts
    refs[-1][(len(refs) - 1) * points :] = counts


def join_kernel(*refs):
    rows = refs[0].shape[0]
    for k, ref in enumerate(refs[:-1]):
        refs[-1][k * rows : (k + 1) * rows] = ref[...]


def prepare_kernel(sizes, lengths_ref, pairs_ref, own_ref, first_ref, marks_ref, list_ref, starts_ref, ends_ref, digits_ref):
    slots, sweeps, groups = sizes.slots, sizes.sweeps, sizes.groups
    family = lax.div(lax.axis_index("row"), sizes.share)
    here = lax.rem(lax.axis_index("row"), sizes.share) * sizes.n_col + lax.axis_index("col")
    lane = lax.broadcasted_iota(jnp.int32, (1, 128), 1)
    row = lax.broadcasted_iota(jnp.int32, (8, 128), 0)
    labels = starts_ref.shape[0]
    depth = POINT_ROWS + labels

    starts_ref[...] = jnp.zeros_like(starts_ref)
    ends_ref[...] = jnp.zeros_like(ends_ref)
    slot_row = lax.broadcasted_iota(jnp.int32, (slots, 128), 0)
    block = modulo(slot_row, sweeps) * groups + divide(slot_row, sweeps) * sizes.plane + here
    first_bead = block * 128
    low = jnp.zeros((slots, 128), jnp.int32)
    high = jnp.full((slots, 128), sizes.blocks * 128)
    end = jnp.int32(0)
    for k in range(lengths_ref.shape[0]):
        start = end
        end = end + lengths_ref[k]
        starts_ref[k : k + 1] = jnp.full((1, 128), start)
        ends_ref[k : k + 1] = jnp.full((1, 128), end)
        low = jnp.maximum(low, jnp.where(start <= first_bead, start, 0))
        high = jnp.minimum(high, jnp.where(end > first_bead + 127, end, sizes.blocks * 128))

    low = jnp.maximum(low >> 7, block - (sizes.width - 1))
    high = jnp.minimum(jnp.minimum((high - 1) >> 7, block + (sizes.width - 1)), sizes.blocks - 1)
    reach = []
    for value in (low, high, (high - low + 2) >> 1):
        reach.append(jnp.sum(jnp.where(slot_row == lane, value, 0), axis=0, keepdims=True))
    steps = lax.div(jnp.sum(reach[2]) + (UNIT // 2 - 1), UNIT // 2)

    def mark(group, carry):
        for u in range(sweeps):
            bead = (u * groups + group) * 128 + lane
            inside = (bead >= starts_ref[...]) & (bead < ends_ref[...])
            marks_ref[group * sweeps + u] = inside.astype(jnp.float32).astype(jnp.bfloat16)
        return carry

    lax.fori_loop(0, groups, mark, 0)

    def fill(turn, carry):
        origin = lax.rem(family + (sizes.structures - turn), sizes.structures)
        for pair in range(sweeps // 2):
            value = own_ref[pl.ds(pl.multiple_of(turn * sweeps * 4 + pair * 8, 8), 8), :]
            for odd in range(2):
                value = pltpu.roll(value, 4, 0) if odd else value
                high = rounded(value)
                low = rounded(value - high)
                shifted = value + 0.5 * CONTACT_SHIFT
                shifted_high = rounded(shifted)
                shifted_low = rounded(shifted - shifted_high)
                both = jnp.where(row < 4, high, pltpu.roll(high, 4, 0))
                near = jnp.where((row & 3) == 3, 1.0, CONTACT_SLOPE * both)
                rest = jnp.where(row == 4, pltpu.roll(shifted_low, 1, 0), 0.0)
                rest = jnp.where(row == 3, shifted_high, rest)
                rest = jnp.where(row < 3, CONTACT_SLOPE * low, rest)
                u = 2 * pair + odd
                bead = (u * groups + origin * sizes.plane + here) * 128 + lane
                inside = (bead >= starts_ref[...]) & (bead < ends_ref[...])
                apart = jnp.where(inside, 0.0, -FAR)
                blank = jnp.zeros((128 - depth, 128), jnp.float32)
                turned = jnp.transpose(jnp.concatenate([near, rest, apart, blank], axis=0))
                slot = origin * sweeps + u
                first_ref[slot] = turned[:, :depth].astype(jnp.bfloat16)
                other = jnp.where(lane < POINT_ROWS, turned, -FAR - turned)
                first_ref[slots + slot] = other[:, :depth].astype(jnp.bfloat16)
        return carry

    lax.fori_loop(0, sizes.structures, fill, 0)

    half = pairs_ref.shape[2] // 128
    lines = 2 * half
    pairs = pairs_ref[family]
    group = modulo(pairs, groups)
    mine = modulo(group, sizes.plane) == here
    slot = jnp.where(mine, divide(group, sizes.plane) * sweeps + divide(pairs, groups), -1)
    other = sizes.at(pairs)

    def cut(value, line):
        side, at = line // half, line % half * 128
        return value[side : side + 1, at : at + 128]

    before = lax.broadcasted_iota(jnp.int32, (128, 256), 0)
    after = lax.broadcasted_iota(jnp.int32, (128, 256), 1)
    count = (before <= after).astype(jnp.float32).astype(jnp.bfloat16)
    running = jnp.zeros((slots, 128), jnp.float32)
    picked = []
    for line in range(lines):
        chosen = (cut(slot, line) == slot_row).astype(jnp.float32)
        counted = jnp.dot(chosen.astype(jnp.bfloat16), count, preferred_element_type=jnp.float32)
        inner = jnp.sum(chosen * (counted[:, :128] - 1.0 + running), axis=0, keepdims=True)
        picked.append((chosen, inner))
        running = running + counted[:, 128:]
    doubled = 2.0 * jnp.floor(0.5 * (running + 1.0))
    lower = (
        lax.broadcasted_iota(jnp.int32, (slots, slots), 0) > lax.broadcasted_iota(jnp.int32, (slots, slots), 1)
    ).astype(jnp.float32)
    base = jnp.dot(lower, doubled, precision=lax.Precision.HIGHEST, preferred_element_type=jnp.float32)
    number = jnp.max(base + doubled).astype(jnp.int32)
    digit_row = lax.broadcasted_iota(jnp.int32, (POINT_ROWS, 128), 0)
    ranks = []
    for line in range(lines):
        chosen, inner = picked[line]
        rank = inner + jnp.sum(chosen * base, axis=0, keepdims=True)
        ranks.append(jnp.where(cut(slot, line) >= 0, rank.astype(jnp.int32), -1))
        opposite = (line + half) % lines
        partner = cut(other, opposite)
        digits = jnp.zeros((POINT_ROWS, 128), jnp.int32)
        for place, digit in enumerate(
            (partner & 31, partner >> 5, cut(slot, line), lane, line % half + 0 * lane, 1 + 0 * lane)
        ):
            digits = jnp.where(digit_row == place, digit, digits)
        digits_ref[line] = digits.astype(jnp.float32).astype(jnp.bfloat16)
    chunks = (list_ref.shape[0] - 8) // 2
    spot = lax.broadcasted_iota(jnp.int32, (128, 128), 0)

    def compact(chunk, carry):
        found = jnp.zeros((POINT_ROWS, 128), jnp.float32)
        for line in range(0, lines, 2):
            there = jnp.concatenate(
                [(ranks[line + i] == spot + chunk * 128).astype(jnp.float32).astype(jnp.bfloat16) for i in range(2)],
                axis=1,
            )
            found = found + lax.dot_general(
                jnp.concatenate([digits_ref[line], digits_ref[line + 1]], axis=1),
                there,
                (((1,), (1,)), ((), ())),
                preferred_element_type=jnp.float32,
            )
        found = found.astype(jnp.int32)
        at = found[2:3]
        code = found[0:1] + (found[1:2] << 5) + ((slots + at) << 12) + (at << 19)
        list_ref[pl.ds(chunk, 1), :] = jnp.where(found[5:6] > 0, code, slots << 19)
        list_ref[pl.ds(chunks + chunk, 1), :] = (
            sizes.plane * sweeps * 128 + found[3:4] + found[4:5] * 128
        )
        return carry

    lax.fori_loop(0, lax.div(number + 2 * UNIT - 1, 128) + 1, compact, 0)
    end = 2 * chunks
    list_ref[end : end + 1] = jnp.full((1, 128), number)
    list_ref[end + 1 : end + 2] = reach[0]
    list_ref[end + 2 : end + 3] = reach[1]
    list_ref[end + 3 : end + 4] = jnp.full((1, 128), steps)


def tile_kernel(sizes, list_ref, listed_ref, first_ref, marks_ref, same_ref, across_ref, *refs):
    structures, sweeps, slots = sizes.structures, sizes.sweeps, sizes.slots
    out_refs = refs[:structures]
    second_ref, counts_ref, held_ref, sums_ref, picks_ref, diag_ref, total_ref = refs[structures:]
    row_here = lax.axis_index("row")
    column_here = lax.axis_index("col")
    family = lax.div(row_here, sizes.share)
    chip_here = lax.rem(row_here, sizes.share) * sizes.half + lax.div(column_here, 2)
    core_here = lax.rem(column_here, 2)
    lane = lax.broadcasted_iota(jnp.int32, (1, 128), 1)
    row = lax.broadcasted_iota(jnp.int32, (8, 128), 0)
    ones = jnp.where((row == 3) | (row == 4), 1.0, 0.0)

    for core, piece_ref in ((core_here, same_ref), (1 - core_here, across_ref)):
        for k in range(sizes.chips):
            chip = lax.rem(chip_here + (sizes.chips - k), sizes.chips)
            device = chip * 2 + core
            base = k * sizes.rows
            counts_ref[pl.ds(pl.multiple_of(device * sweeps, sweeps), sweeps), :] = piece_ref[
                base + slots * 4 : base + slots * 4 + sweeps
            ]
            for turn in range(structures):
                origin = lax.rem(family + (structures - turn), structures)
                at = (origin * sizes.plane + device) * sweeps
                for pair in range(sweeps // 2):
                    start = base + turn * sweeps * 4 + pair * 8
                    value = piece_ref[start : start + 8]
                    high = rounded(value)
                    low = value - high
                    high_turned = pltpu.roll(high, 4, 0)
                    even = jnp.concatenate(
                        [jnp.where(row < 4, high, pltpu.roll(low, 4, 0)), jnp.where(row < 3, high, ones)],
                        axis=0,
                    )
                    odd = jnp.concatenate(
                        [jnp.where(row < 4, high_turned, low), jnp.where(row < 3, high_turned, ones)],
                        axis=0,
                    )
                    second_ref[at + 2 * pair] = even.astype(jnp.bfloat16)
                    second_ref[at + 2 * pair + 1] = odd.astype(jnp.bfloat16)
    listed_base = sizes.plane * sweeps
    chosen = lax.broadcasted_iota(jnp.int32, (structures, 128), 0) == family
    for k in range(listed_ref.shape[1] // 128):
        line = jnp.where(chosen, listed_ref[:, k * 128 : (k + 1) * 128], 0)
        counts_ref[listed_base + k : listed_base + k + 1] = jnp.sum(line, axis=0, keepdims=True).astype(
            jnp.float32
        )
    chunks = (list_ref.shape[0] - 8) // 2

    total_ref[...] = jnp.zeros_like(total_ref)
    spare = 1.0 / (1.0 + jnp.exp(jnp.float32(-CONTACT_SHIFT)))

    here = lax.rem(row_here, sizes.share) * sizes.n_col + column_here
    groups = sizes.groups

    def step(ending, beginning):
        sums = sums_ref[pl.ds(0, UNIT, stride=8), :]
        for k in range(1, 8):
            sums = sums + sums_ref[pl.ds(k, UNIT, stride=8), :]
        chance = 64.0 * 128.0 + 0.5 * jnp.sum(sums, axis=1, keepdims=True)
        count = jnp.sum(picks_ref[...], axis=1, keepdims=True)
        chance = jnp.where(diag_ref[...] > 0.5, 0.5 * (chance - 128.0 * spare), chance)
        weight = 1.0 - count / (BACKGROUND + chance / 128.0)
        for t in range(0, UNIT, 2):
            left, right = (second_ref[ending[t + i] & 4095] for i in range(2))
            product = lax.dot_general(
                jnp.concatenate([left, right], axis=0),
                held_ref[t * 128 : (t + 2) * 128],
                (((1,), (1,)), ((), ())),
                preferred_element_type=jnp.float32,
            )
            for i in range(2):
                gain = product[i * POINT_ROWS : (i + 1) * POINT_ROWS, i * 128 : (i + 1) * 128]
                at = pl.multiple_of((ending[t + i] >> 19) * POINT_ROWS, POINT_ROWS)
                total_ref[pl.ds(at, POINT_ROWS), :] += weight[t + i : t + i + 1] * gain
        for t in range(0, UNIT, 2):
            seconds = [beginning[t + i][0] & 4095 for i in range(2)]
            logit = jnp.dot(
                first_ref[(beginning[t][0] >> 12) & 127],
                jnp.concatenate(
                    [jnp.concatenate([second_ref[at], marks_ref[at]], axis=0) for at in seconds], axis=1
                ),
                preferred_element_type=jnp.float32,
            )
            bend = jnp.tanh(logit)
            rest = 1.0 - bend * bend
            for i in range(2):
                part = bend[:, i * 128 : (i + 1) * 128]
                sums_ref[(t + i) * 8 : (t + i + 1) * 8] = jnp.sum(part.reshape(16, 8, 128), axis=0)
                held_ref[(t + i) * 128 : (t + i + 1) * 128] = rest[:, i * 128 : (i + 1) * 128].astype(
                    jnp.bfloat16
                )
                code, place, diagonal = beginning[t + i]
                picked = counts_ref[pl.ds(place >> 7, 1), :]
                picks_ref[t + i : t + i + 1] = jnp.where(lane == (place & 127), picked, 0.0)
                diag_ref[t + i : t + i + 1] = jnp.full((1, 128), diagonal)
        return tuple(code for code, _, _ in beginning)

    def band_step(turn, carry):
        slot, other, ending = carry
        beginning = []
        for _ in range(UNIT // 2):
            block = modulo(slot, sweeps) * groups + divide(slot, sweeps) * sizes.plane + here
            high = list_ref[2 * chunks + 2, slot]
            for i in range(2):
                second = jnp.minimum(other + i, high)
                first = jnp.minimum(block, second)
                group = modulo(first, groups)
                line = modulo(group, sizes.plane) * sweeps + divide(first, groups)
                apart = jnp.abs(block - second)
                place = line * 128 + divide(group, sizes.plane) * sizes.width + apart
                total = jnp.where(other + i <= high, slot, slots)
                code = sizes.at(second) + (jnp.minimum(slot, slots - 1) << 12) + (total << 19)
                beginning.append((code, place, (apart == 0).astype(jnp.float32)))
            over = other + 2 > high
            slot = jnp.minimum(slot + over.astype(jnp.int32), slots)
            other = jnp.where(over, list_ref[2 * chunks + 1, slot], other + 2)
        return slot, other, step(ending, beginning)

    def listed_step(turn, ending):
        beginning = []
        for t in range(UNIT):
            at = turn * UNIT + t
            beginning.append(
                (list_ref[at >> 7, at & 127], list_ref[chunks + (at >> 7), at & 127], jnp.float32(0.0))
            )
        return step(ending, beginning)

    idle = (jnp.int32(slots << 19),) * UNIT
    sums_ref[...] = jnp.zeros_like(sums_ref)
    carry = (jnp.int32(0), list_ref[2 * chunks + 1, 0], idle)
    ending = lax.fori_loop(0, list_ref[2 * chunks + 3, 0], band_step, carry)[2]
    listed_steps = lax.div(list_ref[2 * chunks, 0] + UNIT - 1, UNIT)
    lax.fori_loop(0, listed_steps + 1, listed_step, ending)

    scale = -2.0 * CONTACT_SLOPE / 128.0 / 4.0
    for k in range(structures):
        origin = lax.rem(family + k, structures)
        turn = (structures - k) % structures
        first = origin * sweeps * POINT_ROWS
        mass = total_ref[pl.ds(first + 11, sweeps, stride=POINT_ROWS), :]
        for place in range(3):
            point = same_ref[pl.ds(turn * sweeps * 4 + place, sweeps, stride=4), :]
            high = rounded(point)
            near = high + rounded(point - high)
            pull = (
                total_ref[pl.ds(first + place, sweeps, stride=POINT_ROWS), :]
                + total_ref[pl.ds(first + place + 4, sweeps, stride=POINT_ROWS), :]
            )
            out_refs[k][place] = scale * (near * mass - pull)


def place_kernel(sizes, *refs):
    family = lax.div(lax.axis_index("row"), sizes.share)
    for k, ref in enumerate(refs[:-1]):
        refs[-1][lax.rem(family + (sizes.structures - k), sizes.structures)] = ref[...]


def on_device(n_row, n_col, coords, chrom_lengths, band_counts, inter_pairs, inter_counts):
    structures, _, sweeps, block_size = coords.shape
    width = band_counts.shape[3]
    listed = inter_pairs.shape[1]
    sizes = Sizes(n_row, n_col, structures, sweeps, width)
    share, slots, blocks = sizes.share, sizes.slots, sizes.blocks

    messages = pl.pallas_call(
        functools.partial(pack_kernel, sizes),
        out_shape=[jax.ShapeDtypeStruct((5 * sweeps, block_size), jnp.float32)] * structures,
        in_specs=[VMEM, VMEM],
        out_specs=[VMEM] * structures,
        name="pack",
    )(coords, band_counts)
    deal = [
        [(i, (i // share + k) % structures * share + i % share) for i in range(n_row)]
        for k in range(structures)
    ]
    received = [messages[0]]
    for k in range(1, structures):
        received.append(lax.ppermute(messages[k], "row", deal[k]))
    own_row = pl.pallas_call(
        functools.partial(merge_kernel, 4 * sweeps),
        out_shape=jax.ShapeDtypeStruct((sizes.rows, block_size), jnp.float32),
        in_specs=[VMEM] * structures,
        out_specs=VMEM,
        name="merge",
    )(*received)

    def device(family, chip, core):
        row = family * share + chip // sizes.half
        return row * n_col + chip % sizes.half * 2 + core

    pieces = [own_row]
    for k in range(1, sizes.chips):
        moves = [
            (device(f, i, core), device(f, (i + k) % sizes.chips, core))
            for f in range(structures)
            for i in range(sizes.chips)
            for core in range(2)
        ]
        pieces.append(lax.ppermute(own_row, AXES, moves))
    same = pl.pallas_call(
        join_kernel,
        out_shape=jax.ShapeDtypeStruct((sizes.chips * sizes.rows, block_size), jnp.float32),
        in_specs=[VMEM] * sizes.chips,
        out_specs=VMEM,
        name="join",
    )(*pieces)
    across = lax.ppermute(same, "col", [(i, i ^ 1) for i in range(n_col)])

    labels = -(-chrom_lengths.shape[0] // 16) * 16
    depth = POINT_ROWS + labels
    chunks = -(-(2 * listed + slots + 2 * UNIT) // block_size)
    own, marks, tiles = pl.pallas_call(
        functools.partial(prepare_kernel, sizes),
        out_shape=[
            jax.ShapeDtypeStruct((2 * slots, block_size, depth), jnp.bfloat16),
            jax.ShapeDtypeStruct((blocks, labels, block_size), jnp.bfloat16),
            jax.ShapeDtypeStruct((2 * chunks + 8, block_size), jnp.int32),
        ],
        in_specs=[SMEM, VMEM, VMEM],
        out_specs=[VMEM] * 3,
        scratch_shapes=[
            pltpu.VMEM((labels, block_size), jnp.int32),
            pltpu.VMEM((labels, block_size), jnp.int32),
            pltpu.VMEM((2 * listed // block_size, POINT_ROWS, block_size), jnp.bfloat16),
        ],
        cost_estimate=pl.CostEstimate(flops=1 << 30, bytes_accessed=1 << 23, transcendentals=0),
        compiler_params=pltpu.CompilerParams(vmem_limit_bytes=24 * 1024 * 1024),
        name="prepare",
    )(chrom_lengths, jnp.transpose(inter_pairs, (0, 2, 1)), own_row)

    gains = pl.pallas_call(
        functools.partial(tile_kernel, sizes),
        out_shape=[jax.ShapeDtypeStruct((3, sweeps, block_size), jnp.float32)] * structures,
        in_specs=[SMEM] + [VMEM] * 5,
        out_specs=[VMEM] * structures,
        scratch_shapes=[
            pltpu.VMEM((blocks, POINT_ROWS, block_size), jnp.bfloat16),
            pltpu.VMEM((sizes.plane * sweeps + listed // block_size, block_size), jnp.float32),
            pltpu.VMEM((UNIT * block_size, block_size), jnp.bfloat16),
            pltpu.VMEM((UNIT * 8, block_size), jnp.float32),
            pltpu.VMEM((UNIT, block_size), jnp.float32),
            pltpu.VMEM((UNIT, block_size), jnp.float32),
            pltpu.VMEM(((slots + 1) * POINT_ROWS, block_size), jnp.float32),
        ],
        compiler_params=pltpu.CompilerParams(vmem_limit_bytes=40 * 1024 * 1024),
        name="tiles",
    )(tiles, inter_counts, own, marks, same, across)

    arrived = [gains[0]]
    for k in range(1, structures):
        arrived.append(lax.ppermute(gains[k], "row", deal[k]))
    return pl.pallas_call(
        functools.partial(place_kernel, sizes),
        out_shape=jax.ShapeDtypeStruct(coords.shape, jnp.float32),
        in_specs=[VMEM] * structures,
        out_specs=VMEM,
        name="place",
    )(*arrived)


def solution(mesh):
    placed = (
        P(None, None, None, ("row", "col")),
        P(),
        P(None, None, ("row", "col"), None),
        P(),
        P(),
    )
    return jax.shard_map(
        functools.partial(on_device, mesh.shape["row"], mesh.shape["col"]),
        mesh=mesh,
        in_specs=placed,
        out_specs=P(None, None, None, ("row", "col")),
        check_vma=False,
    )
```

```python
import functools

import jax
import jax.numpy as jnp
from jax import lax
from jax.experimental import pallas as pl
from jax.experimental.pallas import tpu as pltpu
from jax.sharding import PartitionSpec as P

CONTACT_SHIFT = 3.0
CONTACT_SLOPE = 0.5
BACKGROUND = 0.5
FAR = 32.0
UNIT = 32
POINT_ROWS = 16
AXES = ("row", "col")
VMEM = pl.BlockSpec(memory_space=pltpu.VMEM)
SMEM = pl.BlockSpec(memory_space=pltpu.SMEM)
ANY = pl.BlockSpec(memory_space=pl.ANY)
SMALL = pltpu.CompilerParams(vmem_limit_bytes=8 * 1024 * 1024)


def rounded(value):
    return value.astype(jnp.bfloat16).astype(jnp.float32)


def divide(value, by):
    return value >> (by.bit_length() - 1) if by & (by - 1) == 0 else lax.div(value, by)


def modulo(value, by):
    return value & (by - 1) if by & (by - 1) == 0 else lax.rem(value, by)


class Sizes:
    def __init__(self, n_row, n_col, structures, sweeps, width):
        self.n_row, self.n_col, self.structures, self.sweeps = n_row, n_col, structures, sweeps
        self.width = width
        self.share = n_row // structures
        self.plane = self.share * n_col
        self.chips = self.plane // 2
        self.half = n_col // 2
        self.groups = n_row * n_col
        self.blocks = self.groups * sweeps
        self.slots = structures * sweeps
        self.rows = self.slots * 4 + sweeps

    def at(self, block):
        return modulo(block, self.groups) * self.sweeps + divide(block, self.groups)


def pack_kernel(sizes, coords_ref, counts_ref, *out_refs):
    sweeps, width = sizes.sweeps, sizes.width
    family = lax.div(lax.axis_index("row"), sizes.share)
    lane = lax.broadcasted_iota(jnp.int32, (width, 128), 1)
    place = lax.broadcasted_iota(jnp.int32, (width, 128), 0) + family * width
    spread = (lane == place).astype(jnp.float32)
    for k, out_ref in enumerate(out_refs):
        member = lax.rem(family + k, sizes.structures)
        norm = jnp.zeros((sweeps, 128), jnp.float32)
        for place in range(3):
            point = coords_ref[member, place]
            out_ref[pl.ds(place, sweeps, stride=4), :] = point
            high = rounded(point)
            near = high + rounded(point - high)
            norm = norm - 0.5 * CONTACT_SLOPE * near * near
        out_ref[pl.ds(3, sweeps, stride=4), :] = norm
        counts = counts_ref[member][:, 0, :].astype(jnp.float32)
        out_ref[4 * sweeps : 5 * sweeps] = jnp.dot(counts, spread, preferred_element_type=jnp.float32)


def merge_kernel(points, after_ref, *refs):
    counts = refs[0][points:]
    for k, ref in enumerate(refs[:-1]):
        refs[-1][k * points : (k + 1) * points] = ref[:points]
        counts = counts + ref[points:] if k else counts
    refs[-1][(len(refs) - 1) * points :] = counts


def join_kernel(*refs):
    rows = refs[0].shape[0]
    for k, ref in enumerate(refs[:-1]):
        refs[-1][k * rows : (k + 1) * rows] = ref[...]


def list_kernel(sizes, lengths_ref, pairs_ref, list_ref, digits_ref):
    slots, sweeps, groups = sizes.slots, sizes.sweeps, sizes.groups
    family = lax.div(lax.axis_index("row"), sizes.share)
    here = lax.rem(lax.axis_index("row"), sizes.share) * sizes.n_col + lax.axis_index("col")
    lane = lax.broadcasted_iota(jnp.int32, (1, 128), 1)

    slot_row = lax.broadcasted_iota(jnp.int32, (slots, 128), 0)
    block = modulo(slot_row, sweeps) * groups + divide(slot_row, sweeps) * sizes.plane + here
    first_bead = block * 128
    low = jnp.zeros((slots, 128), jnp.int32)
    high = jnp.full((slots, 128), sizes.blocks * 128)
    end = jnp.int32(0)
    for k in range(lengths_ref.shape[0]):
        start = end
        end = end + lengths_ref[k]
        low = jnp.maximum(low, jnp.where(start <= first_bead, start, 0))
        high = jnp.minimum(high, jnp.where(end > first_bead + 127, end, sizes.blocks * 128))
    low = jnp.maximum(low >> 7, block - (sizes.width - 1))
    high = jnp.minimum(jnp.minimum((high - 1) >> 7, block + (sizes.width - 1)), sizes.blocks - 1)
    reach = []
    for value in (low, high, (high - low + 2) >> 1):
        reach.append(jnp.sum(jnp.where(slot_row == lane, value, 0), axis=0, keepdims=True))
    steps = lax.div(jnp.sum(reach[2]) + (UNIT // 2 - 1), UNIT // 2)

    half = pairs_ref.shape[2] // 128
    lines = 2 * half
    pairs = pairs_ref[family]
    group = modulo(pairs, groups)
    mine = modulo(group, sizes.plane) == here
    slot = jnp.where(mine, divide(group, sizes.plane) * sweeps + divide(pairs, groups), -1)
    other = sizes.at(pairs)

    def cut(value, line):
        side, at = line // half, line % half * 128
        return value[side : side + 1, at : at + 128]

    before = lax.broadcasted_iota(jnp.int32, (128, 256), 0)
    after = lax.broadcasted_iota(jnp.int32, (128, 256), 1)
    count = (before <= after).astype(jnp.float32).astype(jnp.bfloat16)
    running = jnp.zeros((slots, 128), jnp.float32)
    picked = []
    for line in range(lines):
        chosen = (cut(slot, line) == slot_row).astype(jnp.float32)
        counted = jnp.dot(chosen.astype(jnp.bfloat16), count, preferred_element_type=jnp.float32)
        inner = jnp.sum(chosen * (counted[:, :128] - 1.0 + running), axis=0, keepdims=True)
        picked.append((chosen, inner))
        running = running + counted[:, 128:]
    doubled = 2.0 * jnp.floor(0.5 * (running + 1.0))
    lower = (
        lax.broadcasted_iota(jnp.int32, (slots, slots), 0) > lax.broadcasted_iota(jnp.int32, (slots, slots), 1)
    ).astype(jnp.float32)
    base = jnp.dot(lower, doubled, precision=lax.Precision.HIGHEST, preferred_element_type=jnp.float32)
    number = jnp.max(base + doubled).astype(jnp.int32)
    digit_row = lax.broadcasted_iota(jnp.int32, (POINT_ROWS, 128), 0)
    ranks = []
    for line in range(lines):
        chosen, inner = picked[line]
        rank = inner + jnp.sum(chosen * base, axis=0, keepdims=True)
        ranks.append(jnp.where(cut(slot, line) >= 0, rank.astype(jnp.int32), -1))
        opposite = (line + half) % lines
        partner = cut(other, opposite)
        digits = jnp.zeros((POINT_ROWS, 128), jnp.int32)
        for place, digit in enumerate(
            (partner & 31, partner >> 5, cut(slot, line), lane, line % half + 0 * lane, 1 + 0 * lane)
        ):
            digits = jnp.where(digit_row == place, digit, digits)
        digits_ref[line] = digits.astype(jnp.float32).astype(jnp.bfloat16)
    chunks = (list_ref.shape[0] - 8) // 2
    spot = lax.broadcasted_iota(jnp.int32, (128, 128), 0)

    def compact(chunk, carry):
        found = jnp.zeros((POINT_ROWS, 128), jnp.float32)
        for line in range(0, lines, 2):
            there = jnp.concatenate(
                [(ranks[line + i] == spot + chunk * 128).astype(jnp.float32).astype(jnp.bfloat16) for i in range(2)],
                axis=1,
            )
            found = found + lax.dot_general(
                jnp.concatenate([digits_ref[line], digits_ref[line + 1]], axis=1),
                there,
                (((1,), (1,)), ((), ())),
                preferred_element_type=jnp.float32,
            )
        found = found.astype(jnp.int32)
        at = found[2:3]
        code = found[0:1] + (found[1:2] << 5) + ((slots + at) << 12) + (at << 19)
        list_ref[pl.ds(chunk, 1), :] = jnp.where(found[5:6] > 0, code, slots << 19)
        list_ref[pl.ds(chunks + chunk, 1), :] = (
            sizes.plane * sweeps * 128 + found[3:4] + found[4:5] * 128
        )
        return carry

    lax.fori_loop(0, lax.div(number + 2 * UNIT - 1, 128) + 1, compact, 0)
    end = 2 * chunks
    list_ref[end : end + 1] = jnp.full((1, 128), number)
    list_ref[end + 1 : end + 2] = reach[0]
    list_ref[end + 2 : end + 3] = reach[1]
    list_ref[end + 3 : end + 4] = jnp.full((1, 128), steps)


def own_kernel(sizes, lengths_ref, own_ref, first_ref, marks_ref, starts_ref, ends_ref):
    slots, sweeps, groups = sizes.slots, sizes.sweeps, sizes.groups
    family = lax.div(lax.axis_index("row"), sizes.share)
    here = lax.rem(lax.axis_index("row"), sizes.share) * sizes.n_col + lax.axis_index("col")
    lane = lax.broadcasted_iota(jnp.int32, (1, 128), 1)
    row = lax.broadcasted_iota(jnp.int32, (8, 128), 0)
    labels = starts_ref.shape[0]
    depth = POINT_ROWS + labels

    starts_ref[...] = jnp.zeros_like(starts_ref)
    ends_ref[...] = jnp.zeros_like(ends_ref)
    end = jnp.int32(0)
    for k in range(lengths_ref.shape[0]):
        starts_ref[k : k + 1] = jnp.full((1, 128), end)
        end = end + lengths_ref[k]
        ends_ref[k : k + 1] = jnp.full((1, 128), end)

    def mark(group, carry):
        for u in range(sweeps):
            bead = (u * groups + group) * 128 + lane
            inside = (bead >= starts_ref[...]) & (bead < ends_ref[...])
            marks_ref[group * sweeps + u] = inside.astype(jnp.float32).astype(jnp.bfloat16)
        return carry

    lax.fori_loop(0, groups, mark, 0)

    def fill(turn, carry):
        origin = lax.rem(family + (sizes.structures - turn), sizes.structures)
        for pair in range(sweeps // 2):
            value = own_ref[pl.ds(pl.multiple_of(turn * sweeps * 4 + pair * 8, 8), 8), :]
            for odd in range(2):
                value = pltpu.roll(value, 4, 0) if odd else value
                high = rounded(value)
                low = rounded(value - high)
                shifted = value + 0.5 * CONTACT_SHIFT
                shifted_high = rounded(shifted)
                shifted_low = rounded(shifted - shifted_high)
                both = jnp.where(row < 4, high, pltpu.roll(high, 4, 0))
                near = jnp.where((row & 3) == 3, 1.0, CONTACT_SLOPE * both)
                rest = jnp.where(row == 4, pltpu.roll(shifted_low, 1, 0), 0.0)
                rest = jnp.where(row == 3, shifted_high, rest)
                rest = jnp.where(row < 3, CONTACT_SLOPE * low, rest)
                u = 2 * pair + odd
                bead = (u * groups + origin * sizes.plane + here) * 128 + lane
                inside = (bead >= starts_ref[...]) & (bead < ends_ref[...])
                apart = jnp.where(inside, 0.0, -FAR)
                blank = jnp.zeros((128 - depth, 128), jnp.float32)
                turned = jnp.transpose(jnp.concatenate([near, rest, apart, blank], axis=0))
                slot = origin * sweeps + u
                first_ref[slot] = turned[:, :depth].astype(jnp.bfloat16)
                other = jnp.where(lane < POINT_ROWS, turned, -FAR - turned)
                first_ref[slots + slot] = other[:, :depth].astype(jnp.bfloat16)
        return carry

    lax.fori_loop(0, sizes.structures, fill, 0)


def tile_kernel(sizes, list_ref, listed_ref, first_ref, marks_ref, same_ref, across_ref, *refs):
    structures, sweeps, slots = sizes.structures, sizes.sweeps, sizes.slots
    out_refs = refs[:structures]
    second_ref, counts_ref, held_ref, sums_ref, picks_ref, diag_ref, total_ref = refs[structures:]
    row_here = lax.axis_index("row")
    column_here = lax.axis_index("col")
    family = lax.div(row_here, sizes.share)
    chip_here = lax.rem(row_here, sizes.share) * sizes.half + lax.div(column_here, 2)
    core_here = lax.rem(column_here, 2)
    lane = lax.broadcasted_iota(jnp.int32, (1, 128), 1)
    row = lax.broadcasted_iota(jnp.int32, (8, 128), 0)
    ones = jnp.where((row == 3) | (row == 4), 1.0, 0.0)

    for core, piece_ref in ((core_here, same_ref), (1 - core_here, across_ref)):
        for k in range(sizes.chips):
            chip = lax.rem(chip_here + (sizes.chips - k), sizes.chips)
            device = chip * 2 + core
            base = k * sizes.rows
            counts_ref[pl.ds(pl.multiple_of(device * sweeps, sweeps), sweeps), :] = piece_ref[
                base + slots * 4 : base + slots * 4 + sweeps
            ]
            for turn in range(structures):
                origin = lax.rem(family + (structures - turn), structures)
                at = (origin * sizes.plane + device) * sweeps
                for pair in range(sweeps // 2):
                    start = base + turn * sweeps * 4 + pair * 8
                    value = piece_ref[start : start + 8]
                    high = rounded(value)
                    low = value - high
                    high_turned = pltpu.roll(high, 4, 0)
                    even = jnp.concatenate(
                        [jnp.where(row < 4, high, pltpu.roll(low, 4, 0)), jnp.where(row < 3, high, ones)],
                        axis=0,
                    )
                    odd = jnp.concatenate(
                        [jnp.where(row < 4, high_turned, low), jnp.where(row < 3, high_turned, ones)],
                        axis=0,
                    )
                    second_ref[at + 2 * pair] = even.astype(jnp.bfloat16)
                    second_ref[at + 2 * pair + 1] = odd.astype(jnp.bfloat16)
    listed_base = sizes.plane * sweeps
    chosen = lax.broadcasted_iota(jnp.int32, (structures, 128), 0) == family
    for k in range(listed_ref.shape[1] // 128):
        line = jnp.where(chosen, listed_ref[:, k * 128 : (k + 1) * 128], 0)
        counts_ref[listed_base + k : listed_base + k + 1] = jnp.sum(line, axis=0, keepdims=True).astype(
            jnp.float32
        )
    chunks = (list_ref.shape[0] - 8) // 2

    total_ref[...] = jnp.zeros_like(total_ref)
    spare = 1.0 / (1.0 + jnp.exp(jnp.float32(-CONTACT_SHIFT)))

    here = lax.rem(row_here, sizes.share) * sizes.n_col + column_here
    groups = sizes.groups

    def step(ending, beginning):
        sums = sums_ref[pl.ds(0, UNIT, stride=8), :]
        for k in range(1, 8):
            sums = sums + sums_ref[pl.ds(k, UNIT, stride=8), :]
        chance = 64.0 * 128.0 + 0.5 * jnp.sum(sums, axis=1, keepdims=True)
        count = jnp.sum(picks_ref[...], axis=1, keepdims=True)
        chance = jnp.where(diag_ref[...] > 0.5, 0.5 * (chance - 128.0 * spare), chance)
        weight = 1.0 - count / (BACKGROUND + chance / 128.0)
        for t in range(0, UNIT, 2):
            left, right = (second_ref[ending[t + i] & 4095] for i in range(2))
            product = lax.dot_general(
                jnp.concatenate([left, right], axis=0),
                held_ref[t * 128 : (t + 2) * 128],
                (((1,), (1,)), ((), ())),
                preferred_element_type=jnp.float32,
            )
            for i in range(2):
                gain = product[i * POINT_ROWS : (i + 1) * POINT_ROWS, i * 128 : (i + 1) * 128]
                at = pl.multiple_of((ending[t + i] >> 19) * POINT_ROWS, POINT_ROWS)
                total_ref[pl.ds(at, POINT_ROWS), :] += weight[t + i : t + i + 1] * gain
        for t in range(0, UNIT, 2):
            seconds = [beginning[t + i][0] & 4095 for i in range(2)]
            logit = jnp.dot(
                first_ref[(beginning[t][0] >> 12) & 127],
                jnp.concatenate(
                    [jnp.concatenate([second_ref[at], marks_ref[at]], axis=0) for at in seconds], axis=1
                ),
                preferred_element_type=jnp.float32,
            )
            bend = jnp.tanh(logit)
            rest = 1.0 - bend * bend
            for i in range(2):
                part = bend[:, i * 128 : (i + 1) * 128]
                sums_ref[(t + i) * 8 : (t + i + 1) * 8] = jnp.sum(part.reshape(16, 8, 128), axis=0)
                held_ref[(t + i) * 128 : (t + i + 1) * 128] = rest[:, i * 128 : (i + 1) * 128].astype(
                    jnp.bfloat16
                )
                code, place, diagonal = beginning[t + i]
                picked = counts_ref[pl.ds(place >> 7, 1), :]
                picks_ref[t + i : t + i + 1] = jnp.where(lane == (place & 127), picked, 0.0)
                diag_ref[t + i : t + i + 1] = jnp.full((1, 128), diagonal)
        return tuple(code for code, _, _ in beginning)

    def band_step(turn, carry):
        slot, other, ending = carry
        beginning = []
        for _ in range(UNIT // 2):
            block = modulo(slot, sweeps) * groups + divide(slot, sweeps) * sizes.plane + here
            high = list_ref[2 * chunks + 2, slot]
            for i in range(2):
                second = jnp.minimum(other + i, high)
                first = jnp.minimum(block, second)
                group = modulo(first, groups)
                line = modulo(group, sizes.plane) * sweeps + divide(first, groups)
                apart = jnp.abs(block - second)
                place = line * 128 + divide(group, sizes.plane) * sizes.width + apart
                total = jnp.where(other + i <= high, slot, slots)
                code = sizes.at(second) + (jnp.minimum(slot, slots - 1) << 12) + (total << 19)
                beginning.append((code, place, (apart == 0).astype(jnp.float32)))
            over = other + 2 > high
            slot = jnp.minimum(slot + over.astype(jnp.int32), slots)
            other = jnp.where(over, list_ref[2 * chunks + 1, slot], other + 2)
        return slot, other, step(ending, beginning)

    def listed_step(turn, ending):
        beginning = []
        for t in range(UNIT):
            at = turn * UNIT + t
            beginning.append(
                (list_ref[at >> 7, at & 127], list_ref[chunks + (at >> 7), at & 127], jnp.float32(0.0))
            )
        return step(ending, beginning)

    idle = (jnp.int32(slots << 19),) * UNIT
    sums_ref[...] = jnp.zeros_like(sums_ref)
    carry = (jnp.int32(0), list_ref[2 * chunks + 1, 0], idle)
    ending = lax.fori_loop(0, list_ref[2 * chunks + 3, 0], band_step, carry)[2]
    listed_steps = lax.div(list_ref[2 * chunks, 0] + UNIT - 1, UNIT)
    lax.fori_loop(0, listed_steps + 1, listed_step, ending)

    scale = -2.0 * CONTACT_SLOPE / 128.0 / 4.0
    for k in range(structures):
        origin = lax.rem(family + k, structures)
        turn = (structures - k) % structures
        first = origin * sweeps * POINT_ROWS
        mass = total_ref[pl.ds(first + 11, sweeps, stride=POINT_ROWS), :]
        for place in range(3):
            point = same_ref[pl.ds(turn * sweeps * 4 + place, sweeps, stride=4), :]
            high = rounded(point)
            near = high + rounded(point - high)
            pull = (
                total_ref[pl.ds(first + place, sweeps, stride=POINT_ROWS), :]
                + total_ref[pl.ds(first + place + 4, sweeps, stride=POINT_ROWS), :]
            )
            out_refs[k][place] = scale * (near * mass - pull)


def place_kernel(sizes, *refs):
    family = lax.div(lax.axis_index("row"), sizes.share)
    for k, ref in enumerate(refs[:-1]):
        refs[-1][lax.rem(family + (sizes.structures - k), sizes.structures)] = ref[...]


def on_device(n_row, n_col, coords, chrom_lengths, band_counts, inter_pairs, inter_counts):
    structures, _, sweeps, block_size = coords.shape
    width = band_counts.shape[3]
    listed = inter_pairs.shape[1]
    sizes = Sizes(n_row, n_col, structures, sweeps, width)
    share, slots, blocks = sizes.share, sizes.slots, sizes.blocks

    messages = pl.pallas_call(
        functools.partial(pack_kernel, sizes),
        out_shape=[jax.ShapeDtypeStruct((5 * sweeps, block_size), jnp.float32)] * structures,
        in_specs=[VMEM, VMEM],
        out_specs=[VMEM] * structures,
        compiler_params=SMALL,
        name="pack",
    )(coords, band_counts)
    deal = [
        [(i, (i // share + k) % structures * share + i % share) for i in range(n_row)]
        for k in range(structures)
    ]
    received = [messages[0]]
    for k in range(1, structures):
        received.append(lax.ppermute(messages[k], "row", deal[k]))
    chunks = -(-(2 * listed + slots + 2 * UNIT) // block_size)
    tiles = pl.pallas_call(
        functools.partial(list_kernel, sizes),
        out_shape=jax.ShapeDtypeStruct((2 * chunks + 8, block_size), jnp.int32),
        in_specs=[SMEM, VMEM],
        out_specs=VMEM,
        scratch_shapes=[pltpu.VMEM((2 * listed // block_size, POINT_ROWS, block_size), jnp.bfloat16)],
        compiler_params=SMALL,
        name="list_tiles",
    )(chrom_lengths, jnp.transpose(inter_pairs, (0, 2, 1)))

    own_row = pl.pallas_call(
        functools.partial(merge_kernel, 4 * sweeps),
        out_shape=jax.ShapeDtypeStruct((sizes.rows, block_size), jnp.float32),
        in_specs=[ANY] + [VMEM] * structures,
        out_specs=VMEM,
        compiler_params=SMALL,
        name="merge",
    )(tiles, *received)

    def device(family, chip, core):
        row = family * share + chip // sizes.half
        return row * n_col + chip % sizes.half * 2 + core

    pieces = [own_row]
    for k in range(1, sizes.chips):
        moves = [
            (device(f, i, core), device(f, (i + k) % sizes.chips, core))
            for f in range(structures)
            for i in range(sizes.chips)
            for core in range(2)
        ]
        pieces.append(lax.ppermute(own_row, AXES, moves))
    same = pl.pallas_call(
        join_kernel,
        out_shape=jax.ShapeDtypeStruct((sizes.chips * sizes.rows, block_size), jnp.float32),
        in_specs=[VMEM] * sizes.chips,
        out_specs=VMEM,
        compiler_params=SMALL,
        name="join",
    )(*pieces)
    across = lax.ppermute(same, "col", [(i, i ^ 1) for i in range(n_col)])

    labels = -(-chrom_lengths.shape[0] // 16) * 16
    depth = POINT_ROWS + labels
    own, marks = pl.pallas_call(
        functools.partial(own_kernel, sizes),
        out_shape=[
            jax.ShapeDtypeStruct((2 * slots, block_size, depth), jnp.bfloat16),
            jax.ShapeDtypeStruct((blocks, labels, block_size), jnp.bfloat16),
        ],
        in_specs=[SMEM, VMEM],
        out_specs=[VMEM] * 2,
        scratch_shapes=[
            pltpu.VMEM((labels, block_size), jnp.int32),
            pltpu.VMEM((labels, block_size), jnp.int32),
        ],
        cost_estimate=pl.CostEstimate(flops=1 << 30, bytes_accessed=1 << 23, transcendentals=0),
        compiler_params=pltpu.CompilerParams(vmem_limit_bytes=24 * 1024 * 1024),
        name="own_features",
    )(chrom_lengths, own_row)

    gains = pl.pallas_call(
        functools.partial(tile_kernel, sizes),
        out_shape=[jax.ShapeDtypeStruct((3, sweeps, block_size), jnp.float32)] * structures,
        in_specs=[SMEM] + [VMEM] * 5,
        out_specs=[VMEM] * structures,
        scratch_shapes=[
            pltpu.VMEM((blocks, POINT_ROWS, block_size), jnp.bfloat16),
            pltpu.VMEM((sizes.plane * sweeps + listed // block_size, block_size), jnp.float32),
            pltpu.VMEM((UNIT * block_size, block_size), jnp.bfloat16),
            pltpu.VMEM((UNIT * 8, block_size), jnp.float32),
            pltpu.VMEM((UNIT, block_size), jnp.float32),
            pltpu.VMEM((UNIT, block_size), jnp.float32),
            pltpu.VMEM(((slots + 1) * POINT_ROWS, block_size), jnp.float32),
        ],
        compiler_params=pltpu.CompilerParams(vmem_limit_bytes=40 * 1024 * 1024),
        name="tiles",
    )(tiles, inter_counts, own, marks, same, across)

    arrived = [gains[0]]
    for k in range(1, structures):
        arrived.append(lax.ppermute(gains[k], "row", deal[k]))
    return pl.pallas_call(
        functools.partial(place_kernel, sizes),
        out_shape=jax.ShapeDtypeStruct(coords.shape, jnp.float32),
        in_specs=[VMEM] * structures,
        out_specs=VMEM,
        compiler_params=SMALL,
        name="place",
    )(*arrived)


def solution(mesh):
    placed = (
        P(None, None, None, ("row", "col")),
        P(),
        P(None, None, ("row", "col"), None),
        P(),
        P(),
    )
    return jax.shard_map(
        functools.partial(on_device, mesh.shape["row"], mesh.shape["col"]),
        mesh=mesh,
        in_specs=placed,
        out_specs=P(None, None, None, ("row", "col")),
        check_vma=False,
    )
```

```python
import functools

import jax
import jax.numpy as jnp
from jax import lax
from jax.experimental import pallas as pl
from jax.experimental.pallas import tpu as pltpu
from jax.sharding import PartitionSpec as P

CONTACT_SHIFT = 3.0
CONTACT_SLOPE = 0.5
BACKGROUND = 0.5
FAR = 32.0
UNIT = 32
POINT_ROWS = 16
AXES = ("row", "col")
VMEM = pl.BlockSpec(memory_space=pltpu.VMEM)
SMEM = pl.BlockSpec(memory_space=pltpu.SMEM)
ANY = pl.BlockSpec(memory_space=pl.ANY)
SMALL = pltpu.CompilerParams(vmem_limit_bytes=8 * 1024 * 1024)


def rounded(value):
    return value.astype(jnp.bfloat16).astype(jnp.float32)


def divide(value, by):
    return value >> (by.bit_length() - 1) if by & (by - 1) == 0 else lax.div(value, by)


def modulo(value, by):
    return value & (by - 1) if by & (by - 1) == 0 else lax.rem(value, by)


class Sizes:
    def __init__(self, n_row, n_col, structures, sweeps, width):
        self.n_row, self.n_col, self.structures, self.sweeps = n_row, n_col, structures, sweeps
        self.width = width
        self.share = n_row // structures
        self.plane = self.share * n_col
        self.chips = self.plane // 2
        self.half = n_col // 2
        self.groups = n_row * n_col
        self.blocks = self.groups * sweeps
        self.slots = structures * sweeps
        self.rows = self.slots * 4 + sweeps

    def at(self, block):
        return modulo(block, self.groups) * self.sweeps + divide(block, self.groups)


def pack_kernel(sizes, coords_ref, counts_ref, *out_refs):
    sweeps, width = sizes.sweeps, sizes.width
    family = lax.div(lax.axis_index("row"), sizes.share)
    lane = lax.broadcasted_iota(jnp.int32, (width, 128), 1)
    place = lax.broadcasted_iota(jnp.int32, (width, 128), 0) + family * width
    spread = (lane == place).astype(jnp.float32)
    for k, out_ref in enumerate(out_refs):
        member = lax.rem(family + k, sizes.structures)
        norm = jnp.zeros((sweeps, 128), jnp.float32)
        for place in range(3):
            point = coords_ref[member, place]
            out_ref[pl.ds(place, sweeps, stride=4), :] = point
            high = rounded(point)
            near = high + rounded(point - high)
            norm = norm - 0.5 * CONTACT_SLOPE * near * near
        out_ref[pl.ds(3, sweeps, stride=4), :] = norm
        counts = counts_ref[member][:, 0, :].astype(jnp.float32)
        out_ref[4 * sweeps : 5 * sweeps] = jnp.dot(counts, spread, preferred_element_type=jnp.float32)


def merge_kernel(points, after_ref, *refs):
    counts = refs[0][points:]
    for k, ref in enumerate(refs[:-1]):
        refs[-1][k * points : (k + 1) * points] = ref[:points]
        counts = counts + ref[points:] if k else counts
    refs[-1][(len(refs) - 1) * points :] = counts


def join_kernel(after_ref, *refs):
    rows = refs[0].shape[0]
    for k, ref in enumerate(refs[:-1]):
        refs[-1][k * rows : (k + 1) * rows] = ref[...]


def list_kernel(sizes, lengths_ref, pairs_ref, list_ref, edges_ref, digits_ref):
    slots, sweeps, groups = sizes.slots, sizes.sweeps, sizes.groups
    family = lax.div(lax.axis_index("row"), sizes.share)
    here = lax.rem(lax.axis_index("row"), sizes.share) * sizes.n_col + lax.axis_index("col")
    lane = lax.broadcasted_iota(jnp.int32, (1, 128), 1)

    slot_row = lax.broadcasted_iota(jnp.int32, (slots, 128), 0)
    block = modulo(slot_row, sweeps) * groups + divide(slot_row, sweeps) * sizes.plane + here
    first_bead = block * 128
    low = jnp.zeros((slots, 128), jnp.int32)
    high = jnp.full((slots, 128), sizes.blocks * 128)
    edges_ref[...] = jnp.zeros_like(edges_ref)
    end = jnp.int32(0)
    for k in range(lengths_ref.shape[0]):
        start = end
        end = end + lengths_ref[k]
        edges_ref[0, k : k + 1] = jnp.full((1, 128), start)
        edges_ref[1, k : k + 1] = jnp.full((1, 128), end)
        low = jnp.maximum(low, jnp.where(start <= first_bead, start, 0))
        high = jnp.minimum(high, jnp.where(end > first_bead + 127, end, sizes.blocks * 128))
    low = jnp.maximum(low >> 7, block - (sizes.width - 1))
    high = jnp.minimum(jnp.minimum((high - 1) >> 7, block + (sizes.width - 1)), sizes.blocks - 1)
    reach = []
    for value in (low, high, (high - low + 2) >> 1):
        reach.append(jnp.sum(jnp.where(slot_row == lane, value, 0), axis=0, keepdims=True))
    steps = lax.div(jnp.sum(reach[2]) + (UNIT // 2 - 1), UNIT // 2)

    half = pairs_ref.shape[2] // 128
    lines = 2 * half
    pairs = pairs_ref[family]
    group = modulo(pairs, groups)
    mine = modulo(group, sizes.plane) == here
    slot = jnp.where(mine, divide(group, sizes.plane) * sweeps + divide(pairs, groups), -1)
    other = sizes.at(pairs)

    def cut(value, line):
        side, at = line // half, line % half * 128
        return value[side : side + 1, at : at + 128]

    before = lax.broadcasted_iota(jnp.int32, (128, 256), 0)
    after = lax.broadcasted_iota(jnp.int32, (128, 256), 1)
    count = (before <= after).astype(jnp.float32).astype(jnp.bfloat16)
    running = jnp.zeros((slots, 128), jnp.float32)
    picked = []
    for line in range(lines):
        chosen = (cut(slot, line) == slot_row).astype(jnp.float32)
        counted = jnp.dot(chosen.astype(jnp.bfloat16), count, preferred_element_type=jnp.float32)
        inner = jnp.sum(chosen * (counted[:, :128] - 1.0 + running), axis=0, keepdims=True)
        picked.append((chosen, inner))
        running = running + counted[:, 128:]
    doubled = 2.0 * jnp.floor(0.5 * (running + 1.0))
    lower = (
        lax.broadcasted_iota(jnp.int32, (slots, slots), 0) > lax.broadcasted_iota(jnp.int32, (slots, slots), 1)
    ).astype(jnp.float32)
    base = jnp.dot(lower, doubled, precision=lax.Precision.HIGHEST, preferred_element_type=jnp.float32)
    number = jnp.max(base + doubled).astype(jnp.int32)
    digit_row = lax.broadcasted_iota(jnp.int32, (POINT_ROWS, 128), 0)
    ranks = []
    for line in range(lines):
        chosen, inner = picked[line]
        rank = inner + jnp.sum(chosen * base, axis=0, keepdims=True)
        ranks.append(jnp.where(cut(slot, line) >= 0, rank.astype(jnp.int32), -1))
        opposite = (line + half) % lines
        partner = cut(other, opposite)
        digits = jnp.zeros((POINT_ROWS, 128), jnp.int32)
        for place, digit in enumerate(
            (partner & 31, partner >> 5, cut(slot, line), lane, line % half + 0 * lane, 1 + 0 * lane)
        ):
            digits = jnp.where(digit_row == place, digit, digits)
        digits_ref[line] = digits.astype(jnp.float32).astype(jnp.bfloat16)
    chunks = (list_ref.shape[0] - 8) // 2
    spot = lax.broadcasted_iota(jnp.int32, (128, 128), 0)

    def compact(chunk, carry):
        found = jnp.zeros((POINT_ROWS, 128), jnp.float32)
        for line in range(0, lines, 2):
            there = jnp.concatenate(
                [(ranks[line + i] == spot + chunk * 128).astype(jnp.float32).astype(jnp.bfloat16) for i in range(2)],
                axis=1,
            )
            found = found + lax.dot_general(
                jnp.concatenate([digits_ref[line], digits_ref[line + 1]], axis=1),
                there,
                (((1,), (1,)), ((), ())),
                preferred_element_type=jnp.float32,
            )
        found = found.astype(jnp.int32)
        at = found[2:3]
        code = found[0:1] + (found[1:2] << 5) + ((slots + at) << 12) + (at << 19)
        list_ref[pl.ds(chunk, 1), :] = jnp.where(found[5:6] > 0, code, slots << 19)
        list_ref[pl.ds(chunks + chunk, 1), :] = (
            sizes.plane * sweeps * 128 + found[3:4] + found[4:5] * 128
        )
        return carry

    lax.fori_loop(0, lax.div(number + 2 * UNIT - 1, 128) + 1, compact, 0)
    end = 2 * chunks
    list_ref[end : end + 1] = jnp.full((1, 128), number)
    list_ref[end + 1 : end + 2] = reach[0]
    list_ref[end + 2 : end + 3] = reach[1]
    list_ref[end + 3 : end + 4] = jnp.full((1, 128), steps)


def own_kernel(sizes, edges_ref, own_ref, first_ref, marks_ref):
    slots, sweeps, groups = sizes.slots, sizes.sweeps, sizes.groups
    family = lax.div(lax.axis_index("row"), sizes.share)
    here = lax.rem(lax.axis_index("row"), sizes.share) * sizes.n_col + lax.axis_index("col")
    lane = lax.broadcasted_iota(jnp.int32, (1, 128), 1)
    row = lax.broadcasted_iota(jnp.int32, (8, 128), 0)
    labels = edges_ref.shape[1]
    depth = POINT_ROWS + labels

    def mark(group, carry):
        for u in range(sweeps):
            bead = (u * groups + group) * 128 + lane
            inside = (bead >= edges_ref[0]) & (bead < edges_ref[1])
            marks_ref[group * sweeps + u] = inside.astype(jnp.float32).astype(jnp.bfloat16)
        return carry

    lax.fori_loop(0, groups, mark, 0)

    def fill(turn, carry):
        origin = lax.rem(family + (sizes.structures - turn), sizes.structures)
        for pair in range(sweeps // 2):
            value = own_ref[pl.ds(pl.multiple_of(turn * sweeps * 4 + pair * 8, 8), 8), :]
            for odd in range(2):
                value = pltpu.roll(value, 4, 0) if odd else value
                high = rounded(value)
                low = rounded(value - high)
                shifted = value + 0.5 * CONTACT_SHIFT
                shifted_high = rounded(shifted)
                shifted_low = rounded(shifted - shifted_high)
                both = jnp.where(row < 4, high, pltpu.roll(high, 4, 0))
                near = jnp.where((row & 3) == 3, 1.0, CONTACT_SLOPE * both)
                rest = jnp.where(row == 4, pltpu.roll(shifted_low, 1, 0), 0.0)
                rest = jnp.where(row == 3, shifted_high, rest)
                rest = jnp.where(row < 3, CONTACT_SLOPE * low, rest)
                u = 2 * pair + odd
                bead = (u * groups + origin * sizes.plane + here) * 128 + lane
                inside = (bead >= edges_ref[0]) & (bead < edges_ref[1])
                apart = jnp.where(inside, 0.0, -FAR)
                blank = jnp.zeros((128 - depth, 128), jnp.float32)
                turned = jnp.transpose(jnp.concatenate([near, rest, apart, blank], axis=0))
                slot = origin * sweeps + u
                first_ref[slot] = turned[:, :depth].astype(jnp.bfloat16)
                other = jnp.where(lane < POINT_ROWS, turned, -FAR - turned)
                first_ref[slots + slot] = other[:, :depth].astype(jnp.bfloat16)
        return carry

    lax.fori_loop(0, sizes.structures, fill, 0)


def tile_kernel(sizes, list_ref, listed_ref, first_ref, marks_ref, same_ref, across_ref, *refs):
    structures, sweeps, slots = sizes.structures, sizes.sweeps, sizes.slots
    out_refs = refs[:structures]
    second_ref, turned_ref, mask_ref, counts_ref, held_ref, sums_ref, picks_ref, state_ref, total_ref, gain_ref = refs[
        structures:
    ]
    row_here = lax.axis_index("row")
    column_here = lax.axis_index("col")
    family = lax.div(row_here, sizes.share)
    chip_here = lax.rem(row_here, sizes.share) * sizes.half + lax.div(column_here, 2)
    core_here = lax.rem(column_here, 2)
    lane = lax.broadcasted_iota(jnp.int32, (1, 128), 1)
    row = lax.broadcasted_iota(jnp.int32, (8, 128), 0)
    ones = jnp.where((row == 3) | (row == 4), 1.0, 0.0)
    unit = jnp.where(row == 3, 1.0, 0.0)
    for k in range(2 * sweeps):
        mask_ref[k] = jnp.broadcast_to(lane >> 3 == k, (16, 128)).astype(jnp.float32).astype(jnp.bfloat16)

    for core, piece_ref in ((core_here, same_ref), (1 - core_here, across_ref)):
        for k in range(sizes.chips):
            chip = lax.rem(chip_here + (sizes.chips - k), sizes.chips)
            device = chip * 2 + core
            base = k * sizes.rows
            counts_ref[pl.ds(pl.multiple_of(device * sweeps, sweeps), sweeps), :] = piece_ref[
                base + slots * 4 : base + slots * 4 + sweeps
            ]
            for turn in range(structures):
                origin = lax.rem(family + (structures - turn), structures)
                group = origin * sizes.plane + device
                columns = []
                for pair in range(sweeps // 2):
                    start = base + turn * sweeps * 4 + pair * 8
                    value = piece_ref[start : start + 8]
                    high = rounded(value)
                    low = value - high
                    high_turned = pltpu.roll(high, 4, 0)
                    for odd, (top, bottom) in enumerate(
                        ((high, pltpu.roll(low, 4, 0)), (high_turned, low))
                    ):
                        points = jnp.where(row < 4, top, bottom)
                        features = jnp.concatenate([points, jnp.where(row < 3, top, ones)], axis=0)
                        second_ref[group * sweeps + 2 * pair + odd] = features.astype(jnp.bfloat16)
                        columns.append(jnp.where((row & 3) == 3, unit, points))
                turned_ref[group] = jnp.transpose(jnp.concatenate(columns * 2, axis=0)).astype(jnp.bfloat16)
    listed_base = sizes.plane * sweeps
    chosen = lax.broadcasted_iota(jnp.int32, (structures, 128), 0) == family
    for k in range(listed_ref.shape[1] // 128):
        line = jnp.where(chosen, listed_ref[:, k * 128 : (k + 1) * 128], 0)
        counts_ref[listed_base + k : listed_base + k + 1] = jnp.sum(line, axis=0, keepdims=True).astype(
            jnp.float32
        )
    chunks = (list_ref.shape[0] - 8) // 2

    total_ref[...] = jnp.zeros_like(total_ref)
    spare = 1.0 / (1.0 + jnp.exp(jnp.float32(-CONTACT_SHIFT)))

    here = lax.rem(row_here, sizes.share) * sizes.n_col + column_here
    groups = sizes.groups

    def step(ending, beginning):
        sums = sums_ref[pl.ds(0, UNIT, stride=8), :]
        for k in range(1, 8):
            sums = sums + sums_ref[pl.ds(k, UNIT, stride=8), :]
        chance = 64.0 * 128.0 + 0.5 * jnp.sum(sums, axis=1, keepdims=True)
        count = jnp.sum(picks_ref[...], axis=1, keepdims=True)
        state = state_ref[...]
        chance = jnp.where(state == 1.0, 0.5 * (chance - 128.0 * spare), chance)
        weight = jnp.where(state == 2.0, 0.0, 1.0 - count / (BACKGROUND + chance / 128.0))
        for t in range(0, UNIT, 2):
            columns = []
            for i in range(2):
                at = ending[t + i] & 4095
                mask = mask_ref[modulo(at, sweeps) + i * sweeps]
                column = turned_ref[divide(at, sweeps)].reshape(8, 16, 128) * mask[None]
                columns.append(column.reshape(128, 128))
            product = jnp.dot(
                held_ref[t // 2], jnp.concatenate(columns, axis=0), preferred_element_type=jnp.float32
            )
            scale = jnp.where(lane < 64, weight[t : t + 1], weight[t + 1 : t + 2])
            total_ref[ending[t] >> 19] += scale * product
        for t in range(0, UNIT, 2):
            seconds = [beginning[t + i][0] & 4095 for i in range(2)]
            logit = jnp.dot(
                first_ref[(beginning[t][0] >> 12) & 127],
                jnp.concatenate(
                    [jnp.concatenate([second_ref[at], marks_ref[at]], axis=0) for at in seconds], axis=1
                ),
                preferred_element_type=jnp.float32,
            )
            bend = jnp.tanh(logit)
            held_ref[t // 2] = (1.0 - bend * bend).astype(jnp.bfloat16)
            for i in range(2):
                part = bend[:, i * 128 : (i + 1) * 128]
                sums_ref[(t + i) * 8 : (t + i + 1) * 8] = jnp.sum(part.reshape(16, 8, 128), axis=0)
                code, place, state = beginning[t + i]
                picked = counts_ref[pl.ds(place >> 7, 1), :]
                picks_ref[t + i : t + i + 1] = jnp.where(lane == (place & 127), picked, 0.0)
                state_ref[t + i : t + i + 1] = jnp.full((1, 128), state)
        return tuple(code for code, _, _ in beginning)

    def band_step(turn, carry):
        slot, other, ending = carry
        beginning = []
        for _ in range(UNIT // 2):
            block = modulo(slot, sweeps) * groups + divide(slot, sweeps) * sizes.plane + here
            high = list_ref[2 * chunks + 2, slot]
            for i in range(2):
                second = jnp.minimum(other + i, high)
                first = jnp.minimum(block, second)
                group = modulo(first, groups)
                line = modulo(group, sizes.plane) * sweeps + divide(first, groups)
                apart = jnp.abs(block - second)
                place = line * 128 + divide(group, sizes.plane) * sizes.width + apart
                live = (other + i <= high) & (slot < slots)
                code = sizes.at(second) + (jnp.minimum(slot, slots - 1) << 12) + (slot << 19)
                state = jnp.where(live, (apart == 0).astype(jnp.float32), 2.0)
                beginning.append((code, place, state))
            over = other + 2 > high
            slot = jnp.minimum(slot + over.astype(jnp.int32), slots)
            other = jnp.where(over, list_ref[2 * chunks + 1, slot], other + 2)
        return slot, other, step(ending, beginning)

    def listed_step(turn, ending):
        beginning = []
        for t in range(UNIT):
            at = turn * UNIT + t
            code = list_ref[at >> 7, at & 127]
            state = jnp.where(code >> 19 < slots, 0.0, 2.0)
            beginning.append((code, list_ref[chunks + (at >> 7), at & 127], state))
        return step(ending, beginning)

    idle = (jnp.int32(slots << 19),) * UNIT
    sums_ref[...] = jnp.zeros_like(sums_ref)
    carry = (jnp.int32(0), list_ref[2 * chunks + 1, 0], idle)
    ending = lax.fori_loop(0, list_ref[2 * chunks + 3, 0], band_step, carry)[2]
    listed_steps = lax.div(list_ref[2 * chunks, 0] + UNIT - 1, UNIT)
    lax.fori_loop(0, listed_steps + 1, listed_step, ending)

    def collect(slot, carry):
        turned = jnp.transpose(total_ref[slot])
        gain_ref[pl.ds(pl.multiple_of(slot * 8, 8), 8), :] = jnp.sum(turned.reshape(16, 8, 128), axis=0)
        return carry

    lax.fori_loop(0, slots, collect, 0, unroll=4)
    scale = -2.0 * CONTACT_SLOPE / 128.0 / 4.0
    for k in range(structures):
        origin = lax.rem(family + k, structures)
        turn = (structures - k) % structures
        first = origin * sweeps * 8
        mass = gain_ref[pl.ds(first + 3, sweeps, stride=8), :]
        for place in range(3):
            point = same_ref[pl.ds(turn * sweeps * 4 + place, sweeps, stride=4), :]
            high = rounded(point)
            near = high + rounded(point - high)
            pull = (
                gain_ref[pl.ds(first + place, sweeps, stride=8), :]
                + gain_ref[pl.ds(first + place + 4, sweeps, stride=8), :]
            )
            out_refs[k][place] = scale * (near * mass - pull)


def place_kernel(sizes, *refs):
    family = lax.div(lax.axis_index("row"), sizes.share)
    for k, ref in enumerate(refs[:-1]):
        refs[-1][lax.rem(family + (sizes.structures - k), sizes.structures)] = ref[...]


def on_device(n_row, n_col, coords, chrom_lengths, band_counts, inter_pairs, inter_counts):
    structures, _, sweeps, block_size = coords.shape
    width = band_counts.shape[3]
    listed = inter_pairs.shape[1]
    sizes = Sizes(n_row, n_col, structures, sweeps, width)
    share, slots, blocks = sizes.share, sizes.slots, sizes.blocks

    messages = pl.pallas_call(
        functools.partial(pack_kernel, sizes),
        out_shape=[jax.ShapeDtypeStruct((5 * sweeps, block_size), jnp.float32)] * structures,
        in_specs=[VMEM, VMEM],
        out_specs=[VMEM] * structures,
        compiler_params=SMALL,
        name="pack",
    )(coords, band_counts)
    deal = [
        [(i, (i // share + k) % structures * share + i % share) for i in range(n_row)]
        for k in range(structures)
    ]
    received = [messages[0]]
    for k in range(1, structures):
        received.append(lax.ppermute(messages[k], "row", deal[k]))
    chunks = -(-(2 * listed + slots + 2 * UNIT) // block_size)
    labels = -(-chrom_lengths.shape[0] // 16) * 16
    tiles, edges = pl.pallas_call(
        functools.partial(list_kernel, sizes),
        out_shape=[
            jax.ShapeDtypeStruct((2 * chunks + 8, block_size), jnp.int32),
            jax.ShapeDtypeStruct((2, labels, block_size), jnp.int32),
        ],
        in_specs=[SMEM, VMEM],
        out_specs=[VMEM] * 2,
        scratch_shapes=[pltpu.VMEM((2 * listed // block_size, POINT_ROWS, block_size), jnp.bfloat16)],
        compiler_params=SMALL,
        name="list_tiles",
    )(chrom_lengths, jnp.transpose(inter_pairs, (0, 2, 1)))

    own_row = pl.pallas_call(
        functools.partial(merge_kernel, 4 * sweeps),
        out_shape=jax.ShapeDtypeStruct((sizes.rows, block_size), jnp.float32),
        in_specs=[ANY] + [VMEM] * structures,
        out_specs=VMEM,
        compiler_params=SMALL,
        name="merge",
    )(tiles, *received)

    def device(family, chip, core):
        row = family * share + chip // sizes.half
        return row * n_col + chip % sizes.half * 2 + core

    pieces = [own_row]
    for k in range(1, sizes.chips):
        moves = [
            (device(f, i, core), device(f, (i + k) % sizes.chips, core))
            for f in range(structures)
            for i in range(sizes.chips)
            for core in range(2)
        ]
        pieces.append(lax.ppermute(own_row, AXES, moves))
    depth = POINT_ROWS + labels
    own, marks = pl.pallas_call(
        functools.partial(own_kernel, sizes),
        out_shape=[
            jax.ShapeDtypeStruct((2 * slots, block_size, depth), jnp.bfloat16),
            jax.ShapeDtypeStruct((blocks, labels, block_size), jnp.bfloat16),
        ],
        in_specs=[VMEM, VMEM],
        out_specs=[VMEM] * 2,
        compiler_params=pltpu.CompilerParams(vmem_limit_bytes=24 * 1024 * 1024),
        name="own_features",
    )(edges, own_row)

    same = pl.pallas_call(
        join_kernel,
        out_shape=jax.ShapeDtypeStruct((sizes.chips * sizes.rows, block_size), jnp.float32),
        in_specs=[ANY] + [VMEM] * sizes.chips,
        out_specs=VMEM,
        compiler_params=SMALL,
        name="join",
    )(marks, *pieces)
    across = lax.ppermute(same, "col", [(i, i ^ 1) for i in range(n_col)])

    gains = pl.pallas_call(
        functools.partial(tile_kernel, sizes),
        out_shape=[jax.ShapeDtypeStruct((3, sweeps, block_size), jnp.float32)] * structures,
        in_specs=[SMEM] + [VMEM] * 5,
        out_specs=[VMEM] * structures,
        scratch_shapes=[
            pltpu.VMEM((blocks, POINT_ROWS, block_size), jnp.bfloat16),
            pltpu.VMEM((sizes.groups, block_size, block_size), jnp.bfloat16),
            pltpu.VMEM((2 * sweeps, POINT_ROWS, block_size), jnp.bfloat16),
            pltpu.VMEM((sizes.plane * sweeps + listed // block_size, block_size), jnp.float32),
            pltpu.VMEM((UNIT // 2, block_size, 2 * block_size), jnp.bfloat16),
            pltpu.VMEM((UNIT * 8, block_size), jnp.float32),
            pltpu.VMEM((UNIT, block_size), jnp.float32),
            pltpu.VMEM((UNIT, block_size), jnp.float32),
            pltpu.VMEM((slots + 1, block_size, block_size), jnp.float32),
            pltpu.VMEM((slots * 8, block_size), jnp.float32),
        ],
        compiler_params=pltpu.CompilerParams(vmem_limit_bytes=40 * 1024 * 1024),
        name="tiles",
    )(tiles, inter_counts, own, marks, same, across)

    arrived = [gains[0]]
    for k in range(1, structures):
        arrived.append(lax.ppermute(gains[k], "row", deal[k]))
    return pl.pallas_call(
        functools.partial(place_kernel, sizes),
        out_shape=jax.ShapeDtypeStruct(coords.shape, jnp.float32),
        in_specs=[VMEM] * structures,
        out_specs=VMEM,
        compiler_params=SMALL,
        name="place",
    )(*arrived)


def solution(mesh):
    placed = (
        P(None, None, None, ("row", "col")),
        P(),
        P(None, None, ("row", "col"), None),
        P(),
        P(),
    )
    return jax.shard_map(
        functools.partial(on_device, mesh.shape["row"], mesh.shape["col"]),
        mesh=mesh,
        in_specs=placed,
        out_specs=P(None, None, None, ("row", "col")),
        check_vma=False,
    )
```

```python
import functools

import jax
import jax.numpy as jnp
from jax import lax
from jax.experimental import pallas as pl
from jax.experimental.pallas import tpu as pltpu
from jax.sharding import PartitionSpec as P

CONTACT_SHIFT = 3.0
CONTACT_SLOPE = 0.5
BACKGROUND = 0.5
LOG2E = 1.4426950408889634
FAR = 256.0
UNIT = 32
POINT_ROWS = 16
AXES = ("row", "col")
VMEM = pl.BlockSpec(memory_space=pltpu.VMEM)
SMEM = pl.BlockSpec(memory_space=pltpu.SMEM)
ANY = pl.BlockSpec(memory_space=pl.ANY)
SMALL = pltpu.CompilerParams(vmem_limit_bytes=8 * 1024 * 1024)


def rounded(value):
    return value.astype(jnp.bfloat16).astype(jnp.float32)


def divide(value, by):
    return value >> (by.bit_length() - 1) if by & (by - 1) == 0 else lax.div(value, by)


def modulo(value, by):
    return value & (by - 1) if by & (by - 1) == 0 else lax.rem(value, by)


class Sizes:
    def __init__(self, n_row, n_col, structures, sweeps, width):
        self.n_row, self.n_col, self.structures, self.sweeps = n_row, n_col, structures, sweeps
        self.width = width
        self.share = n_row // structures
        self.plane = self.share * n_col
        self.chips = self.plane // 2
        self.half = n_col // 2
        self.groups = n_row * n_col
        self.blocks = self.groups * sweeps
        self.slots = structures * sweeps
        self.rows = self.slots * 4 + sweeps

    def at(self, block):
        return modulo(block, self.groups) * self.sweeps + divide(block, self.groups)


def pack_kernel(sizes, coords_ref, counts_ref, *out_refs):
    sweeps, width = sizes.sweeps, sizes.width
    family = lax.div(lax.axis_index("row"), sizes.share)
    lane = lax.broadcasted_iota(jnp.int32, (width, 128), 1)
    place = lax.broadcasted_iota(jnp.int32, (width, 128), 0) + family * width
    spread = (lane == place).astype(jnp.float32)
    for k, out_ref in enumerate(out_refs):
        member = lax.rem(family + k, sizes.structures)
        norm = jnp.zeros((sweeps, 128), jnp.float32)
        for place in range(3):
            point = coords_ref[member, place]
            out_ref[pl.ds(place, sweeps, stride=4), :] = point
            high = rounded(point)
            near = high + rounded(point - high)
            norm = norm + LOG2E * CONTACT_SLOPE * near * near
        out_ref[pl.ds(3, sweeps, stride=4), :] = norm
        counts = counts_ref[member][:, 0, :].astype(jnp.float32)
        out_ref[4 * sweeps : 5 * sweeps] = jnp.dot(counts, spread, preferred_element_type=jnp.float32)


def merge_kernel(points, after_ref, *refs):
    counts = refs[0][points:]
    for k, ref in enumerate(refs[:-1]):
        refs[-1][k * points : (k + 1) * points] = ref[:points]
        counts = counts + ref[points:] if k else counts
    refs[-1][(len(refs) - 1) * points :] = counts


def join_kernel(after_ref, *refs):
    rows = refs[0].shape[0]
    for k, ref in enumerate(refs[:-1]):
        refs[-1][k * rows : (k + 1) * rows] = ref[...]


def list_kernel(sizes, lengths_ref, pairs_ref, list_ref, edges_ref, digits_ref):
    slots, sweeps, groups = sizes.slots, sizes.sweeps, sizes.groups
    family = lax.div(lax.axis_index("row"), sizes.share)
    here = lax.rem(lax.axis_index("row"), sizes.share) * sizes.n_col + lax.axis_index("col")
    lane = lax.broadcasted_iota(jnp.int32, (1, 128), 1)

    slot_row = lax.broadcasted_iota(jnp.int32, (slots, 128), 0)
    block = modulo(slot_row, sweeps) * groups + divide(slot_row, sweeps) * sizes.plane + here
    first_bead = block * 128
    low = jnp.zeros((slots, 128), jnp.int32)
    high = jnp.full((slots, 128), sizes.blocks * 128)
    edges_ref[...] = jnp.zeros_like(edges_ref)
    end = jnp.int32(0)
    for k in range(lengths_ref.shape[0]):
        start = end
        end = end + lengths_ref[k]
        edges_ref[0, k : k + 1] = jnp.full((1, 128), start)
        edges_ref[1, k : k + 1] = jnp.full((1, 128), end)
        low = jnp.maximum(low, jnp.where(start <= first_bead, start, 0))
        high = jnp.minimum(high, jnp.where(end > first_bead + 127, end, sizes.blocks * 128))
    low = jnp.maximum(low >> 7, block - (sizes.width - 1))
    high = jnp.minimum(jnp.minimum((high - 1) >> 7, block + (sizes.width - 1)), sizes.blocks - 1)
    reach = []
    for value in (low, high, (high - low + 2) >> 1):
        reach.append(jnp.sum(jnp.where(slot_row == lane, value, 0), axis=0, keepdims=True))
    steps = lax.div(jnp.sum(reach[2]) + (UNIT // 2 - 1), UNIT // 2)

    half = pairs_ref.shape[2] // 128
    lines = 2 * half
    pairs = pairs_ref[family]
    group = modulo(pairs, groups)
    mine = modulo(group, sizes.plane) == here
    slot = jnp.where(mine, divide(group, sizes.plane) * sweeps + divide(pairs, groups), -1)
    other = sizes.at(pairs)

    def cut(value, line):
        side, at = line // half, line % half * 128
        return value[side : side + 1, at : at + 128]

    before = lax.broadcasted_iota(jnp.int32, (128, 256), 0)
    after = lax.broadcasted_iota(jnp.int32, (128, 256), 1)
    count = (before <= after).astype(jnp.float32).astype(jnp.bfloat16)
    running = jnp.zeros((slots, 128), jnp.float32)
    picked = []
    for line in range(lines):
        chosen = (cut(slot, line) == slot_row).astype(jnp.float32)
        counted = jnp.dot(chosen.astype(jnp.bfloat16), count, preferred_element_type=jnp.float32)
        inner = jnp.sum(chosen * (counted[:, :128] - 1.0 + running), axis=0, keepdims=True)
        picked.append((chosen, inner))
        running = running + counted[:, 128:]
    doubled = 2.0 * jnp.floor(0.5 * (running + 1.0))
    lower = (
        lax.broadcasted_iota(jnp.int32, (slots, slots), 0) > lax.broadcasted_iota(jnp.int32, (slots, slots), 1)
    ).astype(jnp.float32)
    base = jnp.dot(lower, doubled, precision=lax.Precision.HIGHEST, preferred_element_type=jnp.float32)
    number = jnp.max(base + doubled).astype(jnp.int32)
    digit_row = lax.broadcasted_iota(jnp.int32, (POINT_ROWS, 128), 0)
    ranks = []
    for line in range(lines):
        chosen, inner = picked[line]
        rank = inner + jnp.sum(chosen * base, axis=0, keepdims=True)
        ranks.append(jnp.where(cut(slot, line) >= 0, rank.astype(jnp.int32), -1))
        opposite = (line + half) % lines
        partner = cut(other, opposite)
        digits = jnp.zeros((POINT_ROWS, 128), jnp.int32)
        for place, digit in enumerate(
            (partner & 31, partner >> 5, cut(slot, line), lane, line % half + 0 * lane, 1 + 0 * lane)
        ):
            digits = jnp.where(digit_row == place, digit, digits)
        digits_ref[line] = digits.astype(jnp.float32).astype(jnp.bfloat16)
    chunks = (list_ref.shape[0] - 8) // 2
    spot = lax.broadcasted_iota(jnp.int32, (128, 128), 0)

    def compact(chunk, carry):
        found = jnp.zeros((POINT_ROWS, 128), jnp.float32)
        for line in range(0, lines, 2):
            there = jnp.concatenate(
                [(ranks[line + i] == spot + chunk * 128).astype(jnp.float32).astype(jnp.bfloat16) for i in range(2)],
                axis=1,
            )
            found = found + lax.dot_general(
                jnp.concatenate([digits_ref[line], digits_ref[line + 1]], axis=1),
                there,
                (((1,), (1,)), ((), ())),
                preferred_element_type=jnp.float32,
            )
        found = found.astype(jnp.int32)
        at = found[2:3]
        code = found[0:1] + (found[1:2] << 5) + ((slots + at) << 12) + (at << 19)
        list_ref[pl.ds(chunk, 1), :] = jnp.where(found[5:6] > 0, code, slots << 19)
        list_ref[pl.ds(chunks + chunk, 1), :] = (
            sizes.plane * sweeps * 128 + found[3:4] + found[4:5] * 128
        )
        return carry

    lax.fori_loop(0, lax.div(number + 2 * UNIT - 1, 128) + 1, compact, 0)
    end = 2 * chunks
    list_ref[end : end + 1] = jnp.full((1, 128), number)
    list_ref[end + 1 : end + 2] = reach[0]
    list_ref[end + 2 : end + 3] = reach[1]
    list_ref[end + 3 : end + 4] = jnp.full((1, 128), steps)


def own_kernel(sizes, edges_ref, own_ref, first_ref, marks_ref):
    slots, sweeps, groups = sizes.slots, sizes.sweeps, sizes.groups
    family = lax.div(lax.axis_index("row"), sizes.share)
    here = lax.rem(lax.axis_index("row"), sizes.share) * sizes.n_col + lax.axis_index("col")
    lane = lax.broadcasted_iota(jnp.int32, (1, 128), 1)
    row = lax.broadcasted_iota(jnp.int32, (8, 128), 0)
    labels = edges_ref.shape[1]
    depth = POINT_ROWS + labels

    def mark(group, carry):
        for u in range(sweeps):
            bead = (u * groups + group) * 128 + lane
            inside = (bead >= edges_ref[0]) & (bead < edges_ref[1])
            marks_ref[group * sweeps + u] = inside.astype(jnp.float32).astype(jnp.bfloat16)
        return carry

    lax.fori_loop(0, groups, mark, 0)

    def fill(turn, carry):
        origin = lax.rem(family + (sizes.structures - turn), sizes.structures)
        for pair in range(sweeps // 2):
            value = own_ref[pl.ds(pl.multiple_of(turn * sweeps * 4 + pair * 8, 8), 8), :]
            for odd in range(2):
                value = pltpu.roll(value, 4, 0) if odd else value
                high = rounded(value)
                low = rounded(value - high)
                scaled = -2.0 * LOG2E * CONTACT_SLOPE * (high + low)
                scaled_high = rounded(scaled)
                scaled_low = rounded(scaled - scaled_high)
                shifted = value - LOG2E * CONTACT_SHIFT
                shifted_high = rounded(shifted)
                shifted_low = rounded(shifted - shifted_high)
                both = jnp.where(row < 4, scaled_high, pltpu.roll(scaled_high, 4, 0))
                near = jnp.where((row & 3) == 3, 1.0, both)
                rest = jnp.where(row == 4, pltpu.roll(shifted_low, 1, 0), 0.0)
                rest = jnp.where(row == 3, shifted_high, rest)
                rest = jnp.where(row < 3, scaled_low, rest)
                u = 2 * pair + odd
                bead = (u * groups + origin * sizes.plane + here) * 128 + lane
                inside = (bead >= edges_ref[0]) & (bead < edges_ref[1])
                apart = jnp.where(inside, 0.0, FAR)
                blank = jnp.zeros((128 - depth, 128), jnp.float32)
                turned = jnp.transpose(jnp.concatenate([near, rest, apart, blank], axis=0))
                slot = origin * sweeps + u
                first_ref[slot] = turned[:, :depth].astype(jnp.bfloat16)
                other = jnp.where(lane < POINT_ROWS, turned, FAR - turned)
                first_ref[slots + slot] = other[:, :depth].astype(jnp.bfloat16)
        return carry

    lax.fori_loop(0, sizes.structures, fill, 0)


def tile_kernel(sizes, list_ref, listed_ref, first_ref, marks_ref, same_ref, across_ref, *refs):
    structures, sweeps, slots = sizes.structures, sizes.sweeps, sizes.slots
    out_refs = refs[:structures]
    second_ref, turned_ref, mask_ref, counts_ref, held_ref, sums_ref, picks_ref, state_ref, total_ref, gain_ref = refs[
        structures:
    ]
    row_here = lax.axis_index("row")
    column_here = lax.axis_index("col")
    family = lax.div(row_here, sizes.share)
    chip_here = lax.rem(row_here, sizes.share) * sizes.half + lax.div(column_here, 2)
    core_here = lax.rem(column_here, 2)
    lane = lax.broadcasted_iota(jnp.int32, (1, 128), 1)
    row = lax.broadcasted_iota(jnp.int32, (8, 128), 0)
    ones = jnp.where((row == 3) | (row == 4), 1.0, 0.0)
    unit = jnp.where(row == 3, 1.0, 0.0)
    for k in range(2 * sweeps):
        mask_ref[k] = jnp.broadcast_to(lane >> 3 == k, (16, 128)).astype(jnp.float32).astype(jnp.bfloat16)

    for core, piece_ref in ((core_here, same_ref), (1 - core_here, across_ref)):
        for k in range(sizes.chips):
            chip = lax.rem(chip_here + (sizes.chips - k), sizes.chips)
            device = chip * 2 + core
            base = k * sizes.rows
            counts_ref[pl.ds(pl.multiple_of(device * sweeps, sweeps), sweeps), :] = piece_ref[
                base + slots * 4 : base + slots * 4 + sweeps
            ]
            for turn in range(structures):
                origin = lax.rem(family + (structures - turn), structures)
                group = origin * sizes.plane + device
                columns = []
                for pair in range(sweeps // 2):
                    start = base + turn * sweeps * 4 + pair * 8
                    value = piece_ref[start : start + 8]
                    high = rounded(value)
                    low = value - high
                    high_turned = pltpu.roll(high, 4, 0)
                    for odd, (top, bottom) in enumerate(
                        ((high, pltpu.roll(low, 4, 0)), (high_turned, low))
                    ):
                        points = jnp.where(row < 4, top, bottom)
                        features = jnp.concatenate([points, jnp.where(row < 3, top, ones)], axis=0)
                        second_ref[group * sweeps + 2 * pair + odd] = features.astype(jnp.bfloat16)
                        columns.append(jnp.where((row & 3) == 3, unit, points))
                turned_ref[group] = jnp.transpose(jnp.concatenate(columns * 2, axis=0)).astype(jnp.bfloat16)
    listed_base = sizes.plane * sweeps
    chosen = lax.broadcasted_iota(jnp.int32, (structures, 128), 0) == family
    for k in range(listed_ref.shape[1] // 128):
        line = jnp.where(chosen, listed_ref[:, k * 128 : (k + 1) * 128], 0)
        counts_ref[listed_base + k : listed_base + k + 1] = jnp.sum(line, axis=0, keepdims=True).astype(
            jnp.float32
        )
    chunks = (list_ref.shape[0] - 8) // 2

    total_ref[...] = jnp.zeros_like(total_ref)
    spare = 1.0 / (1.0 + jnp.exp(jnp.float32(-CONTACT_SHIFT)))

    here = lax.rem(row_here, sizes.share) * sizes.n_col + column_here
    groups = sizes.groups

    def step(ending, beginning):
        sums = sums_ref[pl.ds(0, UNIT, stride=8), :]
        for k in range(1, 8):
            sums = sums + sums_ref[pl.ds(k, UNIT, stride=8), :]
        chance = jnp.sum(sums, axis=1, keepdims=True)
        count = jnp.sum(picks_ref[...], axis=1, keepdims=True)
        state = state_ref[...]
        chance = jnp.where(state == 1.0, 0.5 * (chance - 128.0 * spare), chance)
        weight = jnp.where(state == 2.0, 0.0, 1.0 - count / (BACKGROUND + chance / 128.0))
        for t in range(0, UNIT, 2):
            columns = []
            for i in range(2):
                at = ending[t + i] & 4095
                mask = mask_ref[modulo(at, sweeps) + i * sweeps]
                column = turned_ref[divide(at, sweeps)].reshape(8, 16, 128) * mask[None]
                columns.append(column.reshape(128, 128))
            product = jnp.dot(
                held_ref[t // 2], jnp.concatenate(columns, axis=0), preferred_element_type=jnp.float32
            )
            scale = jnp.where(lane < 64, weight[t : t + 1], weight[t + 1 : t + 2])
            total_ref[ending[t] >> 19] += scale * product
        for t in range(0, UNIT, 2):
            seconds = [beginning[t + i][0] & 4095 for i in range(2)]
            power = jnp.dot(
                first_ref[(beginning[t][0] >> 12) & 127],
                jnp.concatenate(
                    [jnp.concatenate([second_ref[at], marks_ref[at]], axis=0) for at in seconds], axis=1
                ),
                preferred_element_type=jnp.float32,
            )
            chance = pl.reciprocal(1.0 + jnp.exp2(power), approx=True)
            held_ref[t // 2] = (chance - chance * chance).astype(jnp.bfloat16)
            for i in range(2):
                part = chance[:, i * 128 : (i + 1) * 128]
                sums_ref[(t + i) * 8 : (t + i + 1) * 8] = jnp.sum(part.reshape(16, 8, 128), axis=0)
                code, place, state = beginning[t + i]
                picked = counts_ref[pl.ds(place >> 7, 1), :]
                picks_ref[t + i : t + i + 1] = jnp.where(lane == (place & 127), picked, 0.0)
                state_ref[t + i : t + i + 1] = jnp.full((1, 128), state)
        return tuple(code for code, _, _ in beginning)

    def band_step(turn, carry):
        slot, other, ending = carry
        beginning = []
        for _ in range(UNIT // 2):
            block = modulo(slot, sweeps) * groups + divide(slot, sweeps) * sizes.plane + here
            high = list_ref[2 * chunks + 2, slot]
            for i in range(2):
                second = jnp.minimum(other + i, high)
                first = jnp.minimum(block, second)
                group = modulo(first, groups)
                line = modulo(group, sizes.plane) * sweeps + divide(first, groups)
                apart = jnp.abs(block - second)
                place = line * 128 + divide(group, sizes.plane) * sizes.width + apart
                live = (other + i <= high) & (slot < slots)
                code = sizes.at(second) + (jnp.minimum(slot, slots - 1) << 12) + (slot << 19)
                state = jnp.where(live, (apart == 0).astype(jnp.float32), 2.0)
                beginning.append((code, place, state))
            over = other + 2 > high
            slot = jnp.minimum(slot + over.astype(jnp.int32), slots)
            other = jnp.where(over, list_ref[2 * chunks + 1, slot], other + 2)
        return slot, other, step(ending, beginning)

    def listed_step(turn, ending):
        beginning = []
        for t in range(UNIT):
            at = turn * UNIT + t
            code = list_ref[at >> 7, at & 127]
            state = jnp.where(code >> 19 < slots, 0.0, 2.0)
            beginning.append((code, list_ref[chunks + (at >> 7), at & 127], state))
        return step(ending, beginning)

    idle = (jnp.int32(slots << 19),) * UNIT
    sums_ref[...] = jnp.zeros_like(sums_ref)
    carry = (jnp.int32(0), list_ref[2 * chunks + 1, 0], idle)
    ending = lax.fori_loop(0, list_ref[2 * chunks + 3, 0], band_step, carry)[2]
    listed_steps = lax.div(list_ref[2 * chunks, 0] + UNIT - 1, UNIT)
    lax.fori_loop(0, listed_steps + 1, listed_step, ending)

    def collect(slot, carry):
        turned = jnp.transpose(total_ref[slot])
        gain_ref[pl.ds(pl.multiple_of(slot * 8, 8), 8), :] = jnp.sum(turned.reshape(16, 8, 128), axis=0)
        return carry

    lax.fori_loop(0, slots, collect, 0, unroll=4)
    scale = -2.0 * CONTACT_SLOPE / 128.0
    for k in range(structures):
        origin = lax.rem(family + k, structures)
        turn = (structures - k) % structures
        first = origin * sweeps * 8
        mass = gain_ref[pl.ds(first + 3, sweeps, stride=8), :]
        for place in range(3):
            point = same_ref[pl.ds(turn * sweeps * 4 + place, sweeps, stride=4), :]
            high = rounded(point)
            near = high + rounded(point - high)
            pull = (
                gain_ref[pl.ds(first + place, sweeps, stride=8), :]
                + gain_ref[pl.ds(first + place + 4, sweeps, stride=8), :]
            )
            out_refs[k][place] = scale * (near * mass - pull)


def place_kernel(sizes, *refs):
    family = lax.div(lax.axis_index("row"), sizes.share)
    for k, ref in enumerate(refs[:-1]):
        refs[-1][lax.rem(family + (sizes.structures - k), sizes.structures)] = ref[...]


def on_device(n_row, n_col, coords, chrom_lengths, band_counts, inter_pairs, inter_counts):
    structures, _, sweeps, block_size = coords.shape
    width = band_counts.shape[3]
    listed = inter_pairs.shape[1]
    sizes = Sizes(n_row, n_col, structures, sweeps, width)
    share, slots, blocks = sizes.share, sizes.slots, sizes.blocks

    messages = pl.pallas_call(
        functools.partial(pack_kernel, sizes),
        out_shape=[jax.ShapeDtypeStruct((5 * sweeps, block_size), jnp.float32)] * structures,
        in_specs=[VMEM, VMEM],
        out_specs=[VMEM] * structures,
        compiler_params=SMALL,
        name="pack",
    )(coords, band_counts)
    deal = [
        [(i, (i // share + k) % structures * share + i % share) for i in range(n_row)]
        for k in range(structures)
    ]
    received = [messages[0]]
    for k in range(1, structures):
        received.append(lax.ppermute(messages[k], "row", deal[k]))
    chunks = -(-(2 * listed + slots + 2 * UNIT) // block_size)
    labels = -(-chrom_lengths.shape[0] // 16) * 16
    tiles, edges = pl.pallas_call(
        functools.partial(list_kernel, sizes),
        out_shape=[
            jax.ShapeDtypeStruct((2 * chunks + 8, block_size), jnp.int32),
            jax.ShapeDtypeStruct((2, labels, block_size), jnp.int32),
        ],
        in_specs=[SMEM, VMEM],
        out_specs=[VMEM] * 2,
        scratch_shapes=[pltpu.VMEM((2 * listed // block_size, POINT_ROWS, block_size), jnp.bfloat16)],
        compiler_params=SMALL,
        name="list_tiles",
    )(chrom_lengths, jnp.transpose(inter_pairs, (0, 2, 1)))

    own_row = pl.pallas_call(
        functools.partial(merge_kernel, 4 * sweeps),
        out_shape=jax.ShapeDtypeStruct((sizes.rows, block_size), jnp.float32),
        in_specs=[ANY] + [VMEM] * structures,
        out_specs=VMEM,
        compiler_params=SMALL,
        name="merge",
    )(tiles, *received)

    def device(family, chip, core):
        row = family * share + chip // sizes.half
        return row * n_col + chip % sizes.half * 2 + core

    pieces = [own_row]
    for k in range(1, sizes.chips):
        moves = [
            (device(f, i, core), device(f, (i + k) % sizes.chips, core))
            for f in range(structures)
            for i in range(sizes.chips)
            for core in range(2)
        ]
        pieces.append(lax.ppermute(own_row, AXES, moves))
    depth = POINT_ROWS + labels
    own, marks = pl.pallas_call(
        functools.partial(own_kernel, sizes),
        out_shape=[
            jax.ShapeDtypeStruct((2 * slots, block_size, depth), jnp.bfloat16),
            jax.ShapeDtypeStruct((blocks, labels, block_size), jnp.bfloat16),
        ],
        in_specs=[VMEM, VMEM],
        out_specs=[VMEM] * 2,
        compiler_params=pltpu.CompilerParams(vmem_limit_bytes=24 * 1024 * 1024),
        name="own_features",
    )(edges, own_row)

    same = pl.pallas_call(
        join_kernel,
        out_shape=jax.ShapeDtypeStruct((sizes.chips * sizes.rows, block_size), jnp.float32),
        in_specs=[ANY] + [VMEM] * sizes.chips,
        out_specs=VMEM,
        compiler_params=SMALL,
        name="join",
    )(marks, *pieces)
    across = lax.ppermute(same, "col", [(i, i ^ 1) for i in range(n_col)])

    gains = pl.pallas_call(
        functools.partial(tile_kernel, sizes),
        out_shape=[jax.ShapeDtypeStruct((3, sweeps, block_size), jnp.float32)] * structures,
        in_specs=[SMEM] + [VMEM] * 5,
        out_specs=[VMEM] * structures,
        scratch_shapes=[
            pltpu.VMEM((blocks, POINT_ROWS, block_size), jnp.bfloat16),
            pltpu.VMEM((sizes.groups, block_size, block_size), jnp.bfloat16),
            pltpu.VMEM((2 * sweeps, POINT_ROWS, block_size), jnp.bfloat16),
            pltpu.VMEM((sizes.plane * sweeps + listed // block_size, block_size), jnp.float32),
            pltpu.VMEM((UNIT // 2, block_size, 2 * block_size), jnp.bfloat16),
            pltpu.VMEM((UNIT * 8, block_size), jnp.float32),
            pltpu.VMEM((UNIT, block_size), jnp.float32),
            pltpu.VMEM((UNIT, block_size), jnp.float32),
            pltpu.VMEM((slots + 1, block_size, block_size), jnp.float32),
            pltpu.VMEM((slots * 8, block_size), jnp.float32),
        ],
        compiler_params=pltpu.CompilerParams(vmem_limit_bytes=40 * 1024 * 1024),
        name="tiles",
    )(tiles, inter_counts, own, marks, same, across)

    arrived = [gains[0]]
    for k in range(1, structures):
        arrived.append(lax.ppermute(gains[k], "row", deal[k]))
    return pl.pallas_call(
        functools.partial(place_kernel, sizes),
        out_shape=jax.ShapeDtypeStruct(coords.shape, jnp.float32),
        in_specs=[VMEM] * structures,
        out_specs=VMEM,
        compiler_params=SMALL,
        name="place",
    )(*arrived)


def solution(mesh):
    placed = (
        P(None, None, None, ("row", "col")),
        P(),
        P(None, None, ("row", "col"), None),
        P(),
        P(),
    )
    return jax.shard_map(
        functools.partial(on_device, mesh.shape["row"], mesh.shape["col"]),
        mesh=mesh,
        in_specs=placed,
        out_specs=P(None, None, None, ("row", "col")),
        check_vma=False,
    )
```

```python
import functools

import jax
import jax.numpy as jnp
from jax import lax
from jax.experimental import pallas as pl
from jax.experimental.pallas import tpu as pltpu
from jax.sharding import PartitionSpec as P

CONTACT_SHIFT = 3.0
CONTACT_SLOPE = 0.5
BACKGROUND = 0.5
FAR = 32.0
UNIT = 32
POINT_ROWS = 16
AXES = ("row", "col")
VMEM = pl.BlockSpec(memory_space=pltpu.VMEM)
SMEM = pl.BlockSpec(memory_space=pltpu.SMEM)
ANY = pl.BlockSpec(memory_space=pl.ANY)
SMALL = pltpu.CompilerParams(vmem_limit_bytes=8 * 1024 * 1024)


def rounded(value):
    return value.astype(jnp.bfloat16).astype(jnp.float32)


def divide(value, by):
    return value >> (by.bit_length() - 1) if by & (by - 1) == 0 else lax.div(value, by)


def modulo(value, by):
    return value & (by - 1) if by & (by - 1) == 0 else lax.rem(value, by)


class Sizes:
    def __init__(self, n_row, n_col, structures, sweeps, width):
        self.n_row, self.n_col, self.structures, self.sweeps = n_row, n_col, structures, sweeps
        self.width = width
        self.share = n_row // structures
        self.plane = self.share * n_col
        self.chips = self.plane // 2
        self.half = n_col // 2
        self.groups = n_row * n_col
        self.blocks = self.groups * sweeps
        self.slots = structures * sweeps
        self.rows = self.slots * 4 + sweeps

    def at(self, block):
        return modulo(block, self.groups) * self.sweeps + divide(block, self.groups)


def pack_kernel(sizes, coords_ref, counts_ref, *out_refs):
    sweeps, width = sizes.sweeps, sizes.width
    family = lax.div(lax.axis_index("row"), sizes.share)
    lane = lax.broadcasted_iota(jnp.int32, (width, 128), 1)
    place = lax.broadcasted_iota(jnp.int32, (width, 128), 0) + family * width
    spread = (lane == place).astype(jnp.float32)
    for k, out_ref in enumerate(out_refs):
        member = lax.rem(family + k, sizes.structures)
        norm = jnp.zeros((sweeps, 128), jnp.float32)
        for place in range(3):
            point = coords_ref[member, place]
            out_ref[pl.ds(place, sweeps, stride=4), :] = point
            high = rounded(point)
            near = high + rounded(point - high)
            norm = norm - 0.5 * CONTACT_SLOPE * near * near
        out_ref[pl.ds(3, sweeps, stride=4), :] = norm
        counts = counts_ref[member][:, 0, :].astype(jnp.float32)
        out_ref[4 * sweeps : 5 * sweeps] = jnp.dot(counts, spread, preferred_element_type=jnp.float32)


def merge_kernel(points, after_ref, *refs):
    counts = refs[0][points:]
    for k, ref in enumerate(refs[:-1]):
        refs[-1][k * points : (k + 1) * points] = ref[:points]
        counts = counts + ref[points:] if k else counts
    refs[-1][(len(refs) - 1) * points :] = counts


def join_kernel(after_ref, *refs):
    rows = refs[0].shape[0]
    for k, ref in enumerate(refs[:-1]):
        refs[-1][k * rows : (k + 1) * rows] = ref[...]


def list_kernel(sizes, lengths_ref, pairs_ref, list_ref, edges_ref, digits_ref):
    slots, sweeps, groups = sizes.slots, sizes.sweeps, sizes.groups
    family = lax.div(lax.axis_index("row"), sizes.share)
    here = lax.rem(lax.axis_index("row"), sizes.share) * sizes.n_col + lax.axis_index("col")
    lane = lax.broadcasted_iota(jnp.int32, (1, 128), 1)

    slot_row = lax.broadcasted_iota(jnp.int32, (slots, 128), 0)
    block = modulo(slot_row, sweeps) * groups + divide(slot_row, sweeps) * sizes.plane + here
    first_bead = block * 128
    low = jnp.zeros((slots, 128), jnp.int32)
    high = jnp.full((slots, 128), sizes.blocks * 128)
    edges_ref[...] = jnp.zeros_like(edges_ref)
    end = jnp.int32(0)
    for k in range(lengths_ref.shape[0]):
        start = end
        end = end + lengths_ref[k]
        edges_ref[0, k : k + 1] = jnp.full((1, 128), start)
        edges_ref[1, k : k + 1] = jnp.full((1, 128), end)
        low = jnp.maximum(low, jnp.where(start <= first_bead, start, 0))
        high = jnp.minimum(high, jnp.where(end > first_bead + 127, end, sizes.blocks * 128))
    low = jnp.maximum(low >> 7, block - (sizes.width - 1))
    high = jnp.minimum(jnp.minimum((high - 1) >> 7, block + (sizes.width - 1)), sizes.blocks - 1)
    reach = []
    for value in (low, high, (high - low + 2) >> 1):
        reach.append(jnp.sum(jnp.where(slot_row == lane, value, 0), axis=0, keepdims=True))
    steps = lax.div(jnp.sum(reach[2]) + (UNIT // 2 - 1), UNIT // 2)

    half = pairs_ref.shape[2] // 128
    lines = 2 * half
    pairs = pairs_ref[family]
    group = modulo(pairs, groups)
    mine = modulo(group, sizes.plane) == here
    slot = jnp.where(mine, divide(group, sizes.plane) * sweeps + divide(pairs, groups), -1)
    other = sizes.at(pairs)

    def cut(value, line):
        side, at = line // half, line % half * 128
        return value[side : side + 1, at : at + 128]

    before = lax.broadcasted_iota(jnp.int32, (128, 256), 0)
    after = lax.broadcasted_iota(jnp.int32, (128, 256), 1)
    count = (before <= after).astype(jnp.float32).astype(jnp.bfloat16)
    running = jnp.zeros((slots, 128), jnp.float32)
    picked = []
    for line in range(lines):
        chosen = (cut(slot, line) == slot_row).astype(jnp.float32)
        counted = jnp.dot(chosen.astype(jnp.bfloat16), count, preferred_element_type=jnp.float32)
        inner = jnp.sum(chosen * (counted[:, :128] - 1.0 + running), axis=0, keepdims=True)
        picked.append((chosen, inner))
        running = running + counted[:, 128:]
    doubled = 2.0 * jnp.floor(0.5 * (running + 1.0))
    lower = (
        lax.broadcasted_iota(jnp.int32, (slots, slots), 0) > lax.broadcasted_iota(jnp.int32, (slots, slots), 1)
    ).astype(jnp.float32)
    base = jnp.dot(lower, doubled, precision=lax.Precision.HIGHEST, preferred_element_type=jnp.float32)
    number = jnp.max(base + doubled).astype(jnp.int32)
    digit_row = lax.broadcasted_iota(jnp.int32, (POINT_ROWS, 128), 0)
    ranks = []
    for line in range(lines):
        chosen, inner = picked[line]
        rank = inner + jnp.sum(chosen * base, axis=0, keepdims=True)
        ranks.append(jnp.where(cut(slot, line) >= 0, rank.astype(jnp.int32), -1))
        opposite = (line + half) % lines
        partner = cut(other, opposite)
        digits = jnp.zeros((POINT_ROWS, 128), jnp.int32)
        for place, digit in enumerate(
            (partner & 31, partner >> 5, cut(slot, line), lane, line % half + 0 * lane, 1 + 0 * lane)
        ):
            digits = jnp.where(digit_row == place, digit, digits)
        digits_ref[line] = digits.astype(jnp.float32).astype(jnp.bfloat16)
    chunks = (list_ref.shape[0] - 8) // 2
    spot = lax.broadcasted_iota(jnp.int32, (128, 128), 0)

    def compact(chunk, carry):
        found = jnp.zeros((POINT_ROWS, 128), jnp.float32)
        for line in range(0, lines, 2):
            there = jnp.concatenate(
                [(ranks[line + i] == spot + chunk * 128).astype(jnp.float32).astype(jnp.bfloat16) for i in range(2)],
                axis=1,
            )
            found = found + lax.dot_general(
                jnp.concatenate([digits_ref[line], digits_ref[line + 1]], axis=1),
                there,
                (((1,), (1,)), ((), ())),
                preferred_element_type=jnp.float32,
            )
        found = found.astype(jnp.int32)
        at = found[2:3]
        code = found[0:1] + (found[1:2] << 5) + ((slots + at) << 12) + (at << 19)
        list_ref[pl.ds(chunk, 1), :] = jnp.where(found[5:6] > 0, code, slots << 19)
        list_ref[pl.ds(chunks + chunk, 1), :] = (
            sizes.plane * sweeps * 128 + found[3:4] + found[4:5] * 128
        )
        return carry

    lax.fori_loop(0, lax.div(number + 2 * UNIT - 1, 128) + 1, compact, 0)
    end = 2 * chunks
    list_ref[end : end + 1] = jnp.full((1, 128), number)
    list_ref[end + 1 : end + 2] = reach[0]
    list_ref[end + 2 : end + 3] = reach[1]
    list_ref[end + 3 : end + 4] = jnp.full((1, 128), steps)


def own_kernel(sizes, edges_ref, own_ref, first_ref, marks_ref):
    slots, sweeps, groups = sizes.slots, sizes.sweeps, sizes.groups
    family = lax.div(lax.axis_index("row"), sizes.share)
    here = lax.rem(lax.axis_index("row"), sizes.share) * sizes.n_col + lax.axis_index("col")
    lane = lax.broadcasted_iota(jnp.int32, (1, 128), 1)
    row = lax.broadcasted_iota(jnp.int32, (8, 128), 0)
    labels = edges_ref.shape[1]
    depth = POINT_ROWS + labels

    def mark(group, carry):
        for u in range(sweeps):
            bead = (u * groups + group) * 128 + lane
            inside = (bead >= edges_ref[0]) & (bead < edges_ref[1])
            marks_ref[group * sweeps + u] = inside.astype(jnp.float32).astype(jnp.bfloat16)
        return carry

    lax.fori_loop(0, groups, mark, 0)

    def fill(turn, carry):
        origin = lax.rem(family + (sizes.structures - turn), sizes.structures)
        for pair in range(sweeps // 2):
            value = own_ref[pl.ds(pl.multiple_of(turn * sweeps * 4 + pair * 8, 8), 8), :]
            for odd in range(2):
                value = pltpu.roll(value, 4, 0) if odd else value
                high = rounded(value)
                low = rounded(value - high)
                shifted = value + 0.5 * CONTACT_SHIFT
                shifted_high = rounded(shifted)
                shifted_low = rounded(shifted - shifted_high)
                both = jnp.where(row < 4, high, pltpu.roll(high, 4, 0))
                near = jnp.where((row & 3) == 3, 1.0, CONTACT_SLOPE * both)
                rest = jnp.where(row == 4, pltpu.roll(shifted_low, 1, 0), 0.0)
                rest = jnp.where(row == 3, shifted_high, rest)
                rest = jnp.where(row < 3, CONTACT_SLOPE * low, rest)
                u = 2 * pair + odd
                bead = (u * groups + origin * sizes.plane + here) * 128 + lane
                inside = (bead >= edges_ref[0]) & (bead < edges_ref[1])
                apart = jnp.where(inside, 0.0, -FAR)
                blank = jnp.zeros((128 - depth, 128), jnp.float32)
                turned = jnp.transpose(jnp.concatenate([near, rest, apart, blank], axis=0))
                slot = origin * sweeps + u
                first_ref[slot] = turned[:, :depth].astype(jnp.bfloat16)
                other = jnp.where(lane < POINT_ROWS, turned, -FAR - turned)
                first_ref[slots + slot] = other[:, :depth].astype(jnp.bfloat16)
        return carry

    lax.fori_loop(0, sizes.structures, fill, 0)


def tile_kernel(sizes, list_ref, listed_ref, first_ref, marks_ref, same_ref, across_ref, *refs):
    structures, sweeps, slots = sizes.structures, sizes.sweeps, sizes.slots
    out_refs = refs[:structures]
    second_ref, counts_ref, held_ref, sums_ref, picks_ref, state_ref, total_ref, gain_ref = refs[structures:]
    row_here = lax.axis_index("row")
    column_here = lax.axis_index("col")
    family = lax.div(row_here, sizes.share)
    chip_here = lax.rem(row_here, sizes.share) * sizes.half + lax.div(column_here, 2)
    core_here = lax.rem(column_here, 2)
    lane = lax.broadcasted_iota(jnp.int32, (1, 128), 1)
    row = lax.broadcasted_iota(jnp.int32, (8, 128), 0)
    ones = jnp.where((row == 3) | (row == 4), 1.0, 0.0)
    narrow = lax.broadcasted_iota(jnp.int32, (1, 2 * POINT_ROWS), 1)

    for core, piece_ref in ((core_here, same_ref), (1 - core_here, across_ref)):
        for k in range(sizes.chips):
            chip = lax.rem(chip_here + (sizes.chips - k), sizes.chips)
            device = chip * 2 + core
            base = k * sizes.rows
            counts_ref[pl.ds(pl.multiple_of(device * sweeps, sweeps), sweeps), :] = piece_ref[
                base + slots * 4 : base + slots * 4 + sweeps
            ]
            for turn in range(structures):
                origin = lax.rem(family + (structures - turn), structures)
                group = origin * sizes.plane + device
                for pair in range(sweeps // 2):
                    start = base + turn * sweeps * 4 + pair * 8
                    value = piece_ref[start : start + 8]
                    high = rounded(value)
                    low = value - high
                    high_turned = pltpu.roll(high, 4, 0)
                    for odd, (top, bottom) in enumerate(
                        ((high, pltpu.roll(low, 4, 0)), (high_turned, low))
                    ):
                        points = jnp.where(row < 4, top, bottom)
                        features = jnp.concatenate([points, jnp.where(row < 3, top, ones)], axis=0)
                        second_ref[group * sweeps + 2 * pair + odd] = features.astype(jnp.bfloat16)
    listed_base = sizes.plane * sweeps
    chosen = lax.broadcasted_iota(jnp.int32, (structures, 128), 0) == family
    for k in range(listed_ref.shape[1] // 128):
        line = jnp.where(chosen, listed_ref[:, k * 128 : (k + 1) * 128], 0)
        counts_ref[listed_base + k : listed_base + k + 1] = jnp.sum(line, axis=0, keepdims=True).astype(
            jnp.float32
        )
    chunks = (list_ref.shape[0] - 8) // 2

    total_ref[...] = jnp.zeros_like(total_ref)
    spare = 1.0 / (1.0 + jnp.exp(jnp.float32(-CONTACT_SHIFT)))

    here = lax.rem(row_here, sizes.share) * sizes.n_col + column_here
    groups = sizes.groups

    def step(ending, beginning):
        sums = sums_ref[pl.ds(0, UNIT, stride=8), :]
        for k in range(1, 8):
            sums = sums + sums_ref[pl.ds(k, UNIT, stride=8), :]
        chance = 64.0 * 128.0 + 0.5 * jnp.sum(sums, axis=1, keepdims=True)
        count = jnp.sum(picks_ref[...], axis=1, keepdims=True)
        state = state_ref[...]
        chance = jnp.where(state == 1.0, 0.5 * (chance - 128.0 * spare), chance)
        weight = jnp.where(state == 2.0, 0.0, 1.0 - count / (BACKGROUND + chance / 128.0))
        for t in range(0, UNIT, 2):
            left, right = (second_ref[ending[t + i] & 4095] for i in range(2))
            blank = jnp.zeros_like(left)
            both = jnp.concatenate(
                [jnp.concatenate([left, blank], axis=1), jnp.concatenate([blank, right], axis=1)], axis=0
            )
            product = lax.dot_general(
                held_ref[t // 2], both, (((1,), (1,)), ((), ())), preferred_element_type=jnp.float32
            )
            scale = jnp.where(
                narrow < POINT_ROWS,
                weight[t : t + 1, : 2 * POINT_ROWS],
                weight[t + 1 : t + 2, : 2 * POINT_ROWS],
            )
            total_ref[ending[t] >> 19] += scale * product
        for t in range(0, UNIT, 2):
            seconds = [beginning[t + i][0] & 4095 for i in range(2)]
            logit = jnp.dot(
                first_ref[(beginning[t][0] >> 12) & 127],
                jnp.concatenate(
                    [jnp.concatenate([second_ref[at], marks_ref[at]], axis=0) for at in seconds], axis=1
                ),
                preferred_element_type=jnp.float32,
            )
            bend = jnp.tanh(logit)
            held_ref[t // 2] = (1.0 - bend * bend).astype(jnp.bfloat16)
            for i in range(2):
                part = bend[:, i * 128 : (i + 1) * 128]
                sums_ref[(t + i) * 8 : (t + i + 1) * 8] = jnp.sum(part.reshape(16, 8, 128), axis=0)
                code, place, state = beginning[t + i]
                picked = counts_ref[pl.ds(place >> 7, 1), :]
                picks_ref[t + i : t + i + 1] = jnp.where(lane == (place & 127), picked, 0.0)
                state_ref[t + i : t + i + 1] = jnp.full((1, 128), state)
        return tuple(code for code, _, _ in beginning)

    def band_step(turn, carry):
        slot, other, ending = carry
        beginning = []
        for _ in range(UNIT // 2):
            block = modulo(slot, sweeps) * groups + divide(slot, sweeps) * sizes.plane + here
            high = list_ref[2 * chunks + 2, slot]
            for i in range(2):
                second = jnp.minimum(other + i, high)
                first = jnp.minimum(block, second)
                group = modulo(first, groups)
                line = modulo(group, sizes.plane) * sweeps + divide(first, groups)
                apart = jnp.abs(block - second)
                place = line * 128 + divide(group, sizes.plane) * sizes.width + apart
                live = (other + i <= high) & (slot < slots)
                code = sizes.at(second) + (jnp.minimum(slot, slots - 1) << 12) + (slot << 19)
                state = jnp.where(live, (apart == 0).astype(jnp.float32), 2.0)
                beginning.append((code, place, state))
            over = other + 2 > high
            slot = jnp.minimum(slot + over.astype(jnp.int32), slots)
            other = jnp.where(over, list_ref[2 * chunks + 1, slot], other + 2)
        return slot, other, step(ending, beginning)

    def listed_step(turn, ending):
        beginning = []
        for t in range(UNIT):
            at = turn * UNIT + t
            code = list_ref[at >> 7, at & 127]
            state = jnp.where(code >> 19 < slots, 0.0, 2.0)
            beginning.append((code, list_ref[chunks + (at >> 7), at & 127], state))
        return step(ending, beginning)

    idle = (jnp.int32(slots << 19),) * UNIT
    sums_ref[...] = jnp.zeros_like(sums_ref)
    carry = (jnp.int32(0), list_ref[2 * chunks + 1, 0], idle)
    ending = lax.fori_loop(0, list_ref[2 * chunks + 3, 0], band_step, carry)[2]
    listed_steps = lax.div(list_ref[2 * chunks, 0] + UNIT - 1, UNIT)
    lax.fori_loop(0, listed_steps + 1, listed_step, ending)

    def collect(slot, carry):
        turned = jnp.transpose(total_ref[slot])
        gain_ref[pl.ds(pl.multiple_of(slot * POINT_ROWS, POINT_ROWS), POINT_ROWS), :] = (
            turned[:POINT_ROWS] + turned[POINT_ROWS:]
        )
        return carry

    lax.fori_loop(0, slots, collect, 0, unroll=4)
    scale = -2.0 * CONTACT_SLOPE / 128.0 / 4.0
    for k in range(structures):
        origin = lax.rem(family + k, structures)
        turn = (structures - k) % structures
        first = origin * sweeps * POINT_ROWS
        mass = gain_ref[pl.ds(first + 11, sweeps, stride=POINT_ROWS), :]
        for place in range(3):
            point = same_ref[pl.ds(turn * sweeps * 4 + place, sweeps, stride=4), :]
            high = rounded(point)
            near = high + rounded(point - high)
            pull = (
                gain_ref[pl.ds(first + place, sweeps, stride=POINT_ROWS), :]
                + gain_ref[pl.ds(first + place + 4, sweeps, stride=POINT_ROWS), :]
            )
            out_refs[k][place] = scale * (near * mass - pull)


def place_kernel(sizes, *refs):
    family = lax.div(lax.axis_index("row"), sizes.share)
    for k, ref in enumerate(refs[:-1]):
        refs[-1][lax.rem(family + (sizes.structures - k), sizes.structures)] = ref[...]


def on_device(n_row, n_col, coords, chrom_lengths, band_counts, inter_pairs, inter_counts):
    structures, _, sweeps, block_size = coords.shape
    width = band_counts.shape[3]
    listed = inter_pairs.shape[1]
    sizes = Sizes(n_row, n_col, structures, sweeps, width)
    share, slots, blocks = sizes.share, sizes.slots, sizes.blocks

    messages = pl.pallas_call(
        functools.partial(pack_kernel, sizes),
        out_shape=[jax.ShapeDtypeStruct((5 * sweeps, block_size), jnp.float32)] * structures,
        in_specs=[VMEM, VMEM],
        out_specs=[VMEM] * structures,
        compiler_params=SMALL,
        name="pack",
    )(coords, band_counts)
    deal = [
        [(i, (i // share + k) % structures * share + i % share) for i in range(n_row)]
        for k in range(structures)
    ]
    received = [messages[0]]
    for k in range(1, structures):
        received.append(lax.ppermute(messages[k], "row", deal[k]))
    chunks = -(-(2 * listed + slots + 2 * UNIT) // block_size)
    labels = -(-chrom_lengths.shape[0] // 16) * 16
    tiles, edges = pl.pallas_call(
        functools.partial(list_kernel, sizes),
        out_shape=[
            jax.ShapeDtypeStruct((2 * chunks + 8, block_size), jnp.int32),
            jax.ShapeDtypeStruct((2, labels, block_size), jnp.int32),
        ],
        in_specs=[SMEM, VMEM],
        out_specs=[VMEM] * 2,
        scratch_shapes=[pltpu.VMEM((2 * listed // block_size, POINT_ROWS, block_size), jnp.bfloat16)],
        compiler_params=SMALL,
        name="list_tiles",
    )(chrom_lengths, jnp.transpose(inter_pairs, (0, 2, 1)))

    own_row = pl.pallas_call(
        functools.partial(merge_kernel, 4 * sweeps),
        out_shape=jax.ShapeDtypeStruct((sizes.rows, block_size), jnp.float32),
        in_specs=[ANY] + [VMEM] * structures,
        out_specs=VMEM,
        compiler_params=SMALL,
        name="merge",
    )(tiles, *received)

    def device(family, chip, core):
        row = family * share + chip // sizes.half
        return row * n_col + chip % sizes.half * 2 + core

    pieces = [own_row]
    for k in range(1, sizes.chips):
        moves = [
            (device(f, i, core), device(f, (i + k) % sizes.chips, core))
            for f in range(structures)
            for i in range(sizes.chips)
            for core in range(2)
        ]
        pieces.append(lax.ppermute(own_row, AXES, moves))
    depth = POINT_ROWS + labels
    own, marks = pl.pallas_call(
        functools.partial(own_kernel, sizes),
        out_shape=[
            jax.ShapeDtypeStruct((2 * slots, block_size, depth), jnp.bfloat16),
            jax.ShapeDtypeStruct((blocks, labels, block_size), jnp.bfloat16),
        ],
        in_specs=[VMEM, VMEM],
        out_specs=[VMEM] * 2,
        compiler_params=pltpu.CompilerParams(vmem_limit_bytes=24 * 1024 * 1024),
        name="own_features",
    )(edges, own_row)

    same = pl.pallas_call(
        join_kernel,
        out_shape=jax.ShapeDtypeStruct((sizes.chips * sizes.rows, block_size), jnp.float32),
        in_specs=[ANY] + [VMEM] * sizes.chips,
        out_specs=VMEM,
        compiler_params=SMALL,
        name="join",
    )(marks, *pieces)
    across = lax.ppermute(same, "col", [(i, i ^ 1) for i in range(n_col)])

    gains = pl.pallas_call(
        functools.partial(tile_kernel, sizes),
        out_shape=[jax.ShapeDtypeStruct((3, sweeps, block_size), jnp.float32)] * structures,
        in_specs=[SMEM] + [VMEM] * 5,
        out_specs=[VMEM] * structures,
        scratch_shapes=[
            pltpu.VMEM((blocks, POINT_ROWS, block_size), jnp.bfloat16),
            pltpu.VMEM((sizes.plane * sweeps + listed // block_size, block_size), jnp.float32),
            pltpu.VMEM((UNIT // 2, block_size, 2 * block_size), jnp.bfloat16),
            pltpu.VMEM((UNIT * 8, block_size), jnp.float32),
            pltpu.VMEM((UNIT, block_size), jnp.float32),
            pltpu.VMEM((UNIT, block_size), jnp.float32),
            pltpu.VMEM((slots + 1, block_size, 2 * POINT_ROWS), jnp.float32),
            pltpu.VMEM((slots * POINT_ROWS, block_size), jnp.float32),
        ],
        compiler_params=pltpu.CompilerParams(vmem_limit_bytes=40 * 1024 * 1024),
        name="tiles",
    )(tiles, inter_counts, own, marks, same, across)

    arrived = [gains[0]]
    for k in range(1, structures):
        arrived.append(lax.ppermute(gains[k], "row", deal[k]))
    return pl.pallas_call(
        functools.partial(place_kernel, sizes),
        out_shape=jax.ShapeDtypeStruct(coords.shape, jnp.float32),
        in_specs=[VMEM] * structures,
        out_specs=VMEM,
        compiler_params=SMALL,
        name="place",
    )(*arrived)


def solution(mesh):
    placed = (
        P(None, None, None, ("row", "col")),
        P(),
        P(None, None, ("row", "col"), None),
        P(),
        P(),
    )
    return jax.shard_map(
        functools.partial(on_device, mesh.shape["row"], mesh.shape["col"]),
        mesh=mesh,
        in_specs=placed,
        out_specs=P(None, None, None, ("row", "col")),
        check_vma=False,
    )
```

```python
import functools

import jax
import jax.numpy as jnp
from jax import lax
from jax.experimental import pallas as pl
from jax.experimental.pallas import tpu as pltpu
from jax.sharding import PartitionSpec as P

CONTACT_SHIFT = 3.0
CONTACT_SLOPE = 0.5
BACKGROUND = 0.5
FAR = 32.0
UNIT = 32
POINT_ROWS = 16
AXES = ("row", "col")
VMEM = pl.BlockSpec(memory_space=pltpu.VMEM)
SMEM = pl.BlockSpec(memory_space=pltpu.SMEM)
ANY = pl.BlockSpec(memory_space=pl.ANY)
SMALL = pltpu.CompilerParams(vmem_limit_bytes=8 * 1024 * 1024)


def rounded(value):
    return value.astype(jnp.bfloat16).astype(jnp.float32)


def divide(value, by):
    return value >> (by.bit_length() - 1) if by & (by - 1) == 0 else lax.div(value, by)


def modulo(value, by):
    return value & (by - 1) if by & (by - 1) == 0 else lax.rem(value, by)


class Sizes:
    def __init__(self, n_row, n_col, structures, sweeps, width, listed):
        self.n_row, self.n_col, self.structures, self.sweeps = n_row, n_col, structures, sweeps
        self.width = width
        self.share = n_row // structures
        self.plane = self.share * n_col
        self.chips = self.plane // 2
        self.half = n_col // 2
        self.groups = n_row * n_col
        self.blocks = self.groups * sweeps
        self.slots = structures * sweeps
        self.chunks = (2 * listed + self.slots + 2 * UNIT) // 128 + 1
        self.band_chunks = (self.slots * width + UNIT) // 128 + 1
        self.rows = self.slots * 4 + sweeps


def pack_kernel(sizes, coords_ref, counts_ref, *out_refs):
    sweeps, width = sizes.sweeps, sizes.width
    family = lax.div(lax.axis_index("row"), sizes.share)
    lane = lax.broadcasted_iota(jnp.int32, (width, 128), 1)
    place = lax.broadcasted_iota(jnp.int32, (width, 128), 0) + family * width
    spread = (lane == place).astype(jnp.float32)
    for k, out_ref in enumerate(out_refs):
        member = lax.rem(family + k, sizes.structures)
        norm = jnp.zeros((sweeps, 128), jnp.float32)
        for place in range(3):
            point = coords_ref[member, place]
            out_ref[pl.ds(place, sweeps, stride=4), :] = point
            high = rounded(point)
            near = high + rounded(point - high)
            norm = norm - 0.5 * CONTACT_SLOPE * near * near
        out_ref[pl.ds(3, sweeps, stride=4), :] = norm
        counts = counts_ref[member][:, 0, :].astype(jnp.float32)
        out_ref[4 * sweeps : 5 * sweeps] = jnp.dot(counts, spread, preferred_element_type=jnp.float32)


def merge_kernel(points, after_ref, *refs):
    counts = refs[0][points:]
    for k, ref in enumerate(refs[:-1]):
        refs[-1][k * points : (k + 1) * points] = ref[:points]
        counts = counts + ref[points:] if k else counts
    refs[-1][(len(refs) - 1) * points :] = counts


def join_kernel(after_ref, *refs):
    rows = refs[0].shape[0]
    for k, ref in enumerate(refs[:-1]):
        refs[-1][k * rows : (k + 1) * rows] = ref[...]


def list_kernel(sizes, lengths_ref, pairs_ref, list_ref, edges_ref, digits_ref):
    slots, sweeps, groups = sizes.slots, sizes.sweeps, sizes.groups
    family = lax.div(lax.axis_index("row"), sizes.share)
    here = lax.rem(lax.axis_index("row"), sizes.share) * sizes.n_col + lax.axis_index("col")
    lane = lax.broadcasted_iota(jnp.int32, (1, 128), 1)

    slot_row = lax.broadcasted_iota(jnp.int32, (slots, 128), 0)
    block = modulo(slot_row, sweeps) * groups + divide(slot_row, sweeps) * sizes.plane + here
    first_bead = block * 128
    low = jnp.zeros((slots, 128), jnp.int32)
    high = jnp.full((slots, 128), sizes.blocks * 128)
    edges_ref[...] = jnp.zeros_like(edges_ref)
    end = jnp.int32(0)
    for k in range(lengths_ref.shape[0]):
        start = end
        end = end + lengths_ref[k]
        edges_ref[0, k : k + 1] = jnp.full((1, 128), start)
        edges_ref[1, k : k + 1] = jnp.full((1, 128), end)
        low = jnp.maximum(low, jnp.where(start <= first_bead, start, 0))
        high = jnp.minimum(high, jnp.where(end > first_bead + 127, end, sizes.blocks * 128))
    low = jnp.maximum(low >> 7, block - (sizes.width - 1))
    high = jnp.minimum(jnp.minimum((high - 1) >> 7, block + (sizes.width - 1)), sizes.blocks - 1)
    in_band = (high - low + 2) >> 1
    lower = (
        lax.broadcasted_iota(jnp.int32, (slots, slots), 0) > lax.broadcasted_iota(jnp.int32, (slots, slots), 1)
    ).astype(jnp.float32)

    def below(value):
        return jnp.dot(lower, value, precision=lax.Precision.HIGHEST, preferred_element_type=jnp.float32)

    begin = below(in_band.astype(jnp.float32)).astype(jnp.int32)
    band_total = jnp.max(begin + in_band)
    chunks, band_chunks = sizes.chunks, sizes.band_chunks

    def band(chunk, carry):
        pair = chunk * 128 + lane
        inside = (begin <= pair) & (pair < begin + in_band)

        def pick(value):
            return jnp.sum(jnp.where(inside, value, 0), axis=0, keepdims=True)

        live = pick(1) > 0
        slot = pick(slot_row)
        near = pick(low - 2 * begin) + 2 * pair
        last = pick(high)
        here_block = pick(block)
        for i in range(2):
            second = jnp.where(live, jnp.minimum(near + i, last), 0)
            first = jnp.minimum(here_block, second)
            group = modulo(first, groups)
            line = modulo(group, sizes.plane) * sweeps + divide(first, groups)
            apart = jnp.abs(here_block - second)
            place = line * 128 + divide(group, sizes.plane) * sizes.width + apart
            state = jnp.where(live & (near + i <= last), jnp.where(apart == 0, 1, 0), 2)
            code = second + (slot << 12) + (jnp.where(live, slot, slots) << 19) + (state << 26)
            at = 2 * chunks + 2 * i * band_chunks + chunk
            list_ref[pl.ds(at, 1), :] = code
            list_ref[pl.ds(at + band_chunks, 1), :] = jnp.where(live, place, 0)
        return carry

    lax.fori_loop(0, lax.div(band_total + UNIT, 128) + 1, band, 0)
    steps = lax.div(band_total + (UNIT // 2 - 1), UNIT // 2)

    half = pairs_ref.shape[2] // 128
    lines = 2 * half
    pairs = pairs_ref[family]
    group = modulo(pairs, groups)
    mine = modulo(group, sizes.plane) == here
    slot = jnp.where(mine, divide(group, sizes.plane) * sweeps + divide(pairs, groups), -1)
    other = pairs

    def cut(value, line):
        side, at = line // half, line % half * 128
        return value[side : side + 1, at : at + 128]

    before = lax.broadcasted_iota(jnp.int32, (128, 256), 0)
    after = lax.broadcasted_iota(jnp.int32, (128, 256), 1)
    count = (before <= after).astype(jnp.float32).astype(jnp.bfloat16)
    running = jnp.zeros((slots, 128), jnp.float32)
    picked = []
    for line in range(lines):
        chosen = (cut(slot, line) == slot_row).astype(jnp.float32)
        counted = jnp.dot(chosen.astype(jnp.bfloat16), count, preferred_element_type=jnp.float32)
        inner = jnp.sum(chosen * (counted[:, :128] - 1.0 + running), axis=0, keepdims=True)
        picked.append((chosen, inner))
        running = running + counted[:, 128:]
    doubled = 2.0 * jnp.floor(0.5 * (running + 1.0))
    base = below(doubled)
    number = jnp.max(base + doubled).astype(jnp.int32)
    digit_row = lax.broadcasted_iota(jnp.int32, (POINT_ROWS, 128), 0)
    ranks = []
    for line in range(lines):
        chosen, inner = picked[line]
        rank = inner + jnp.sum(chosen * base, axis=0, keepdims=True)
        ranks.append(jnp.where(cut(slot, line) >= 0, rank.astype(jnp.int32), -1))
        opposite = (line + half) % lines
        partner = cut(other, opposite)
        digits = jnp.zeros((POINT_ROWS, 128), jnp.int32)
        for place, digit in enumerate(
            (partner & 31, partner >> 5, cut(slot, line), lane, line % half + 0 * lane, 1 + 0 * lane)
        ):
            digits = jnp.where(digit_row == place, digit, digits)
        digits_ref[line] = digits.astype(jnp.float32).astype(jnp.bfloat16)
    spot = lax.broadcasted_iota(jnp.int32, (128, 128), 0)

    def compact(chunk, carry):
        found = jnp.zeros((POINT_ROWS, 128), jnp.float32)
        for line in range(0, lines, 2):
            there = jnp.concatenate(
                [(ranks[line + i] == spot + chunk * 128).astype(jnp.float32).astype(jnp.bfloat16) for i in range(2)],
                axis=1,
            )
            found = found + lax.dot_general(
                jnp.concatenate([digits_ref[line], digits_ref[line + 1]], axis=1),
                there,
                (((1,), (1,)), ((), ())),
                preferred_element_type=jnp.float32,
            )
        found = found.astype(jnp.int32)
        at = found[2:3]
        code = found[0:1] + (found[1:2] << 5) + ((slots + at) << 12) + (at << 19)
        list_ref[pl.ds(chunk, 1), :] = jnp.where(found[5:6] > 0, code, (slots << 19) + (2 << 26))
        list_ref[pl.ds(chunks + chunk, 1), :] = (
            sizes.plane * sweeps * 128 + found[3:4] + found[4:5] * 128
        )
        return carry

    lax.fori_loop(0, lax.div(number + 2 * UNIT - 1, 128) + 1, compact, 0)
    end = 2 * chunks + 4 * band_chunks
    list_ref[end : end + 1] = jnp.full((1, 128), number)
    list_ref[end + 1 : end + 2] = jnp.full((1, 128), steps)


def own_kernel(sizes, edges_ref, own_ref, first_ref, marks_ref):
    slots, sweeps, groups = sizes.slots, sizes.sweeps, sizes.groups
    family = lax.div(lax.axis_index("row"), sizes.share)
    here = lax.rem(lax.axis_index("row"), sizes.share) * sizes.n_col + lax.axis_index("col")
    lane = lax.broadcasted_iota(jnp.int32, (1, 128), 1)
    row = lax.broadcasted_iota(jnp.int32, (8, 128), 0)
    labels = edges_ref.shape[1]
    depth = POINT_ROWS + labels

    def mark(group, carry):
        for u in range(sweeps):
            bead = (u * groups + group) * 128 + lane
            inside = (bead >= edges_ref[0]) & (bead < edges_ref[1])
            marks_ref[u * groups + group] = inside.astype(jnp.float32).astype(jnp.bfloat16)
        return carry

    lax.fori_loop(0, groups, mark, 0)

    def fill(turn, carry):
        origin = lax.rem(family + (sizes.structures - turn), sizes.structures)
        for pair in range(sweeps // 2):
            value = own_ref[pl.ds(pl.multiple_of(turn * sweeps * 4 + pair * 8, 8), 8), :]
            for odd in range(2):
                value = pltpu.roll(value, 4, 0) if odd else value
                high = rounded(value)
                low = rounded(value - high)
                shifted = value + 0.5 * CONTACT_SHIFT
                shifted_high = rounded(shifted)
                shifted_low = rounded(shifted - shifted_high)
                both = jnp.where(row < 4, high, pltpu.roll(high, 4, 0))
                near = jnp.where((row & 3) == 3, 1.0, CONTACT_SLOPE * both)
                rest = jnp.where(row == 4, pltpu.roll(shifted_low, 1, 0), 0.0)
                rest = jnp.where(row == 3, shifted_high, rest)
                rest = jnp.where(row < 3, CONTACT_SLOPE * low, rest)
                u = 2 * pair + odd
                bead = (u * groups + origin * sizes.plane + here) * 128 + lane
                inside = (bead >= edges_ref[0]) & (bead < edges_ref[1])
                apart = jnp.where(inside, 0.0, -FAR)
                blank = jnp.zeros((128 - depth, 128), jnp.float32)
                turned = jnp.transpose(jnp.concatenate([near, rest, apart, blank], axis=0))
                slot = origin * sweeps + u
                first_ref[slot] = turned[:, :depth].astype(jnp.bfloat16)
                other = jnp.where(lane < POINT_ROWS, turned, -FAR - turned)
                first_ref[slots + slot] = other[:, :depth].astype(jnp.bfloat16)
        return carry

    lax.fori_loop(0, sizes.structures, fill, 0)


def tile_kernel(sizes, list_ref, listed_ref, first_ref, marks_ref, same_ref, across_ref, *refs):
    structures, sweeps, slots, groups = sizes.structures, sizes.sweeps, sizes.slots, sizes.groups
    out_refs = refs[:structures]
    second_ref, counts_ref, held_ref, sums_ref, picks_ref, state_ref, total_ref, gain_ref = refs[structures:]
    row_here = lax.axis_index("row")
    column_here = lax.axis_index("col")
    family = lax.div(row_here, sizes.share)
    chip_here = lax.rem(row_here, sizes.share) * sizes.half + lax.div(column_here, 2)
    core_here = lax.rem(column_here, 2)
    lane = lax.broadcasted_iota(jnp.int32, (1, 128), 1)
    row = lax.broadcasted_iota(jnp.int32, (8, 128), 0)
    ones = jnp.where((row == 3) | (row == 4), 1.0, 0.0)
    narrow = lax.broadcasted_iota(jnp.int32, (1, 2 * POINT_ROWS), 1)

    for core, piece_ref in ((core_here, same_ref), (1 - core_here, across_ref)):
        for k in range(sizes.chips):
            chip = lax.rem(chip_here + (sizes.chips - k), sizes.chips)
            device = chip * 2 + core
            base = k * sizes.rows
            counts_ref[pl.ds(pl.multiple_of(device * sweeps, sweeps), sweeps), :] = piece_ref[
                base + slots * 4 : base + slots * 4 + sweeps
            ]
            for turn in range(structures):
                origin = lax.rem(family + (structures - turn), structures)
                group = origin * sizes.plane + device
                for pair in range(sweeps // 2):
                    start = base + turn * sweeps * 4 + pair * 8
                    value = piece_ref[start : start + 8]
                    high = rounded(value)
                    low = value - high
                    high_turned = pltpu.roll(high, 4, 0)
                    for odd, (top, bottom) in enumerate(
                        ((high, pltpu.roll(low, 4, 0)), (high_turned, low))
                    ):
                        points = jnp.where(row < 4, top, bottom)
                        features = jnp.concatenate([points, jnp.where(row < 3, top, ones)], axis=0)
                        second_ref[(2 * pair + odd) * groups + group] = features.astype(jnp.bfloat16)
    listed_base = sizes.plane * sweeps
    chosen = lax.broadcasted_iota(jnp.int32, (structures, 128), 0) == family
    for k in range(listed_ref.shape[1] // 128):
        line = jnp.where(chosen, listed_ref[:, k * 128 : (k + 1) * 128], 0)
        counts_ref[listed_base + k : listed_base + k + 1] = jnp.sum(line, axis=0, keepdims=True).astype(
            jnp.float32
        )
    chunks, band_chunks = sizes.chunks, sizes.band_chunks
    end = 2 * chunks + 4 * band_chunks

    total_ref[...] = jnp.zeros_like(total_ref)
    spare = 1.0 / (1.0 + jnp.exp(jnp.float32(-CONTACT_SHIFT)))

    def step(ending, beginning):
        sums = sums_ref[pl.ds(0, UNIT, stride=8), :]
        for k in range(1, 8):
            sums = sums + sums_ref[pl.ds(k, UNIT, stride=8), :]
        chance = 64.0 * 128.0 + 0.5 * jnp.sum(sums, axis=1, keepdims=True)
        count = jnp.sum(picks_ref[...], axis=1, keepdims=True)
        state = state_ref[...]
        chance = jnp.where(state == 1, 0.5 * (chance - 128.0 * spare), chance)
        weight = jnp.where(state == 2, 0.0, 1.0 - count / (BACKGROUND + chance / 128.0))
        for t in range(0, UNIT, 2):
            left, right = (second_ref[ending[t + i] & 4095] for i in range(2))
            blank = jnp.zeros_like(left)
            both = jnp.concatenate(
                [jnp.concatenate([left, blank], axis=1), jnp.concatenate([blank, right], axis=1)], axis=0
            )
            product = lax.dot_general(
                held_ref[t // 2], both, (((1,), (1,)), ((), ())), preferred_element_type=jnp.float32
            )
            scale = jnp.where(
                narrow < POINT_ROWS,
                weight[t : t + 1, : 2 * POINT_ROWS],
                weight[t + 1 : t + 2, : 2 * POINT_ROWS],
            )
            total_ref[(ending[t] >> 19) & 127] += scale * product
        for t in range(0, UNIT, 2):
            seconds = [beginning[t + i][0] & 4095 for i in range(2)]
            logit = jnp.dot(
                first_ref[(beginning[t][0] >> 12) & 127],
                jnp.concatenate(
                    [jnp.concatenate([second_ref[at], marks_ref[at]], axis=0) for at in seconds], axis=1
                ),
                preferred_element_type=jnp.float32,
            )
            bend = jnp.tanh(logit)
            held_ref[t // 2] = (1.0 - bend * bend).astype(jnp.bfloat16)
            for i in range(2):
                part = bend[:, i * 128 : (i + 1) * 128]
                sums_ref[(t + i) * 8 : (t + i + 1) * 8] = jnp.sum(part.reshape(16, 8, 128), axis=0)
                code, place = beginning[t + i]
                picked = counts_ref[pl.ds(place >> 7, 1), :]
                picks_ref[t + i : t + i + 1] = jnp.where(lane == (place & 127), picked, 0.0)
                state_ref[t + i : t + i + 1] = jnp.full((1, 128), code >> 26)
        return tuple(code for code, _ in beginning)

    def band_step(turn, ending):
        line = 2 * chunks + (turn * (UNIT // 2) >> 7)
        at = turn * (UNIT // 2) & 127
        beginning = []
        for t in range(UNIT):
            row = line + t % 2 * 2 * band_chunks
            beginning.append((list_ref[row, at + t // 2], list_ref[row + band_chunks, at + t // 2]))
        return step(ending, beginning)

    def listed_step(turn, ending):
        line = turn * UNIT >> 7
        at = turn * UNIT & 127
        beginning = [(list_ref[line, at + t], list_ref[chunks + line, at + t]) for t in range(UNIT)]
        return step(ending, beginning)

    idle = (jnp.int32(slots << 19),) * UNIT
    sums_ref[...] = jnp.zeros_like(sums_ref)
    ending = lax.fori_loop(0, list_ref[end + 1, 0], band_step, idle)
    listed_steps = lax.div(list_ref[end, 0] + UNIT - 1, UNIT)
    lax.fori_loop(0, listed_steps + 1, listed_step, ending)

    def collect(slot, carry):
        turned = jnp.transpose(total_ref[slot])
        gain_ref[pl.ds(pl.multiple_of(slot * POINT_ROWS, POINT_ROWS), POINT_ROWS), :] = (
            turned[:POINT_ROWS] + turned[POINT_ROWS:]
        )
        return carry

    lax.fori_loop(0, slots, collect, 0, unroll=4)
    scale = -2.0 * CONTACT_SLOPE / 128.0 / 4.0
    for k in range(structures):
        origin = lax.rem(family + k, structures)
        turn = (structures - k) % structures
        first = origin * sweeps * POINT_ROWS
        mass = gain_ref[pl.ds(first + 11, sweeps, stride=POINT_ROWS), :]
        for place in range(3):
            point = same_ref[pl.ds(turn * sweeps * 4 + place, sweeps, stride=4), :]
            high = rounded(point)
            near = high + rounded(point - high)
            pull = (
                gain_ref[pl.ds(first + place, sweeps, stride=POINT_ROWS), :]
                + gain_ref[pl.ds(first + place + 4, sweeps, stride=POINT_ROWS), :]
            )
            out_refs[k][place] = scale * (near * mass - pull)


def place_kernel(sizes, *refs):
    family = lax.div(lax.axis_index("row"), sizes.share)
    for k, ref in enumerate(refs[:-1]):
        refs[-1][lax.rem(family + (sizes.structures - k), sizes.structures)] = ref[...]


def on_device(n_row, n_col, coords, chrom_lengths, band_counts, inter_pairs, inter_counts):
    structures, _, sweeps, block_size = coords.shape
    width = band_counts.shape[3]
    listed = inter_pairs.shape[1]
    sizes = Sizes(n_row, n_col, structures, sweeps, width, listed)
    share, slots, blocks = sizes.share, sizes.slots, sizes.blocks

    messages = pl.pallas_call(
        functools.partial(pack_kernel, sizes),
        out_shape=[jax.ShapeDtypeStruct((5 * sweeps, block_size), jnp.float32)] * structures,
        in_specs=[VMEM, VMEM],
        out_specs=[VMEM] * structures,
        compiler_params=SMALL,
        name="pack",
    )(coords, band_counts)
    deal = [
        [(i, (i // share + k) % structures * share + i % share) for i in range(n_row)]
        for k in range(structures)
    ]
    received = [messages[0]]
    for k in range(1, structures):
        received.append(lax.ppermute(messages[k], "row", deal[k]))
    lines = 2 * sizes.chunks + 4 * sizes.band_chunks + 8
    labels = -(-chrom_lengths.shape[0] // 16) * 16
    tiles, edges = pl.pallas_call(
        functools.partial(list_kernel, sizes),
        out_shape=[
            jax.ShapeDtypeStruct((lines, block_size), jnp.int32),
            jax.ShapeDtypeStruct((2, labels, block_size), jnp.int32),
        ],
        in_specs=[SMEM, VMEM],
        out_specs=[VMEM] * 2,
        scratch_shapes=[pltpu.VMEM((2 * listed // block_size, POINT_ROWS, block_size), jnp.bfloat16)],
        compiler_params=SMALL,
        name="list_tiles",
    )(chrom_lengths, jnp.transpose(inter_pairs, (0, 2, 1)))

    own_row = pl.pallas_call(
        functools.partial(merge_kernel, 4 * sweeps),
        out_shape=jax.ShapeDtypeStruct((sizes.rows, block_size), jnp.float32),
        in_specs=[ANY] + [VMEM] * structures,
        out_specs=VMEM,
        compiler_params=SMALL,
        name="merge",
    )(tiles, *received)

    def device(family, chip, core):
        row = family * share + chip // sizes.half
        return row * n_col + chip % sizes.half * 2 + core

    pieces = [own_row]
    for k in range(1, sizes.chips):
        moves = [
            (device(f, i, core), device(f, (i + k) % sizes.chips, core))
            for f in range(structures)
            for i in range(sizes.chips)
            for core in range(2)
        ]
        pieces.append(lax.ppermute(own_row, AXES, moves))
    depth = POINT_ROWS + labels
    own, marks = pl.pallas_call(
        functools.partial(own_kernel, sizes),
        out_shape=[
            jax.ShapeDtypeStruct((2 * slots, block_size, depth), jnp.bfloat16),
            jax.ShapeDtypeStruct((blocks, labels, block_size), jnp.bfloat16),
        ],
        in_specs=[VMEM, VMEM],
        out_specs=[VMEM] * 2,
        compiler_params=pltpu.CompilerParams(vmem_limit_bytes=24 * 1024 * 1024),
        name="own_features",
    )(edges, own_row)

    same = pl.pallas_call(
        join_kernel,
        out_shape=jax.ShapeDtypeStruct((sizes.chips * sizes.rows, block_size), jnp.float32),
        in_specs=[ANY] + [VMEM] * sizes.chips,
        out_specs=VMEM,
        compiler_params=SMALL,
        name="join",
    )(marks, *pieces)
    across = lax.ppermute(same, "col", [(i, i ^ 1) for i in range(n_col)])

    gains = pl.pallas_call(
        functools.partial(tile_kernel, sizes),
        out_shape=[jax.ShapeDtypeStruct((3, sweeps, block_size), jnp.float32)] * structures,
        in_specs=[SMEM] + [VMEM] * 5,
        out_specs=[VMEM] * structures,
        scratch_shapes=[
            pltpu.VMEM((blocks, POINT_ROWS, block_size), jnp.bfloat16),
            pltpu.VMEM((sizes.plane * sweeps + listed // block_size, block_size), jnp.float32),
            pltpu.VMEM((UNIT // 2, block_size, 2 * block_size), jnp.bfloat16),
            pltpu.VMEM((UNIT * 8, block_size), jnp.float32),
            pltpu.VMEM((UNIT, block_size), jnp.float32),
            pltpu.VMEM((UNIT, block_size), jnp.int32),
            pltpu.VMEM((slots + 1, block_size, 2 * POINT_ROWS), jnp.float32),
            pltpu.VMEM((slots * POINT_ROWS, block_size), jnp.float32),
        ],
        compiler_params=pltpu.CompilerParams(vmem_limit_bytes=40 * 1024 * 1024),
        name="tiles",
    )(tiles, inter_counts, own, marks, same, across)

    arrived = [gains[0]]
    for k in range(1, structures):
        arrived.append(lax.ppermute(gains[k], "row", deal[k]))
    return pl.pallas_call(
        functools.partial(place_kernel, sizes),
        out_shape=jax.ShapeDtypeStruct(coords.shape, jnp.float32),
        in_specs=[VMEM] * structures,
        out_specs=VMEM,
        compiler_params=SMALL,
        name="place",
    )(*arrived)


def solution(mesh):
    placed = (
        P(None, None, None, ("row", "col")),
        P(),
        P(None, None, ("row", "col"), None),
        P(),
        P(),
    )
    return jax.shard_map(
        functools.partial(on_device, mesh.shape["row"], mesh.shape["col"]),
        mesh=mesh,
        in_specs=placed,
        out_specs=P(None, None, None, ("row", "col")),
        check_vma=False,
    )
```

```python
import functools

import jax
import jax.numpy as jnp
from jax import lax
from jax.experimental import pallas as pl
from jax.experimental.pallas import tpu as pltpu
from jax.sharding import PartitionSpec as P

CONTACT_SHIFT = 3.0
CONTACT_SLOPE = 0.5
BACKGROUND = 0.5
FAR = 32.0
UNIT = 32
POINT_ROWS = 16
AXES = ("row", "col")
VMEM = pl.BlockSpec(memory_space=pltpu.VMEM)
SMEM = pl.BlockSpec(memory_space=pltpu.SMEM)
ANY = pl.BlockSpec(memory_space=pl.ANY)
SMALL = pltpu.CompilerParams(vmem_limit_bytes=8 * 1024 * 1024)


def rounded(value):
    return value.astype(jnp.bfloat16).astype(jnp.float32)


def divide(value, by):
    return value >> (by.bit_length() - 1) if by & (by - 1) == 0 else lax.div(value, by)


def modulo(value, by):
    return value & (by - 1) if by & (by - 1) == 0 else lax.rem(value, by)


class Sizes:
    def __init__(self, n_row, n_col, structures, sweeps, width, listed):
        self.n_row, self.n_col, self.structures, self.sweeps = n_row, n_col, structures, sweeps
        self.width = width
        self.share = n_row // structures
        self.plane = self.share * n_col
        self.chips = self.plane // 2
        self.half = n_col // 2
        self.groups = n_row * n_col
        self.blocks = self.groups * sweeps
        self.slots = structures * sweeps
        self.chunks = (2 * listed + self.slots + 2 * UNIT) // 128 + 1
        self.band_chunks = (self.slots * width + UNIT) // 128 + 1
        self.rows = self.slots * 4 + sweeps


def pack_kernel(sizes, coords_ref, counts_ref, *out_refs):
    sweeps, width = sizes.sweeps, sizes.width
    family = lax.div(lax.axis_index("row"), sizes.share)
    lane = lax.broadcasted_iota(jnp.int32, (width, 128), 1)
    place = lax.broadcasted_iota(jnp.int32, (width, 128), 0) + family * width
    spread = (lane == place).astype(jnp.float32)
    for k, out_ref in enumerate(out_refs):
        member = lax.rem(family + k, sizes.structures)
        norm = jnp.zeros((sweeps, 128), jnp.float32)
        for place in range(3):
            point = coords_ref[member, place]
            out_ref[pl.ds(place, sweeps, stride=4), :] = point
            high = rounded(point)
            near = high + rounded(point - high)
            norm = norm - 0.5 * CONTACT_SLOPE * near * near
        out_ref[pl.ds(3, sweeps, stride=4), :] = norm
        counts = counts_ref[member][:, 0, :].astype(jnp.float32)
        out_ref[4 * sweeps : 5 * sweeps] = jnp.dot(counts, spread, preferred_element_type=jnp.float32)


def merge_kernel(points, after_ref, *refs):
    counts = refs[0][points:]
    for k, ref in enumerate(refs[:-1]):
        refs[-1][k * points : (k + 1) * points] = ref[:points]
        counts = counts + ref[points:] if k else counts
    refs[-1][(len(refs) - 1) * points :] = counts


def join_kernel(after_ref, *refs):
    rows = refs[0].shape[0]
    for k, ref in enumerate(refs[:-1]):
        refs[-1][k * rows : (k + 1) * rows] = ref[...]


def below(value):
    rows = value.shape[0]
    row = lax.broadcasted_iota(jnp.int32, (rows, rows), 0)
    lower = (row > lax.broadcasted_iota(jnp.int32, (rows, rows), 1)).astype(jnp.float32)
    return jnp.dot(lower, value, precision=lax.Precision.HIGHEST, preferred_element_type=jnp.float32)


def band_kernel(sizes, lengths_ref, list_ref, edges_ref):
    slots, sweeps, groups = sizes.slots, sizes.sweeps, sizes.groups
    family = lax.div(lax.axis_index("row"), sizes.share)
    here = lax.rem(lax.axis_index("row"), sizes.share) * sizes.n_col + lax.axis_index("col")
    lane = lax.broadcasted_iota(jnp.int32, (1, 128), 1)

    slot_row = lax.broadcasted_iota(jnp.int32, (slots, 128), 0)
    block = modulo(slot_row, sweeps) * groups + divide(slot_row, sweeps) * sizes.plane + here
    first_bead = block * 128
    low = jnp.zeros((slots, 128), jnp.int32)
    high = jnp.full((slots, 128), sizes.blocks * 128)
    edges_ref[...] = jnp.zeros_like(edges_ref)
    end = jnp.int32(0)
    for k in range(lengths_ref.shape[0]):
        start = end
        end = end + lengths_ref[k]
        edges_ref[0, k : k + 1] = jnp.full((1, 128), start)
        edges_ref[1, k : k + 1] = jnp.full((1, 128), end)
        low = jnp.maximum(low, jnp.where(start <= first_bead, start, 0))
        high = jnp.minimum(high, jnp.where(end > first_bead + 127, end, sizes.blocks * 128))
    low = jnp.maximum(low >> 7, block - (sizes.width - 1))
    high = jnp.minimum(jnp.minimum((high - 1) >> 7, block + (sizes.width - 1)), sizes.blocks - 1)
    in_band = (high - low + 2) >> 1
    begin = below(in_band.astype(jnp.float32)).astype(jnp.int32)
    band_total = jnp.max(begin + in_band)
    chunks = sizes.band_chunks

    def band(chunk, carry):
        pair = chunk * 128 + lane
        inside = (begin <= pair) & (pair < begin + in_band)

        def pick(value):
            return jnp.sum(jnp.where(inside, value, 0), axis=0, keepdims=True)

        live = pick(1) > 0
        slot = pick(slot_row)
        near = pick(low - 2 * begin) + 2 * pair
        last = pick(high)
        here_block = pick(block)
        for i in range(2):
            second = jnp.where(live, jnp.minimum(near + i, last), 0)
            first = jnp.minimum(here_block, second)
            group = modulo(first, groups)
            line = modulo(group, sizes.plane) * sweeps + divide(first, groups)
            apart = jnp.abs(here_block - second)
            place = line * 128 + divide(group, sizes.plane) * sizes.width + apart
            state = jnp.where(live & (near + i <= last), jnp.where(apart == 0, 1, 0), 2)
            code = second + (slot << 12) + (jnp.where(live, slot, slots) << 19) + (state << 26)
            at = 2 * i * chunks + chunk
            list_ref[pl.ds(at, 1), :] = code
            list_ref[pl.ds(at + chunks, 1), :] = jnp.where(live, place, 0)
        return carry

    lax.fori_loop(0, lax.div(band_total + UNIT, 128) + 1, band, 0)
    steps = lax.div(band_total + (UNIT // 2 - 1), UNIT // 2)
    list_ref[4 * chunks : 4 * chunks + 1] = jnp.full((1, 128), steps)


def list_kernel(sizes, pairs_ref, after_ref, list_ref, digits_ref):
    slots, sweeps, groups, chunks = sizes.slots, sizes.sweeps, sizes.groups, sizes.chunks
    family = lax.div(lax.axis_index("row"), sizes.share)
    here = lax.rem(lax.axis_index("row"), sizes.share) * sizes.n_col + lax.axis_index("col")
    lane = lax.broadcasted_iota(jnp.int32, (1, 128), 1)
    slot_row = lax.broadcasted_iota(jnp.int32, (slots, 128), 0)

    half = pairs_ref.shape[2] // 128
    lines = 2 * half
    pairs = pairs_ref[family]
    group = modulo(pairs, groups)
    mine = modulo(group, sizes.plane) == here
    slot = jnp.where(mine, divide(group, sizes.plane) * sweeps + divide(pairs, groups), -1)
    other = pairs

    def cut(value, line):
        side, at = line // half, line % half * 128
        return value[side : side + 1, at : at + 128]

    before = lax.broadcasted_iota(jnp.int32, (128, 256), 0)
    after = lax.broadcasted_iota(jnp.int32, (128, 256), 1)
    count = (before <= after).astype(jnp.float32).astype(jnp.bfloat16)
    running = jnp.zeros((slots, 128), jnp.float32)
    picked = []
    for line in range(lines):
        chosen = (cut(slot, line) == slot_row).astype(jnp.float32)
        counted = jnp.dot(chosen.astype(jnp.bfloat16), count, preferred_element_type=jnp.float32)
        inner = jnp.sum(chosen * (counted[:, :128] - 1.0 + running), axis=0, keepdims=True)
        picked.append((chosen, inner))
        running = running + counted[:, 128:]
    doubled = 2.0 * jnp.floor(0.5 * (running + 1.0))
    base = below(doubled)
    number = jnp.max(base + doubled).astype(jnp.int32)
    digit_row = lax.broadcasted_iota(jnp.int32, (POINT_ROWS, 128), 0)
    ranks = []
    for line in range(lines):
        chosen, inner = picked[line]
        rank = inner + jnp.sum(chosen * base, axis=0, keepdims=True)
        ranks.append(jnp.where(cut(slot, line) >= 0, rank.astype(jnp.int32), -1))
        opposite = (line + half) % lines
        partner = cut(other, opposite)
        digits = jnp.zeros((POINT_ROWS, 128), jnp.int32)
        for place, digit in enumerate(
            (partner & 31, partner >> 5, cut(slot, line), lane, line % half + 0 * lane, 1 + 0 * lane)
        ):
            digits = jnp.where(digit_row == place, digit, digits)
        digits_ref[line] = digits.astype(jnp.float32).astype(jnp.bfloat16)
    spot = lax.broadcasted_iota(jnp.int32, (128, 128), 0)

    def compact(chunk, carry):
        found = jnp.zeros((POINT_ROWS, 128), jnp.float32)
        for line in range(0, lines, 2):
            there = jnp.concatenate(
                [(ranks[line + i] == spot + chunk * 128).astype(jnp.float32).astype(jnp.bfloat16) for i in range(2)],
                axis=1,
            )
            found = found + lax.dot_general(
                jnp.concatenate([digits_ref[line], digits_ref[line + 1]], axis=1),
                there,
                (((1,), (1,)), ((), ())),
                preferred_element_type=jnp.float32,
            )
        found = found.astype(jnp.int32)
        at = found[2:3]
        code = found[0:1] + (found[1:2] << 5) + ((slots + at) << 12) + (at << 19)
        list_ref[pl.ds(chunk, 1), :] = jnp.where(found[5:6] > 0, code, (slots << 19) + (2 << 26))
        list_ref[pl.ds(chunks + chunk, 1), :] = (
            sizes.plane * sweeps * 128 + found[3:4] + found[4:5] * 128
        )
        return carry

    lax.fori_loop(0, lax.div(number + 2 * UNIT - 1, 128) + 1, compact, 0)
    list_ref[2 * chunks : 2 * chunks + 1] = jnp.full((1, 128), number)


def own_kernel(sizes, edges_ref, own_ref, first_ref, marks_ref):
    slots, sweeps, groups = sizes.slots, sizes.sweeps, sizes.groups
    family = lax.div(lax.axis_index("row"), sizes.share)
    here = lax.rem(lax.axis_index("row"), sizes.share) * sizes.n_col + lax.axis_index("col")
    lane = lax.broadcasted_iota(jnp.int32, (1, 128), 1)
    row = lax.broadcasted_iota(jnp.int32, (8, 128), 0)
    labels = edges_ref.shape[1]
    depth = POINT_ROWS + labels

    def mark(group, carry):
        for u in range(sweeps):
            bead = (u * groups + group) * 128 + lane
            inside = (bead >= edges_ref[0]) & (bead < edges_ref[1])
            marks_ref[u * groups + group] = inside.astype(jnp.float32).astype(jnp.bfloat16)
        return carry

    lax.fori_loop(0, groups, mark, 0)

    def fill(turn, carry):
        origin = lax.rem(family + (sizes.structures - turn), sizes.structures)
        for pair in range(sweeps // 2):
            value = own_ref[pl.ds(pl.multiple_of(turn * sweeps * 4 + pair * 8, 8), 8), :]
            for odd in range(2):
                value = pltpu.roll(value, 4, 0) if odd else value
                high = rounded(value)
                low = rounded(value - high)
                shifted = value + 0.5 * CONTACT_SHIFT
                shifted_high = rounded(shifted)
                shifted_low = rounded(shifted - shifted_high)
                both = jnp.where(row < 4, high, pltpu.roll(high, 4, 0))
                near = jnp.where((row & 3) == 3, 1.0, CONTACT_SLOPE * both)
                rest = jnp.where(row == 4, pltpu.roll(shifted_low, 1, 0), 0.0)
                rest = jnp.where(row == 3, shifted_high, rest)
                rest = jnp.where(row < 3, CONTACT_SLOPE * low, rest)
                u = 2 * pair + odd
                bead = (u * groups + origin * sizes.plane + here) * 128 + lane
                inside = (bead >= edges_ref[0]) & (bead < edges_ref[1])
                apart = jnp.where(inside, 0.0, -FAR)
                blank = jnp.zeros((128 - depth, 128), jnp.float32)
                turned = jnp.transpose(jnp.concatenate([near, rest, apart, blank], axis=0))
                slot = origin * sweeps + u
                first_ref[slot] = turned[:, :depth].astype(jnp.bfloat16)
                other = jnp.where(lane < POINT_ROWS, turned, -FAR - turned)
                first_ref[slots + slot] = other[:, :depth].astype(jnp.bfloat16)
        return carry

    lax.fori_loop(0, sizes.structures, fill, 0)


def tile_kernel(sizes, band_ref, list_ref, listed_ref, first_ref, marks_ref, same_ref, across_ref, *refs):
    structures, sweeps, slots, groups = sizes.structures, sizes.sweeps, sizes.slots, sizes.groups
    out_refs = refs[:structures]
    second_ref, counts_ref, held_ref, sums_ref, picks_ref, state_ref, total_ref = refs[structures:]
    row_here = lax.axis_index("row")
    column_here = lax.axis_index("col")
    family = lax.div(row_here, sizes.share)
    chip_here = lax.rem(row_here, sizes.share) * sizes.half + lax.div(column_here, 2)
    core_here = lax.rem(column_here, 2)
    lane = lax.broadcasted_iota(jnp.int32, (1, 128), 1)
    row = lax.broadcasted_iota(jnp.int32, (8, 128), 0)
    ones = jnp.where((row == 3) | (row == 4), 1.0, 0.0)

    for core, piece_ref in ((core_here, same_ref), (1 - core_here, across_ref)):
        for k in range(sizes.chips):
            chip = lax.rem(chip_here + (sizes.chips - k), sizes.chips)
            device = chip * 2 + core
            base = k * sizes.rows
            counts_ref[pl.ds(pl.multiple_of(device * sweeps, sweeps), sweeps), :] = piece_ref[
                base + slots * 4 : base + slots * 4 + sweeps
            ]
            for turn in range(structures):
                origin = lax.rem(family + (structures - turn), structures)
                group = origin * sizes.plane + device
                for pair in range(sweeps // 2):
                    start = base + turn * sweeps * 4 + pair * 8
                    value = piece_ref[start : start + 8]
                    high = rounded(value)
                    low = value - high
                    high_turned = pltpu.roll(high, 4, 0)
                    for odd, (top, bottom) in enumerate(
                        ((high, pltpu.roll(low, 4, 0)), (high_turned, low))
                    ):
                        points = jnp.where(row < 4, top, bottom)
                        features = jnp.concatenate([points, jnp.where(row < 3, top, ones)], axis=0)
                        second_ref[(2 * pair + odd) * groups + group] = features.astype(jnp.bfloat16)
    listed_base = sizes.plane * sweeps
    chosen = lax.broadcasted_iota(jnp.int32, (structures, 128), 0) == family
    for k in range(listed_ref.shape[1] // 128):
        line = jnp.where(chosen, listed_ref[:, k * 128 : (k + 1) * 128], 0)
        counts_ref[listed_base + k : listed_base + k + 1] = jnp.sum(line, axis=0, keepdims=True).astype(
            jnp.float32
        )
    chunks, band_chunks = sizes.chunks, sizes.band_chunks

    total_ref[...] = jnp.zeros_like(total_ref)
    spare = 1.0 / (1.0 + jnp.exp(jnp.float32(-CONTACT_SHIFT)))

    def finish(ending):
        sums = sums_ref[pl.ds(0, UNIT, stride=8), :]
        for k in range(1, 8):
            sums = sums + sums_ref[pl.ds(k, UNIT, stride=8), :]
        chance = 64.0 * 128.0 + 0.5 * jnp.sum(sums, axis=1, keepdims=True)
        count = jnp.sum(picks_ref[...], axis=1, keepdims=True)
        state = state_ref[...]
        chance = jnp.where(state == 1, 0.5 * (chance - 128.0 * spare), chance)
        weight = jnp.where(state == 2, 0.0, 1.0 - count / (BACKGROUND + chance / 128.0))
        for t in range(0, UNIT, 2):
            left, right = (second_ref[ending[t + i] & 4095] for i in range(2))
            blank = jnp.zeros_like(left)
            both = jnp.concatenate(
                [jnp.concatenate([left, blank], axis=1), jnp.concatenate([blank, right], axis=1)], axis=0
            )
            product = lax.dot_general(
                both, held_ref[t // 2], (((1,), (1,)), ((), ())), preferred_element_type=jnp.float32
            )
            at = pl.multiple_of(((ending[t] >> 19) & 127) * POINT_ROWS, POINT_ROWS)
            total_ref[pl.ds(at, POINT_ROWS), :] += (
                weight[t : t + 1] * product[:POINT_ROWS] + weight[t + 1 : t + 2] * product[POINT_ROWS:]
            )

    def begin(beginning):
        for t in range(0, UNIT, 2):
            seconds = [beginning[t + i][0] & 4095 for i in range(2)]
            logit = jnp.dot(
                first_ref[(beginning[t][0] >> 12) & 127],
                jnp.concatenate(
                    [jnp.concatenate([second_ref[at], marks_ref[at]], axis=0) for at in seconds], axis=1
                ),
                preferred_element_type=jnp.float32,
            )
            bend = jnp.tanh(logit)
            held_ref[t // 2] = (1.0 - bend * bend).astype(jnp.bfloat16)
            for i in range(2):
                part = bend[:, i * 128 : (i + 1) * 128]
                sums_ref[(t + i) * 8 : (t + i + 1) * 8] = jnp.sum(part.reshape(16, 8, 128), axis=0)
                code, place = beginning[t + i]
                picked = counts_ref[pl.ds(place >> 7, 1), :]
                picks_ref[t + i : t + i + 1] = jnp.where(lane == (place & 127), picked, 0.0)
                state_ref[t + i : t + i + 1] = jnp.full((1, 128), code >> 26)
        return tuple(code for code, _ in beginning)

    def band_step(turn, ending):
        line = turn * (UNIT // 2) >> 7
        at = turn * (UNIT // 2) & 127
        beginning = []
        for t in range(UNIT):
            row = line + t % 2 * 2 * band_chunks
            beginning.append((band_ref[row, at + t // 2], band_ref[row + band_chunks, at + t // 2]))
        finish(ending)
        return begin(beginning)

    def listed_step(turn, ending):
        line = turn * UNIT >> 7
        at = turn * UNIT & 127
        beginning = [(list_ref[line, at + t], list_ref[chunks + line, at + t]) for t in range(UNIT)]
        finish(ending)
        return begin(beginning)

    idle = (jnp.int32(slots << 19),) * UNIT
    sums_ref[...] = jnp.zeros_like(sums_ref)
    ending = lax.fori_loop(0, band_ref[4 * band_chunks, 0], band_step, idle)
    listed_steps = lax.div(list_ref[2 * chunks, 0] + UNIT - 1, UNIT)
    finish(lax.fori_loop(0, listed_steps, listed_step, ending))

    scale = -2.0 * CONTACT_SLOPE / 128.0 / 4.0
    for k in range(structures):
        origin = lax.rem(family + k, structures)
        turn = (structures - k) % structures
        first = origin * sweeps * POINT_ROWS
        mass = total_ref[pl.ds(first + 11, sweeps, stride=POINT_ROWS), :]
        for place in range(3):
            point = same_ref[pl.ds(turn * sweeps * 4 + place, sweeps, stride=4), :]
            high = rounded(point)
            near = high + rounded(point - high)
            pull = (
                total_ref[pl.ds(first + place, sweeps, stride=POINT_ROWS), :]
                + total_ref[pl.ds(first + place + 4, sweeps, stride=POINT_ROWS), :]
            )
            out_refs[k][place] = scale * (near * mass - pull)


def place_kernel(sizes, *refs):
    family = lax.div(lax.axis_index("row"), sizes.share)
    for k, ref in enumerate(refs[:-1]):
        refs[-1][lax.rem(family + (sizes.structures - k), sizes.structures)] = ref[...]


def on_device(n_row, n_col, coords, chrom_lengths, band_counts, inter_pairs, inter_counts):
    structures, _, sweeps, block_size = coords.shape
    width = band_counts.shape[3]
    listed = inter_pairs.shape[1]
    sizes = Sizes(n_row, n_col, structures, sweeps, width, listed)
    share, slots, blocks = sizes.share, sizes.slots, sizes.blocks

    messages = pl.pallas_call(
        functools.partial(pack_kernel, sizes),
        out_shape=[jax.ShapeDtypeStruct((5 * sweeps, block_size), jnp.float32)] * structures,
        in_specs=[VMEM, VMEM],
        out_specs=[VMEM] * structures,
        compiler_params=SMALL,
        name="pack",
    )(coords, band_counts)
    deal = [
        [(i, (i // share + k) % structures * share + i % share) for i in range(n_row)]
        for k in range(structures)
    ]
    received = [messages[0]]
    for k in range(1, structures):
        received.append(lax.ppermute(messages[k], "row", deal[k]))
    labels = -(-chrom_lengths.shape[0] // 16) * 16
    band, edges = pl.pallas_call(
        functools.partial(band_kernel, sizes),
        out_shape=[
            jax.ShapeDtypeStruct((4 * sizes.band_chunks + 8, block_size), jnp.int32),
            jax.ShapeDtypeStruct((2, labels, block_size), jnp.int32),
        ],
        in_specs=[SMEM],
        out_specs=[VMEM] * 2,
        compiler_params=SMALL,
        name="band_tiles",
    )(chrom_lengths)

    own_row = pl.pallas_call(
        functools.partial(merge_kernel, 4 * sweeps),
        out_shape=jax.ShapeDtypeStruct((sizes.rows, block_size), jnp.float32),
        in_specs=[ANY] + [VMEM] * structures,
        out_specs=VMEM,
        compiler_params=SMALL,
        name="merge",
    )(band, *received)

    def device(family, chip, core):
        row = family * share + chip // sizes.half
        return row * n_col + chip % sizes.half * 2 + core

    pieces = [own_row]
    for k in range(1, sizes.chips):
        moves = [
            (device(f, i, core), device(f, (i + k) % sizes.chips, core))
            for f in range(structures)
            for i in range(sizes.chips)
            for core in range(2)
        ]
        pieces.append(lax.ppermute(own_row, AXES, moves))
    depth = POINT_ROWS + labels
    own, marks = pl.pallas_call(
        functools.partial(own_kernel, sizes),
        out_shape=[
            jax.ShapeDtypeStruct((2 * slots, block_size, depth), jnp.bfloat16),
            jax.ShapeDtypeStruct((blocks, labels, block_size), jnp.bfloat16),
        ],
        in_specs=[VMEM, VMEM],
        out_specs=[VMEM] * 2,
        compiler_params=pltpu.CompilerParams(vmem_limit_bytes=24 * 1024 * 1024),
        name="own_features",
    )(edges, own_row)

    same = pl.pallas_call(
        join_kernel,
        out_shape=jax.ShapeDtypeStruct((sizes.chips * sizes.rows, block_size), jnp.float32),
        in_specs=[ANY] + [VMEM] * sizes.chips,
        out_specs=VMEM,
        compiler_params=SMALL,
        name="join",
    )(marks, *pieces)
    across = lax.ppermute(same, "col", [(i, i ^ 1) for i in range(n_col)])

    tiles = pl.pallas_call(
        functools.partial(list_kernel, sizes),
        out_shape=jax.ShapeDtypeStruct((2 * sizes.chunks + 8, block_size), jnp.int32),
        in_specs=[VMEM, ANY],
        out_specs=VMEM,
        scratch_shapes=[pltpu.VMEM((2 * listed // block_size, POINT_ROWS, block_size), jnp.bfloat16)],
        cost_estimate=pl.CostEstimate(flops=1 << 28, bytes_accessed=1 << 22, transcendentals=0),
        compiler_params=SMALL,
        name="list_tiles",
    )(jnp.transpose(inter_pairs, (0, 2, 1)), same)

    gains = pl.pallas_call(
        functools.partial(tile_kernel, sizes),
        out_shape=[jax.ShapeDtypeStruct((3, sweeps, block_size), jnp.float32)] * structures,
        in_specs=[SMEM] * 2 + [VMEM] * 5,
        out_specs=[VMEM] * structures,
        scratch_shapes=[
            pltpu.VMEM((blocks, POINT_ROWS, block_size), jnp.bfloat16),
            pltpu.VMEM((sizes.plane * sweeps + listed // block_size, block_size), jnp.float32),
            pltpu.VMEM((UNIT // 2, block_size, 2 * block_size), jnp.bfloat16),
            pltpu.VMEM((UNIT * 8, block_size), jnp.float32),
            pltpu.VMEM((UNIT, block_size), jnp.float32),
            pltpu.VMEM((UNIT, block_size), jnp.int32),
            pltpu.VMEM(((slots + 1) * POINT_ROWS, block_size), jnp.float32),
        ],
        compiler_params=pltpu.CompilerParams(vmem_limit_bytes=40 * 1024 * 1024),
        name="tiles",
    )(band, tiles, inter_counts, own, marks, same, across)

    arrived = [gains[0]]
    for k in range(1, structures):
        arrived.append(lax.ppermute(gains[k], "row", deal[k]))
    return pl.pallas_call(
        functools.partial(place_kernel, sizes),
        out_shape=jax.ShapeDtypeStruct(coords.shape, jnp.float32),
        in_specs=[VMEM] * structures,
        out_specs=VMEM,
        compiler_params=SMALL,
        name="place",
    )(*arrived)


def solution(mesh):
    placed = (
        P(None, None, None, ("row", "col")),
        P(),
        P(None, None, ("row", "col"), None),
        P(),
        P(),
    )
    return jax.shard_map(
        functools.partial(on_device, mesh.shape["row"], mesh.shape["col"]),
        mesh=mesh,
        in_specs=placed,
        out_specs=P(None, None, None, ("row", "col")),
        check_vma=False,
    )
```

```python
import functools

import jax
import jax.numpy as jnp
from jax import lax
from jax.experimental import pallas as pl
from jax.experimental.pallas import tpu as pltpu
from jax.sharding import PartitionSpec as P

CONTACT_SHIFT = 3.0
CONTACT_SLOPE = 0.5
BACKGROUND = 0.5
FAR = 32.0
UNIT = 64
POINT_ROWS = 16
AXES = ("row", "col")
VMEM = pl.BlockSpec(memory_space=pltpu.VMEM)
SMEM = pl.BlockSpec(memory_space=pltpu.SMEM)
ANY = pl.BlockSpec(memory_space=pl.ANY)
SMALL = pltpu.CompilerParams(vmem_limit_bytes=8 * 1024 * 1024)


def rounded(value):
    return value.astype(jnp.bfloat16).astype(jnp.float32)


def divide(value, by):
    return value >> (by.bit_length() - 1) if by & (by - 1) == 0 else lax.div(value, by)


def modulo(value, by):
    return value & (by - 1) if by & (by - 1) == 0 else lax.rem(value, by)


class Sizes:
    def __init__(self, n_row, n_col, structures, sweeps, width, listed):
        self.n_row, self.n_col, self.structures, self.sweeps = n_row, n_col, structures, sweeps
        self.width = width
        self.share = n_row // structures
        self.plane = self.share * n_col
        self.chips = self.plane // 2
        self.half = n_col // 2
        self.groups = n_row * n_col
        self.blocks = self.groups * sweeps
        self.slots = structures * sweeps
        self.chunks = (2 * listed + self.slots + 2 * UNIT) // 128 + 1
        self.band_chunks = (self.slots * width + UNIT) // 128 + 1
        self.rows = self.slots * 4 + sweeps


def pack_kernel(sizes, coords_ref, counts_ref, *out_refs):
    sweeps, width = sizes.sweeps, sizes.width
    family = lax.div(lax.axis_index("row"), sizes.share)
    lane = lax.broadcasted_iota(jnp.int32, (width, 128), 1)
    place = lax.broadcasted_iota(jnp.int32, (width, 128), 0) + family * width
    spread = (lane == place).astype(jnp.float32)
    for k, out_ref in enumerate(out_refs):
        member = lax.rem(family + k, sizes.structures)
        norm = jnp.zeros((sweeps, 128), jnp.float32)
        for place in range(3):
            point = coords_ref[member, place]
            out_ref[pl.ds(place, sweeps, stride=4), :] = point
            high = rounded(point)
            near = high + rounded(point - high)
            norm = norm - 0.5 * CONTACT_SLOPE * near * near
        out_ref[pl.ds(3, sweeps, stride=4), :] = norm
        counts = counts_ref[member][:, 0, :].astype(jnp.float32)
        out_ref[4 * sweeps : 5 * sweeps] = jnp.dot(counts, spread, preferred_element_type=jnp.float32)


def merge_kernel(points, after_ref, *refs):
    counts = refs[0][points:]
    for k, ref in enumerate(refs[:-1]):
        refs[-1][k * points : (k + 1) * points] = ref[:points]
        counts = counts + ref[points:] if k else counts
    refs[-1][(len(refs) - 1) * points :] = counts


def join_kernel(after_ref, *refs):
    rows = refs[0].shape[0]
    for k, ref in enumerate(refs[:-1]):
        refs[-1][k * rows : (k + 1) * rows] = ref[...]


def below(value):
    rows = value.shape[0]
    row = lax.broadcasted_iota(jnp.int32, (rows, rows), 0)
    lower = (row > lax.broadcasted_iota(jnp.int32, (rows, rows), 1)).astype(jnp.float32)
    return jnp.dot(lower, value, precision=lax.Precision.HIGHEST, preferred_element_type=jnp.float32)


def band_kernel(sizes, lengths_ref, list_ref, edges_ref):
    slots, sweeps, groups = sizes.slots, sizes.sweeps, sizes.groups
    family = lax.div(lax.axis_index("row"), sizes.share)
    here = lax.rem(lax.axis_index("row"), sizes.share) * sizes.n_col + lax.axis_index("col")
    lane = lax.broadcasted_iota(jnp.int32, (1, 128), 1)

    slot_row = lax.broadcasted_iota(jnp.int32, (slots, 128), 0)
    block = modulo(slot_row, sweeps) * groups + divide(slot_row, sweeps) * sizes.plane + here
    first_bead = block * 128
    low = jnp.zeros((slots, 128), jnp.int32)
    high = jnp.full((slots, 128), sizes.blocks * 128)
    edges_ref[...] = jnp.zeros_like(edges_ref)
    end = jnp.int32(0)
    for k in range(lengths_ref.shape[0]):
        start = end
        end = end + lengths_ref[k]
        edges_ref[0, k : k + 1] = jnp.full((1, 128), start)
        edges_ref[1, k : k + 1] = jnp.full((1, 128), end)
        low = jnp.maximum(low, jnp.where(start <= first_bead, start, 0))
        high = jnp.minimum(high, jnp.where(end > first_bead + 127, end, sizes.blocks * 128))
    low = jnp.maximum(low >> 7, block - (sizes.width - 1))
    high = jnp.minimum(jnp.minimum((high - 1) >> 7, block + (sizes.width - 1)), sizes.blocks - 1)
    in_band = (high - low + 2) >> 1
    begin = below(in_band.astype(jnp.float32)).astype(jnp.int32)
    band_total = jnp.max(begin + in_band)
    chunks = sizes.band_chunks

    def band(chunk, carry):
        pair = chunk * 128 + lane
        inside = (begin <= pair) & (pair < begin + in_band)

        def pick(value):
            return jnp.sum(jnp.where(inside, value, 0), axis=0, keepdims=True)

        live = pick(1) > 0
        slot = pick(slot_row)
        near = pick(low - 2 * begin) + 2 * pair
        last = pick(high)
        here_block = pick(block)
        for i in range(2):
            second = jnp.where(live, jnp.minimum(near + i, last), 0)
            first = jnp.minimum(here_block, second)
            group = modulo(first, groups)
            line = modulo(group, sizes.plane) * sweeps + divide(first, groups)
            apart = jnp.abs(here_block - second)
            place = line * 128 + divide(group, sizes.plane) * sizes.width + apart
            state = jnp.where(live & (near + i <= last), jnp.where(apart == 0, 1, 0), 2)
            code = second + (slot << 12) + (jnp.where(live, slot, slots) << 19) + (state << 26)
            at = 2 * i * chunks + chunk
            list_ref[pl.ds(at, 1), :] = code
            list_ref[pl.ds(at + chunks, 1), :] = jnp.where(live, place, 0)
        return carry

    lax.fori_loop(0, lax.div(band_total + UNIT, 128) + 1, band, 0)
    steps = lax.div(band_total + (UNIT // 2 - 1), UNIT // 2)
    list_ref[4 * chunks : 4 * chunks + 1] = jnp.full((1, 128), steps)


def list_kernel(sizes, pairs_ref, after_ref, list_ref, digits_ref):
    slots, sweeps, groups, chunks = sizes.slots, sizes.sweeps, sizes.groups, sizes.chunks
    family = lax.div(lax.axis_index("row"), sizes.share)
    here = lax.rem(lax.axis_index("row"), sizes.share) * sizes.n_col + lax.axis_index("col")
    lane = lax.broadcasted_iota(jnp.int32, (1, 128), 1)
    slot_row = lax.broadcasted_iota(jnp.int32, (slots, 128), 0)

    half = pairs_ref.shape[2] // 128
    lines = 2 * half
    pairs = pairs_ref[family]
    group = modulo(pairs, groups)
    mine = modulo(group, sizes.plane) == here
    slot = jnp.where(mine, divide(group, sizes.plane) * sweeps + divide(pairs, groups), -1)
    other = pairs

    def cut(value, line):
        side, at = line // half, line % half * 128
        return value[side : side + 1, at : at + 128]

    before = lax.broadcasted_iota(jnp.int32, (128, 256), 0)
    after = lax.broadcasted_iota(jnp.int32, (128, 256), 1)
    count = (before <= after).astype(jnp.float32).astype(jnp.bfloat16)
    running = jnp.zeros((slots, 128), jnp.float32)
    picked = []
    for line in range(lines):
        chosen = (cut(slot, line) == slot_row).astype(jnp.float32)
        counted = jnp.dot(chosen.astype(jnp.bfloat16), count, preferred_element_type=jnp.float32)
        inner = jnp.sum(chosen * (counted[:, :128] - 1.0 + running), axis=0, keepdims=True)
        picked.append((chosen, inner))
        running = running + counted[:, 128:]
    doubled = 2.0 * jnp.floor(0.5 * (running + 1.0))
    base = below(doubled)
    number = jnp.max(base + doubled).astype(jnp.int32)
    digit_row = lax.broadcasted_iota(jnp.int32, (POINT_ROWS, 128), 0)
    ranks = []
    for line in range(lines):
        chosen, inner = picked[line]
        rank = inner + jnp.sum(chosen * base, axis=0, keepdims=True)
        ranks.append(jnp.where(cut(slot, line) >= 0, rank.astype(jnp.int32), -1))
        opposite = (line + half) % lines
        partner = cut(other, opposite)
        digits = jnp.zeros((POINT_ROWS, 128), jnp.int32)
        for place, digit in enumerate(
            (partner & 31, partner >> 5, cut(slot, line), lane, line % half + 0 * lane, 1 + 0 * lane)
        ):
            digits = jnp.where(digit_row == place, digit, digits)
        digits_ref[line] = digits.astype(jnp.float32).astype(jnp.bfloat16)
    spot = lax.broadcasted_iota(jnp.int32, (128, 128), 0)

    def compact(chunk, carry):
        found = jnp.zeros((POINT_ROWS, 128), jnp.float32)
        for line in range(0, lines, 2):
            there = jnp.concatenate(
                [(ranks[line + i] == spot + chunk * 128).astype(jnp.float32).astype(jnp.bfloat16) for i in range(2)],
                axis=1,
            )
            found = found + lax.dot_general(
                jnp.concatenate([digits_ref[line], digits_ref[line + 1]], axis=1),
                there,
                (((1,), (1,)), ((), ())),
                preferred_element_type=jnp.float32,
            )
        found = found.astype(jnp.int32)
        at = found[2:3]
        code = found[0:1] + (found[1:2] << 5) + ((slots + at) << 12) + (at << 19)
        list_ref[pl.ds(chunk, 1), :] = jnp.where(found[5:6] > 0, code, (slots << 19) + (2 << 26))
        list_ref[pl.ds(chunks + chunk, 1), :] = (
            sizes.plane * sweeps * 128 + found[3:4] + found[4:5] * 128
        )
        return carry

    lax.fori_loop(0, lax.div(number + 2 * UNIT - 1, 128) + 1, compact, 0)
    list_ref[2 * chunks : 2 * chunks + 1] = jnp.full((1, 128), number)


def own_kernel(sizes, edges_ref, own_ref, first_ref, marks_ref):
    slots, sweeps, groups = sizes.slots, sizes.sweeps, sizes.groups
    family = lax.div(lax.axis_index("row"), sizes.share)
    here = lax.rem(lax.axis_index("row"), sizes.share) * sizes.n_col + lax.axis_index("col")
    lane = lax.broadcasted_iota(jnp.int32, (1, 128), 1)
    row = lax.broadcasted_iota(jnp.int32, (8, 128), 0)
    labels = edges_ref.shape[1]
    depth = POINT_ROWS + labels

    def mark(group, carry):
        for u in range(sweeps):
            bead = (u * groups + group) * 128 + lane
            inside = (bead >= edges_ref[0]) & (bead < edges_ref[1])
            marks_ref[u * groups + group] = inside.astype(jnp.float32).astype(jnp.bfloat16)
        return carry

    lax.fori_loop(0, groups, mark, 0)

    def fill(turn, carry):
        origin = lax.rem(family + (sizes.structures - turn), sizes.structures)
        for pair in range(sweeps // 2):
            value = own_ref[pl.ds(pl.multiple_of(turn * sweeps * 4 + pair * 8, 8), 8), :]
            for odd in range(2):
                value = pltpu.roll(value, 4, 0) if odd else value
                high = rounded(value)
                low = rounded(value - high)
                shifted = value + 0.5 * CONTACT_SHIFT
                shifted_high = rounded(shifted)
                shifted_low = rounded(shifted - shifted_high)
                both = jnp.where(row < 4, high, pltpu.roll(high, 4, 0))
                near = jnp.where((row & 3) == 3, 1.0, CONTACT_SLOPE * both)
                rest = jnp.where(row == 4, pltpu.roll(shifted_low, 1, 0), 0.0)
                rest = jnp.where(row == 3, shifted_high, rest)
                rest = jnp.where(row < 3, CONTACT_SLOPE * low, rest)
                u = 2 * pair + odd
                bead = (u * groups + origin * sizes.plane + here) * 128 + lane
                inside = (bead >= edges_ref[0]) & (bead < edges_ref[1])
                apart = jnp.where(inside, 0.0, -FAR)
                blank = jnp.zeros((128 - depth, 128), jnp.float32)
                turned = jnp.transpose(jnp.concatenate([near, rest, apart, blank], axis=0))
                slot = origin * sweeps + u
                first_ref[slot] = turned[:, :depth].astype(jnp.bfloat16)
                other = jnp.where(lane < POINT_ROWS, turned, -FAR - turned)
                first_ref[slots + slot] = other[:, :depth].astype(jnp.bfloat16)
        return carry

    lax.fori_loop(0, sizes.structures, fill, 0)


def tile_kernel(sizes, band_ref, list_ref, listed_ref, first_ref, marks_ref, same_ref, across_ref, *refs):
    structures, sweeps, slots, groups = sizes.structures, sizes.sweeps, sizes.slots, sizes.groups
    out_refs = refs[:structures]
    second_ref, counts_ref, held_ref, sums_ref, picks_ref, state_ref, total_ref, gain_ref = refs[structures:]
    row_here = lax.axis_index("row")
    column_here = lax.axis_index("col")
    family = lax.div(row_here, sizes.share)
    chip_here = lax.rem(row_here, sizes.share) * sizes.half + lax.div(column_here, 2)
    core_here = lax.rem(column_here, 2)
    lane = lax.broadcasted_iota(jnp.int32, (1, 128), 1)
    row = lax.broadcasted_iota(jnp.int32, (8, 128), 0)
    ones = jnp.where((row == 3) | (row == 4), 1.0, 0.0)
    narrow = lax.broadcasted_iota(jnp.int32, (1, 2 * POINT_ROWS), 1)

    for core, piece_ref in ((core_here, same_ref), (1 - core_here, across_ref)):
        for k in range(sizes.chips):
            chip = lax.rem(chip_here + (sizes.chips - k), sizes.chips)
            device = chip * 2 + core
            base = k * sizes.rows
            counts_ref[pl.ds(pl.multiple_of(device * sweeps, sweeps), sweeps), :] = piece_ref[
                base + slots * 4 : base + slots * 4 + sweeps
            ]
            for turn in range(structures):
                origin = lax.rem(family + (structures - turn), structures)
                group = origin * sizes.plane + device
                for pair in range(sweeps // 2):
                    start = base + turn * sweeps * 4 + pair * 8
                    value = piece_ref[start : start + 8]
                    high = rounded(value)
                    low = value - high
                    high_turned = pltpu.roll(high, 4, 0)
                    for odd, (top, bottom) in enumerate(
                        ((high, pltpu.roll(low, 4, 0)), (high_turned, low))
                    ):
                        points = jnp.where(row < 4, top, bottom)
                        features = jnp.concatenate([points, jnp.where(row < 3, top, ones)], axis=0)
                        second_ref[(2 * pair + odd) * groups + group] = features.astype(jnp.bfloat16)
    listed_base = sizes.plane * sweeps
    chosen = lax.broadcasted_iota(jnp.int32, (structures, 128), 0) == family
    for k in range(listed_ref.shape[1] // 128):
        line = jnp.where(chosen, listed_ref[:, k * 128 : (k + 1) * 128], 0)
        counts_ref[listed_base + k : listed_base + k + 1] = jnp.sum(line, axis=0, keepdims=True).astype(
            jnp.float32
        )
    chunks, band_chunks = sizes.chunks, sizes.band_chunks

    total_ref[...] = jnp.zeros_like(total_ref)
    spare = 1.0 / (1.0 + jnp.exp(jnp.float32(-CONTACT_SHIFT)))

    def finish(ending):
        sums = sums_ref[pl.ds(0, UNIT, stride=8), :]
        for k in range(1, 8):
            sums = sums + sums_ref[pl.ds(k, UNIT, stride=8), :]
        chance = 64.0 * 128.0 + 0.5 * jnp.sum(sums, axis=1, keepdims=True)
        count = jnp.sum(picks_ref[...], axis=1, keepdims=True)
        state = state_ref[...]
        chance = jnp.where(state == 1, 0.5 * (chance - 128.0 * spare), chance)
        weight = jnp.where(state == 2, 0.0, 1.0 - count / (BACKGROUND + chance / 128.0))
        for t in range(0, UNIT, 2):
            left, right = (second_ref[ending[t + i] & 4095] for i in range(2))
            blank = jnp.zeros_like(left)
            both = jnp.concatenate(
                [jnp.concatenate([left, blank], axis=1), jnp.concatenate([blank, right], axis=1)], axis=0
            )
            product = lax.dot_general(
                held_ref[t // 2], both, (((1,), (1,)), ((), ())), preferred_element_type=jnp.float32
            )
            scale = jnp.where(
                narrow < POINT_ROWS,
                weight[t : t + 1, : 2 * POINT_ROWS],
                weight[t + 1 : t + 2, : 2 * POINT_ROWS],
            )
            total_ref[(ending[t] >> 19) & 127] += scale * product

    def begin(beginning):
        for t in range(0, UNIT, 2):
            seconds = [beginning[t + i][0] & 4095 for i in range(2)]
            logit = jnp.dot(
                first_ref[(beginning[t][0] >> 12) & 127],
                jnp.concatenate(
                    [jnp.concatenate([second_ref[at], marks_ref[at]], axis=0) for at in seconds], axis=1
                ),
                preferred_element_type=jnp.float32,
            )
            bend = jnp.tanh(logit)
            held_ref[t // 2] = (1.0 - bend * bend).astype(jnp.bfloat16)
            for i in range(2):
                part = bend[:, i * 128 : (i + 1) * 128]
                sums_ref[(t + i) * 8 : (t + i + 1) * 8] = jnp.sum(part.reshape(16, 8, 128), axis=0)
                code, place = beginning[t + i]
                picked = counts_ref[pl.ds(place >> 7, 1), :]
                picks_ref[t + i : t + i + 1] = jnp.where(lane == (place & 127), picked, 0.0)
                state_ref[t + i : t + i + 1] = jnp.full((1, 128), code >> 26)
        return tuple(code for code, _ in beginning)

    def band_step(turn, ending):
        line = turn * (UNIT // 2) >> 7
        at = turn * (UNIT // 2) & 127
        beginning = []
        for t in range(UNIT):
            row = line + t % 2 * 2 * band_chunks
            beginning.append((band_ref[row, at + t // 2], band_ref[row + band_chunks, at + t // 2]))
        finish(ending)
        return begin(beginning)

    def listed_step(turn, ending):
        line = turn * UNIT >> 7
        at = turn * UNIT & 127
        beginning = [(list_ref[line, at + t], list_ref[chunks + line, at + t]) for t in range(UNIT)]
        finish(ending)
        return begin(beginning)

    idle = (jnp.int32(slots << 19),) * UNIT
    sums_ref[...] = jnp.zeros_like(sums_ref)
    ending = lax.fori_loop(0, band_ref[4 * band_chunks, 0], band_step, idle)
    listed_steps = lax.div(list_ref[2 * chunks, 0] + UNIT - 1, UNIT)
    finish(lax.fori_loop(0, listed_steps, listed_step, ending))

    def collect(slot, carry):
        turned = jnp.transpose(total_ref[slot])
        gain_ref[pl.ds(pl.multiple_of(slot * POINT_ROWS, POINT_ROWS), POINT_ROWS), :] = (
            turned[:POINT_ROWS] + turned[POINT_ROWS:]
        )
        return carry

    lax.fori_loop(0, slots, collect, 0, unroll=8)
    scale = -2.0 * CONTACT_SLOPE / 128.0 / 4.0
    for k in range(structures):
        origin = lax.rem(family + k, structures)
        turn = (structures - k) % structures
        first = origin * sweeps * POINT_ROWS
        mass = gain_ref[pl.ds(first + 11, sweeps, stride=POINT_ROWS), :]
        for place in range(3):
            point = same_ref[pl.ds(turn * sweeps * 4 + place, sweeps, stride=4), :]
            high = rounded(point)
            near = high + rounded(point - high)
            pull = (
                gain_ref[pl.ds(first + place, sweeps, stride=POINT_ROWS), :]
                + gain_ref[pl.ds(first + place + 4, sweeps, stride=POINT_ROWS), :]
            )
            out_refs[k][place] = scale * (near * mass - pull)


def place_kernel(sizes, *refs):
    family = lax.div(lax.axis_index("row"), sizes.share)
    for k, ref in enumerate(refs[:-1]):
        refs[-1][lax.rem(family + (sizes.structures - k), sizes.structures)] = ref[...]


def on_device(n_row, n_col, coords, chrom_lengths, band_counts, inter_pairs, inter_counts):
    structures, _, sweeps, block_size = coords.shape
    width = band_counts.shape[3]
    listed = inter_pairs.shape[1]
    sizes = Sizes(n_row, n_col, structures, sweeps, width, listed)
    share, slots, blocks = sizes.share, sizes.slots, sizes.blocks

    messages = pl.pallas_call(
        functools.partial(pack_kernel, sizes),
        out_shape=[jax.ShapeDtypeStruct((5 * sweeps, block_size), jnp.float32)] * structures,
        in_specs=[VMEM, VMEM],
        out_specs=[VMEM] * structures,
        compiler_params=SMALL,
        name="pack",
    )(coords, band_counts)
    deal = [
        [(i, (i // share + k) % structures * share + i % share) for i in range(n_row)]
        for k in range(structures)
    ]
    received = [messages[0]]
    for k in range(1, structures):
        received.append(lax.ppermute(messages[k], "row", deal[k]))
    labels = -(-chrom_lengths.shape[0] // 16) * 16
    band, edges = pl.pallas_call(
        functools.partial(band_kernel, sizes),
        out_shape=[
            jax.ShapeDtypeStruct((4 * sizes.band_chunks + 8, block_size), jnp.int32),
            jax.ShapeDtypeStruct((2, labels, block_size), jnp.int32),
        ],
        in_specs=[SMEM],
        out_specs=[VMEM] * 2,
        compiler_params=SMALL,
        name="band_tiles",
    )(chrom_lengths)

    own_row = pl.pallas_call(
        functools.partial(merge_kernel, 4 * sweeps),
        out_shape=jax.ShapeDtypeStruct((sizes.rows, block_size), jnp.float32),
        in_specs=[ANY] + [VMEM] * structures,
        out_specs=VMEM,
        compiler_params=SMALL,
        name="merge",
    )(band, *received)

    def device(family, chip, core):
        row = family * share + chip // sizes.half
        return row * n_col + chip % sizes.half * 2 + core

    pieces = [own_row]
    for k in range(1, sizes.chips):
        moves = [
            (device(f, i, core), device(f, (i + k) % sizes.chips, core))
            for f in range(structures)
            for i in range(sizes.chips)
            for core in range(2)
        ]
        pieces.append(lax.ppermute(own_row, AXES, moves))
    depth = POINT_ROWS + labels
    own, marks = pl.pallas_call(
        functools.partial(own_kernel, sizes),
        out_shape=[
            jax.ShapeDtypeStruct((2 * slots, block_size, depth), jnp.bfloat16),
            jax.ShapeDtypeStruct((blocks, labels, block_size), jnp.bfloat16),
        ],
        in_specs=[VMEM, VMEM],
        out_specs=[VMEM] * 2,
        compiler_params=pltpu.CompilerParams(vmem_limit_bytes=24 * 1024 * 1024),
        name="own_features",
    )(edges, own_row)

    same = pl.pallas_call(
        join_kernel,
        out_shape=jax.ShapeDtypeStruct((sizes.chips * sizes.rows, block_size), jnp.float32),
        in_specs=[ANY] + [VMEM] * sizes.chips,
        out_specs=VMEM,
        compiler_params=SMALL,
        name="join",
    )(marks, *pieces)
    across = lax.ppermute(same, "col", [(i, i ^ 1) for i in range(n_col)])

    tiles = pl.pallas_call(
        functools.partial(list_kernel, sizes),
        out_shape=jax.ShapeDtypeStruct((2 * sizes.chunks + 8, block_size), jnp.int32),
        in_specs=[VMEM, ANY],
        out_specs=VMEM,
        scratch_shapes=[pltpu.VMEM((2 * listed // block_size, POINT_ROWS, block_size), jnp.bfloat16)],
        cost_estimate=pl.CostEstimate(flops=1 << 28, bytes_accessed=1 << 22, transcendentals=0),
        compiler_params=SMALL,
        name="list_tiles",
    )(jnp.transpose(inter_pairs, (0, 2, 1)), same)

    gains = pl.pallas_call(
        functools.partial(tile_kernel, sizes),
        out_shape=[jax.ShapeDtypeStruct((3, sweeps, block_size), jnp.float32)] * structures,
        in_specs=[SMEM] * 2 + [VMEM] * 5,
        out_specs=[VMEM] * structures,
        scratch_shapes=[
            pltpu.VMEM((blocks, POINT_ROWS, block_size), jnp.bfloat16),
            pltpu.VMEM((sizes.plane * sweeps + listed // block_size, block_size), jnp.float32),
            pltpu.VMEM((UNIT // 2, block_size, 2 * block_size), jnp.bfloat16),
            pltpu.VMEM((UNIT * 8, block_size), jnp.float32),
            pltpu.VMEM((UNIT, block_size), jnp.float32),
            pltpu.VMEM((UNIT, block_size), jnp.int32),
            pltpu.VMEM((slots + 1, block_size, 2 * POINT_ROWS), jnp.float32),
            pltpu.VMEM((slots * POINT_ROWS, block_size), jnp.float32),
        ],
        compiler_params=pltpu.CompilerParams(vmem_limit_bytes=40 * 1024 * 1024),
        name="tiles",
    )(band, tiles, inter_counts, own, marks, same, across)

    arrived = [gains[0]]
    for k in range(1, structures):
        arrived.append(lax.ppermute(gains[k], "row", deal[k]))
    return pl.pallas_call(
        functools.partial(place_kernel, sizes),
        out_shape=jax.ShapeDtypeStruct(coords.shape, jnp.float32),
        in_specs=[VMEM] * structures,
        out_specs=VMEM,
        compiler_params=SMALL,
        name="place",
    )(*arrived)


def solution(mesh):
    placed = (
        P(None, None, None, ("row", "col")),
        P(),
        P(None, None, ("row", "col"), None),
        P(),
        P(),
    )
    return jax.shard_map(
        functools.partial(on_device, mesh.shape["row"], mesh.shape["col"]),
        mesh=mesh,
        in_specs=placed,
        out_specs=P(None, None, None, ("row", "col")),
        check_vma=False,
    )
```

```python
import functools

import jax
import jax.numpy as jnp
from jax import lax
from jax.experimental import pallas as pl
from jax.experimental.pallas import tpu as pltpu
from jax.sharding import PartitionSpec as P

CONTACT_SHIFT = 3.0
CONTACT_SLOPE = 0.5
BACKGROUND = 0.5
FAR = 32.0
UNIT = 32
POINT_ROWS = 16
AXES = ("row", "col")
VMEM = pl.BlockSpec(memory_space=pltpu.VMEM)
SMEM = pl.BlockSpec(memory_space=pltpu.SMEM)
ANY = pl.BlockSpec(memory_space=pl.ANY)
SMALL = pltpu.CompilerParams(vmem_limit_bytes=8 * 1024 * 1024)


def rounded(value):
    return value.astype(jnp.bfloat16).astype(jnp.float32)


def divide(value, by):
    return value >> (by.bit_length() - 1) if by & (by - 1) == 0 else lax.div(value, by)


def modulo(value, by):
    return value & (by - 1) if by & (by - 1) == 0 else lax.rem(value, by)


class Sizes:
    def __init__(self, n_row, n_col, structures, sweeps, width, listed):
        self.n_row, self.n_col, self.structures, self.sweeps = n_row, n_col, structures, sweeps
        self.width = width
        self.share = n_row // structures
        self.plane = self.share * n_col
        self.chips = self.plane // 2
        self.half = n_col // 2
        self.groups = n_row * n_col
        self.blocks = self.groups * sweeps
        self.slots = structures * sweeps
        self.chunks = (2 * listed + self.slots + 2 * UNIT) // 128 + 1
        self.band_chunks = (self.slots * width + UNIT) // 128 + 1
        self.rows = self.slots * 4 + sweeps


def pack_kernel(sizes, coords_ref, counts_ref, *out_refs):
    sweeps, width = sizes.sweeps, sizes.width
    family = lax.div(lax.axis_index("row"), sizes.share)
    lane = lax.broadcasted_iota(jnp.int32, (width, 128), 1)
    place = lax.broadcasted_iota(jnp.int32, (width, 128), 0) + family * width
    spread = (lane == place).astype(jnp.float32)
    for k, out_ref in enumerate(out_refs):
        member = lax.rem(family + k, sizes.structures)
        norm = jnp.zeros((sweeps, 128), jnp.float32)
        for place in range(3):
            point = coords_ref[member, place]
            out_ref[pl.ds(place, sweeps, stride=4), :] = point
            high = rounded(point)
            near = high + rounded(point - high)
            norm = norm - 0.5 * CONTACT_SLOPE * near * near
        out_ref[pl.ds(3, sweeps, stride=4), :] = norm
        counts = counts_ref[member][:, 0, :].astype(jnp.float32)
        out_ref[4 * sweeps : 5 * sweeps] = jnp.dot(counts, spread, preferred_element_type=jnp.float32)


def merge_kernel(points, after_ref, *refs):
    counts = refs[0][points:]
    for k, ref in enumerate(refs[:-1]):
        refs[-1][k * points : (k + 1) * points] = ref[:points]
        counts = counts + ref[points:] if k else counts
    refs[-1][(len(refs) - 1) * points :] = counts


def join_kernel(after_ref, *refs):
    rows = refs[0].shape[0]
    for k, ref in enumerate(refs[:-1]):
        refs[-1][k * rows : (k + 1) * rows] = ref[...]


def below(value):
    rows = value.shape[0]
    row = lax.broadcasted_iota(jnp.int32, (rows, rows), 0)
    lower = (row > lax.broadcasted_iota(jnp.int32, (rows, rows), 1)).astype(jnp.float32)
    return jnp.dot(lower, value, precision=lax.Precision.HIGHEST, preferred_element_type=jnp.float32)


def band_kernel(sizes, lengths_ref, list_ref, edges_ref):
    slots, sweeps, groups = sizes.slots, sizes.sweeps, sizes.groups
    family = lax.div(lax.axis_index("row"), sizes.share)
    here = lax.rem(lax.axis_index("row"), sizes.share) * sizes.n_col + lax.axis_index("col")
    lane = lax.broadcasted_iota(jnp.int32, (1, 128), 1)

    slot_row = lax.broadcasted_iota(jnp.int32, (slots, 128), 0)
    block = modulo(slot_row, sweeps) * groups + divide(slot_row, sweeps) * sizes.plane + here
    first_bead = block * 128
    low = jnp.zeros((slots, 128), jnp.int32)
    high = jnp.full((slots, 128), sizes.blocks * 128)
    edges_ref[...] = jnp.zeros_like(edges_ref)
    end = jnp.int32(0)
    for k in range(lengths_ref.shape[0]):
        start = end
        end = end + lengths_ref[k]
        edges_ref[0, k : k + 1] = jnp.full((1, 128), start)
        edges_ref[1, k : k + 1] = jnp.full((1, 128), end)
        low = jnp.maximum(low, jnp.where(start <= first_bead, start, 0))
        high = jnp.minimum(high, jnp.where(end > first_bead + 127, end, sizes.blocks * 128))
    low = jnp.maximum(low >> 7, block - (sizes.width - 1))
    high = jnp.minimum(jnp.minimum((high - 1) >> 7, block + (sizes.width - 1)), sizes.blocks - 1)
    in_band = (high - low + 2) >> 1
    begin = below(in_band.astype(jnp.float32)).astype(jnp.int32)
    band_total = jnp.max(begin + in_band)
    chunks = sizes.band_chunks

    def band(chunk, carry):
        pair = chunk * 128 + lane
        inside = (begin <= pair) & (pair < begin + in_band)

        def pick(value):
            return jnp.sum(jnp.where(inside, value, 0), axis=0, keepdims=True)

        live = pick(1) > 0
        slot = pick(slot_row)
        near = pick(low - 2 * begin) + 2 * pair
        last = pick(high)
        here_block = pick(block)
        for i in range(2):
            second = jnp.where(live, jnp.minimum(near + i, last), 0)
            first = jnp.minimum(here_block, second)
            group = modulo(first, groups)
            line = modulo(group, sizes.plane) * sweeps + divide(first, groups)
            apart = jnp.abs(here_block - second)
            place = line * 128 + divide(group, sizes.plane) * sizes.width + apart
            state = jnp.where(live & (near + i <= last), jnp.where(apart == 0, 1, 0), 2)
            code = second + (slot << 12) + (jnp.where(live, slot, slots) << 19) + (state << 26)
            at = 2 * i * chunks + chunk
            list_ref[pl.ds(at, 1), :] = code
            list_ref[pl.ds(at + chunks, 1), :] = jnp.where(live, place, 0)
        return carry

    lax.fori_loop(0, lax.div(band_total + UNIT, 128) + 1, band, 0)
    steps = lax.div(band_total + (UNIT // 2 - 1), UNIT // 2)
    list_ref[4 * chunks : 4 * chunks + 1] = jnp.full((1, 128), steps)


def list_kernel(sizes, pairs_ref, after_ref, list_ref, digits_ref):
    slots, sweeps, groups, chunks = sizes.slots, sizes.sweeps, sizes.groups, sizes.chunks
    family = lax.div(lax.axis_index("row"), sizes.share)
    here = lax.rem(lax.axis_index("row"), sizes.share) * sizes.n_col + lax.axis_index("col")
    lane = lax.broadcasted_iota(jnp.int32, (1, 128), 1)
    slot_row = lax.broadcasted_iota(jnp.int32, (slots, 128), 0)

    half = pairs_ref.shape[2] // 128
    lines = 2 * half
    pairs = pairs_ref[family]
    group = modulo(pairs, groups)
    mine = modulo(group, sizes.plane) == here
    slot = jnp.where(mine, divide(group, sizes.plane) * sweeps + divide(pairs, groups), -1)
    other = pairs

    def cut(value, line):
        side, at = line // half, line % half * 128
        return value[side : side + 1, at : at + 128]

    before = lax.broadcasted_iota(jnp.int32, (128, 256), 0)
    after = lax.broadcasted_iota(jnp.int32, (128, 256), 1)
    count = (before <= after).astype(jnp.float32).astype(jnp.bfloat16)
    running = jnp.zeros((slots, 128), jnp.float32)
    picked = []
    for line in range(lines):
        chosen = (cut(slot, line) == slot_row).astype(jnp.float32)
        counted = jnp.dot(chosen.astype(jnp.bfloat16), count, preferred_element_type=jnp.float32)
        inner = jnp.sum(chosen * (counted[:, :128] - 1.0 + running), axis=0, keepdims=True)
        picked.append((chosen, inner))
        running = running + counted[:, 128:]
    doubled = 2.0 * jnp.floor(0.5 * (running + 1.0))
    base = below(doubled)
    number = jnp.max(base + doubled).astype(jnp.int32)
    digit_row = lax.broadcasted_iota(jnp.int32, (POINT_ROWS, 128), 0)
    ranks = []
    for line in range(lines):
        chosen, inner = picked[line]
        rank = inner + jnp.sum(chosen * base, axis=0, keepdims=True)
        ranks.append(jnp.where(cut(slot, line) >= 0, rank.astype(jnp.int32), -1))
        opposite = (line + half) % lines
        partner = cut(other, opposite)
        digits = jnp.zeros((POINT_ROWS, 128), jnp.int32)
        for place, digit in enumerate(
            (partner & 31, partner >> 5, cut(slot, line), lane, line % half + 0 * lane, 1 + 0 * lane)
        ):
            digits = jnp.where(digit_row == place, digit, digits)
        digits_ref[line] = digits.astype(jnp.float32).astype(jnp.bfloat16)
    spot = lax.broadcasted_iota(jnp.int32, (128, 128), 0)

    def compact(chunk, carry):
        found = jnp.zeros((POINT_ROWS, 128), jnp.float32)
        for line in range(0, lines, 2):
            there = jnp.concatenate(
                [(ranks[line + i] == spot + chunk * 128).astype(jnp.float32).astype(jnp.bfloat16) for i in range(2)],
                axis=1,
            )
            found = found + lax.dot_general(
                jnp.concatenate([digits_ref[line], digits_ref[line + 1]], axis=1),
                there,
                (((1,), (1,)), ((), ())),
                preferred_element_type=jnp.float32,
            )
        found = found.astype(jnp.int32)
        at = found[2:3]
        code = found[0:1] + (found[1:2] << 5) + ((slots + at) << 12) + (at << 19)
        list_ref[pl.ds(chunk, 1), :] = jnp.where(found[5:6] > 0, code, (slots << 19) + (2 << 26))
        list_ref[pl.ds(chunks + chunk, 1), :] = (
            sizes.plane * sweeps * 128 + found[3:4] + found[4:5] * 128
        )
        return carry

    lax.fori_loop(0, lax.div(number + 2 * UNIT - 1, 128) + 1, compact, 0)
    list_ref[2 * chunks : 2 * chunks + 1] = jnp.full((1, 128), number)


def own_kernel(sizes, edges_ref, own_ref, first_ref, marks_ref):
    slots, sweeps, groups = sizes.slots, sizes.sweeps, sizes.groups
    family = lax.div(lax.axis_index("row"), sizes.share)
    here = lax.rem(lax.axis_index("row"), sizes.share) * sizes.n_col + lax.axis_index("col")
    lane = lax.broadcasted_iota(jnp.int32, (1, 128), 1)
    row = lax.broadcasted_iota(jnp.int32, (8, 128), 0)
    labels = edges_ref.shape[1]
    depth = POINT_ROWS + labels

    def mark(group, carry):
        for u in range(sweeps):
            bead = (u * groups + group) * 128 + lane
            inside = (bead >= edges_ref[0]) & (bead < edges_ref[1])
            marks_ref[u * groups + group] = inside.astype(jnp.float32).astype(jnp.bfloat16)
        return carry

    lax.fori_loop(0, groups, mark, 0)

    def fill(turn, carry):
        origin = lax.rem(family + (sizes.structures - turn), sizes.structures)
        for pair in range(sweeps // 2):
            value = own_ref[pl.ds(pl.multiple_of(turn * sweeps * 4 + pair * 8, 8), 8), :]
            for odd in range(2):
                value = pltpu.roll(value, 4, 0) if odd else value
                high = rounded(value)
                low = rounded(value - high)
                shifted = value + 0.5 * CONTACT_SHIFT
                shifted_high = rounded(shifted)
                shifted_low = rounded(shifted - shifted_high)
                both = jnp.where(row < 4, high, pltpu.roll(high, 4, 0))
                near = jnp.where((row & 3) == 3, 1.0, CONTACT_SLOPE * both)
                rest = jnp.where(row == 4, pltpu.roll(shifted_low, 1, 0), 0.0)
                rest = jnp.where(row == 3, shifted_high, rest)
                rest = jnp.where(row < 3, CONTACT_SLOPE * low, rest)
                u = 2 * pair + odd
                bead = (u * groups + origin * sizes.plane + here) * 128 + lane
                inside = (bead >= edges_ref[0]) & (bead < edges_ref[1])
                apart = jnp.where(inside, 0.0, -FAR)
                blank = jnp.zeros((128 - depth, 128), jnp.float32)
                turned = jnp.transpose(jnp.concatenate([near, rest, apart, blank], axis=0))
                slot = origin * sweeps + u
                first_ref[slot] = turned[:, :depth].astype(jnp.bfloat16)
                other = jnp.where(lane < POINT_ROWS, turned, -FAR - turned)
                first_ref[slots + slot] = other[:, :depth].astype(jnp.bfloat16)
        return carry

    lax.fori_loop(0, sizes.structures, fill, 0)


def tile_kernel(sizes, band_ref, list_ref, listed_ref, first_ref, marks_ref, same_ref, across_ref, *refs):
    structures, sweeps, slots, groups = sizes.structures, sizes.sweeps, sizes.slots, sizes.groups
    out_refs = refs[:structures]
    second_ref, counts_ref, held_ref, sums_ref, picks_ref, state_ref, total_ref, gain_ref = refs[structures:]
    row_here = lax.axis_index("row")
    column_here = lax.axis_index("col")
    family = lax.div(row_here, sizes.share)
    chip_here = lax.rem(row_here, sizes.share) * sizes.half + lax.div(column_here, 2)
    core_here = lax.rem(column_here, 2)
    lane = lax.broadcasted_iota(jnp.int32, (1, 128), 1)
    row = lax.broadcasted_iota(jnp.int32, (8, 128), 0)
    ones = jnp.where((row == 3) | (row == 4), 1.0, 0.0)
    narrow = lax.broadcasted_iota(jnp.int32, (1, 2 * POINT_ROWS), 1)

    for core, piece_ref in ((core_here, same_ref), (1 - core_here, across_ref)):
        for k in range(sizes.chips):
            chip = lax.rem(chip_here + (sizes.chips - k), sizes.chips)
            device = chip * 2 + core
            base = k * sizes.rows
            counts_ref[pl.ds(pl.multiple_of(device * sweeps, sweeps), sweeps), :] = piece_ref[
                base + slots * 4 : base + slots * 4 + sweeps
            ]
            for turn in range(structures):
                origin = lax.rem(family + (structures - turn), structures)
                group = origin * sizes.plane + device
                for pair in range(sweeps // 2):
                    start = base + turn * sweeps * 4 + pair * 8
                    value = piece_ref[start : start + 8]
                    high = rounded(value)
                    low = value - high
                    high_turned = pltpu.roll(high, 4, 0)
                    for odd, (top, bottom) in enumerate(
                        ((high, pltpu.roll(low, 4, 0)), (high_turned, low))
                    ):
                        points = jnp.where(row < 4, top, bottom)
                        features = jnp.concatenate([points, jnp.where(row < 3, top, ones)], axis=0)
                        second_ref[(2 * pair + odd) * groups + group] = features.astype(jnp.bfloat16)
    listed_base = sizes.plane * sweeps
    chosen = lax.broadcasted_iota(jnp.int32, (structures, 128), 0) == family
    for k in range(listed_ref.shape[1] // 128):
        line = jnp.where(chosen, listed_ref[:, k * 128 : (k + 1) * 128], 0)
        counts_ref[listed_base + k : listed_base + k + 1] = jnp.sum(line, axis=0, keepdims=True).astype(
            jnp.float32
        )
    chunks, band_chunks = sizes.chunks, sizes.band_chunks

    total_ref[...] = jnp.zeros_like(total_ref)
    spare = 1.0 / (1.0 + jnp.exp(jnp.float32(-CONTACT_SHIFT)))

    def finish(ending):
        sums = sums_ref[pl.ds(0, UNIT, stride=8), :]
        for k in range(1, 8):
            sums = sums + sums_ref[pl.ds(k, UNIT, stride=8), :]
        chance = 64.0 * 128.0 + 0.5 * jnp.sum(sums, axis=1, keepdims=True)
        count = jnp.sum(picks_ref[...], axis=1, keepdims=True)
        state = state_ref[...]
        chance = jnp.where(state == 1, 0.5 * (chance - 128.0 * spare), chance)
        weight = jnp.where(state == 2, 0.0, 1.0 - count / (BACKGROUND + chance / 128.0))
        for t in range(0, UNIT, 2):
            left, right = (second_ref[ending[t + i] & 4095] for i in range(2))
            blank = jnp.zeros_like(left)
            both = jnp.concatenate(
                [jnp.concatenate([left, blank], axis=1), jnp.concatenate([blank, right], axis=1)], axis=0
            )
            product = lax.dot_general(
                held_ref[t // 2], both, (((1,), (1,)), ((), ())), preferred_element_type=jnp.float32
            )
            scale = jnp.where(
                narrow < POINT_ROWS,
                weight[t : t + 1, : 2 * POINT_ROWS],
                weight[t + 1 : t + 2, : 2 * POINT_ROWS],
            )
            total_ref[(ending[t] >> 19) & 127] += scale * product

    def begin(beginning):
        for t in range(0, UNIT, 2):
            seconds = [beginning[t + i][0] & 4095 for i in range(2)]
            logit = jnp.dot(
                first_ref[(beginning[t][0] >> 12) & 127],
                jnp.concatenate(
                    [jnp.concatenate([second_ref[at], marks_ref[at]], axis=0) for at in seconds], axis=1
                ),
                preferred_element_type=jnp.float32,
            )
            bend = jnp.tanh(logit)
            held_ref[t // 2] = (1.0 - bend * bend).astype(jnp.bfloat16)
            for i in range(2):
                part = bend[:, i * 128 : (i + 1) * 128]
                sums_ref[(t + i) * 8 : (t + i + 1) * 8] = jnp.sum(part.reshape(16, 8, 128), axis=0)
                code, place = beginning[t + i]
                picked = counts_ref[pl.ds(place >> 7, 1), :]
                picks_ref[t + i : t + i + 1] = jnp.where(lane == (place & 127), picked, 0.0)
                state_ref[t + i : t + i + 1] = jnp.full((1, 128), code >> 26)
        return tuple(code for code, _ in beginning)

    def band_step(turn, ending):
        line = turn * (UNIT // 2) >> 7
        at = turn * (UNIT // 2) & 127
        beginning = []
        for t in range(UNIT):
            row = line + t % 2 * 2 * band_chunks
            beginning.append((band_ref[row, at + t // 2], band_ref[row + band_chunks, at + t // 2]))
        finish(ending)
        return begin(beginning)

    def listed_step(turn, ending):
        line = turn * UNIT >> 7
        at = turn * UNIT & 127
        beginning = [(list_ref[line, at + t], list_ref[chunks + line, at + t]) for t in range(UNIT)]
        finish(ending)
        return begin(beginning)

    idle = (jnp.int32(slots << 19),) * UNIT
    sums_ref[...] = jnp.zeros_like(sums_ref)
    ending = lax.fori_loop(0, band_ref[4 * band_chunks, 0], band_step, idle)
    listed_steps = lax.div(list_ref[2 * chunks, 0] + UNIT - 1, UNIT)
    finish(lax.fori_loop(0, listed_steps, listed_step, ending))

    def collect(slot, carry):
        turned = jnp.transpose(total_ref[slot])
        gain_ref[pl.ds(pl.multiple_of(slot * POINT_ROWS, POINT_ROWS), POINT_ROWS), :] = (
            turned[:POINT_ROWS] + turned[POINT_ROWS:]
        )
        return carry

    lax.fori_loop(0, slots, collect, 0, unroll=8)
    scale = -2.0 * CONTACT_SLOPE / 128.0 / 4.0
    for k in range(structures):
        origin = lax.rem(family + k, structures)
        turn = (structures - k) % structures
        first = origin * sweeps * POINT_ROWS
        mass = gain_ref[pl.ds(first + 11, sweeps, stride=POINT_ROWS), :]
        for place in range(3):
            point = same_ref[pl.ds(turn * sweeps * 4 + place, sweeps, stride=4), :]
            high = rounded(point)
            near = high + rounded(point - high)
            pull = (
                gain_ref[pl.ds(first + place, sweeps, stride=POINT_ROWS), :]
                + gain_ref[pl.ds(first + place + 4, sweeps, stride=POINT_ROWS), :]
            )
            out_refs[k][place] = scale * (near * mass - pull)


def place_kernel(sizes, *refs):
    family = lax.div(lax.axis_index("row"), sizes.share)
    for k, ref in enumerate(refs[:-1]):
        refs[-1][lax.rem(family + (sizes.structures - k), sizes.structures)] = ref[...]


def on_device(n_row, n_col, coords, chrom_lengths, band_counts, inter_pairs, inter_counts):
    structures, _, sweeps, block_size = coords.shape
    width = band_counts.shape[3]
    listed = inter_pairs.shape[1]
    sizes = Sizes(n_row, n_col, structures, sweeps, width, listed)
    share, slots, blocks = sizes.share, sizes.slots, sizes.blocks

    messages = pl.pallas_call(
        functools.partial(pack_kernel, sizes),
        out_shape=[jax.ShapeDtypeStruct((5 * sweeps, block_size), jnp.float32)] * structures,
        in_specs=[VMEM, VMEM],
        out_specs=[VMEM] * structures,
        compiler_params=SMALL,
        name="pack",
    )(coords, band_counts)
    deal = [
        [(i, (i // share + k) % structures * share + i % share) for i in range(n_row)]
        for k in range(structures)
    ]
    received = [messages[0]]
    for k in range(1, structures):
        received.append(lax.ppermute(messages[k], "row", deal[k]))
    labels = -(-chrom_lengths.shape[0] // 16) * 16
    band, edges = pl.pallas_call(
        functools.partial(band_kernel, sizes),
        out_shape=[
            jax.ShapeDtypeStruct((4 * sizes.band_chunks + 8, block_size), jnp.int32),
            jax.ShapeDtypeStruct((2, labels, block_size), jnp.int32),
        ],
        in_specs=[SMEM],
        out_specs=[VMEM] * 2,
        compiler_params=SMALL,
        name="band_tiles",
    )(chrom_lengths)

    own_row = pl.pallas_call(
        functools.partial(merge_kernel, 4 * sweeps),
        out_shape=jax.ShapeDtypeStruct((sizes.rows, block_size), jnp.float32),
        in_specs=[ANY] + [VMEM] * structures,
        out_specs=VMEM,
        compiler_params=SMALL,
        name="merge",
    )(band, *received)

    def device(family, chip, core):
        row = family * share + chip // sizes.half
        return row * n_col + chip % sizes.half * 2 + core

    pieces = [own_row]
    for k in range(1, sizes.chips):
        moves = [
            (device(f, i, core), device(f, (i + k) % sizes.chips, core))
            for f in range(structures)
            for i in range(sizes.chips)
            for core in range(2)
        ]
        pieces.append(lax.ppermute(own_row, AXES, moves))
    depth = POINT_ROWS + labels
    own, marks = pl.pallas_call(
        functools.partial(own_kernel, sizes),
        out_shape=[
            jax.ShapeDtypeStruct((2 * slots, block_size, depth), jnp.bfloat16),
            jax.ShapeDtypeStruct((blocks, labels, block_size), jnp.bfloat16),
        ],
        in_specs=[VMEM, VMEM],
        out_specs=[VMEM] * 2,
        compiler_params=pltpu.CompilerParams(vmem_limit_bytes=24 * 1024 * 1024),
        name="own_features",
    )(edges, own_row)

    same = pl.pallas_call(
        join_kernel,
        out_shape=jax.ShapeDtypeStruct((sizes.chips * sizes.rows, block_size), jnp.float32),
        in_specs=[ANY] + [VMEM] * sizes.chips,
        out_specs=VMEM,
        compiler_params=SMALL,
        name="join",
    )(marks, *pieces)
    across = lax.ppermute(same, "col", [(i, i ^ 1) for i in range(n_col)])

    tiles = pl.pallas_call(
        functools.partial(list_kernel, sizes),
        out_shape=jax.ShapeDtypeStruct((2 * sizes.chunks + 8, block_size), jnp.int32),
        in_specs=[VMEM, ANY],
        out_specs=VMEM,
        scratch_shapes=[pltpu.VMEM((2 * listed // block_size, POINT_ROWS, block_size), jnp.bfloat16)],
        cost_estimate=pl.CostEstimate(flops=1 << 28, bytes_accessed=1 << 22, transcendentals=0),
        compiler_params=SMALL,
        name="list_tiles",
    )(jnp.transpose(inter_pairs, (0, 2, 1)), same)

    gains = pl.pallas_call(
        functools.partial(tile_kernel, sizes),
        out_shape=[jax.ShapeDtypeStruct((3, sweeps, block_size), jnp.float32)] * structures,
        in_specs=[SMEM] * 2 + [VMEM] * 5,
        out_specs=[VMEM] * structures,
        scratch_shapes=[
            pltpu.VMEM((blocks, POINT_ROWS, block_size), jnp.bfloat16),
            pltpu.VMEM((sizes.plane * sweeps + listed // block_size, block_size), jnp.float32),
            pltpu.VMEM((UNIT // 2, block_size, 2 * block_size), jnp.bfloat16),
            pltpu.VMEM((UNIT * 8, block_size), jnp.float32),
            pltpu.VMEM((UNIT, block_size), jnp.float32),
            pltpu.VMEM((UNIT, block_size), jnp.int32),
            pltpu.VMEM((slots + 1, block_size, 2 * POINT_ROWS), jnp.float32),
            pltpu.VMEM((slots * POINT_ROWS, block_size), jnp.float32),
        ],
        compiler_params=pltpu.CompilerParams(vmem_limit_bytes=40 * 1024 * 1024),
        name="tiles",
    )(band, tiles, inter_counts, own, marks, same, across)

    arrived = [gains[0]]
    for k in range(1, structures):
        arrived.append(lax.ppermute(gains[k], "row", deal[k]))
    return pl.pallas_call(
        functools.partial(place_kernel, sizes),
        out_shape=jax.ShapeDtypeStruct(coords.shape, jnp.float32),
        in_specs=[VMEM] * structures,
        out_specs=VMEM,
        compiler_params=SMALL,
        name="place",
    )(*arrived)


def solution(mesh):
    placed = (
        P(None, None, None, ("row", "col")),
        P(),
        P(None, None, ("row", "col"), None),
        P(),
        P(),
    )
    return jax.shard_map(
        functools.partial(on_device, mesh.shape["row"], mesh.shape["col"]),
        mesh=mesh,
        in_specs=placed,
        out_specs=P(None, None, None, ("row", "col")),
        check_vma=False,
    )
```

```python
import functools

import jax
import jax.numpy as jnp
from jax import lax
from jax.experimental import pallas as pl
from jax.experimental.pallas import tpu as pltpu
from jax.sharding import PartitionSpec as P

CONTACT_SHIFT = 3.0
CONTACT_SLOPE = 0.5
BACKGROUND = 0.5
FAR = 32.0
UNIT = 64
SHORT = 32
POINT_ROWS = 16
AXES = ("row", "col")
VMEM = pl.BlockSpec(memory_space=pltpu.VMEM)
SMEM = pl.BlockSpec(memory_space=pltpu.SMEM)
ANY = pl.BlockSpec(memory_space=pl.ANY)
SMALL = pltpu.CompilerParams(vmem_limit_bytes=8 * 1024 * 1024)


def rounded(value):
    return value.astype(jnp.bfloat16).astype(jnp.float32)


def divide(value, by):
    return value >> (by.bit_length() - 1) if by & (by - 1) == 0 else lax.div(value, by)


def modulo(value, by):
    return value & (by - 1) if by & (by - 1) == 0 else lax.rem(value, by)


class Sizes:
    def __init__(self, n_row, n_col, structures, sweeps, width, listed):
        self.n_row, self.n_col, self.structures, self.sweeps = n_row, n_col, structures, sweeps
        self.width = width
        self.share = n_row // structures
        self.plane = self.share * n_col
        self.chips = self.plane // 2
        self.half = n_col // 2
        self.groups = n_row * n_col
        self.blocks = self.groups * sweeps
        self.slots = structures * sweeps
        self.chunks = (2 * listed + self.slots + 2 * UNIT) // 128 + 1
        self.band_chunks = (self.slots * width + UNIT) // 128 + 1
        self.rows = self.slots * 4 + sweeps


def pack_kernel(sizes, coords_ref, counts_ref, *out_refs):
    sweeps, width = sizes.sweeps, sizes.width
    family = lax.div(lax.axis_index("row"), sizes.share)
    lane = lax.broadcasted_iota(jnp.int32, (width, 128), 1)
    place = lax.broadcasted_iota(jnp.int32, (width, 128), 0) + family * width
    spread = (lane == place).astype(jnp.float32)
    for k, out_ref in enumerate(out_refs):
        member = lax.rem(family + k, sizes.structures)
        norm = jnp.zeros((sweeps, 128), jnp.float32)
        for place in range(3):
            point = coords_ref[member, place]
            out_ref[pl.ds(place, sweeps, stride=4), :] = point
            high = rounded(point)
            near = high + rounded(point - high)
            norm = norm - 0.5 * CONTACT_SLOPE * near * near
        out_ref[pl.ds(3, sweeps, stride=4), :] = norm
        counts = counts_ref[member][:, 0, :].astype(jnp.float32)
        out_ref[4 * sweeps : 5 * sweeps] = jnp.dot(counts, spread, preferred_element_type=jnp.float32)


def merge_kernel(points, after_ref, *refs):
    counts = refs[0][points:]
    for k, ref in enumerate(refs[:-1]):
        refs[-1][k * points : (k + 1) * points] = ref[:points]
        counts = counts + ref[points:] if k else counts
    refs[-1][(len(refs) - 1) * points :] = counts


def join_kernel(after_ref, *refs):
    rows = refs[0].shape[0]
    for k, ref in enumerate(refs[:-1]):
        refs[-1][k * rows : (k + 1) * rows] = ref[...]


def below(value):
    rows = value.shape[0]
    row = lax.broadcasted_iota(jnp.int32, (rows, rows), 0)
    lower = (row > lax.broadcasted_iota(jnp.int32, (rows, rows), 1)).astype(jnp.float32)
    return jnp.dot(lower, value, precision=lax.Precision.HIGHEST, preferred_element_type=jnp.float32)


def band_kernel(sizes, lengths_ref, list_ref, edges_ref):
    slots, sweeps, groups = sizes.slots, sizes.sweeps, sizes.groups
    family = lax.div(lax.axis_index("row"), sizes.share)
    here = lax.rem(lax.axis_index("row"), sizes.share) * sizes.n_col + lax.axis_index("col")
    lane = lax.broadcasted_iota(jnp.int32, (1, 128), 1)

    slot_row = lax.broadcasted_iota(jnp.int32, (slots, 128), 0)
    block = modulo(slot_row, sweeps) * groups + divide(slot_row, sweeps) * sizes.plane + here
    first_bead = block * 128
    low = jnp.zeros((slots, 128), jnp.int32)
    high = jnp.full((slots, 128), sizes.blocks * 128)
    edges_ref[...] = jnp.zeros_like(edges_ref)
    end = jnp.int32(0)
    for k in range(lengths_ref.shape[0]):
        start = end
        end = end + lengths_ref[k]
        edges_ref[0, k : k + 1] = jnp.full((1, 128), start)
        edges_ref[1, k : k + 1] = jnp.full((1, 128), end)
        low = jnp.maximum(low, jnp.where(start <= first_bead, start, 0))
        high = jnp.minimum(high, jnp.where(end > first_bead + 127, end, sizes.blocks * 128))
    low = jnp.maximum(low >> 7, block - (sizes.width - 1))
    high = jnp.minimum(jnp.minimum((high - 1) >> 7, block + (sizes.width - 1)), sizes.blocks - 1)
    in_band = (high - low + 2) >> 1
    begin = below(in_band.astype(jnp.float32)).astype(jnp.int32)
    band_total = jnp.max(begin + in_band)
    chunks = sizes.band_chunks

    def band(chunk, carry):
        pair = chunk * 128 + lane
        inside = (begin <= pair) & (pair < begin + in_band)

        def pick(value):
            return jnp.sum(jnp.where(inside, value, 0), axis=0, keepdims=True)

        live = pick(1) > 0
        slot = pick(slot_row)
        near = pick(low - 2 * begin) + 2 * pair
        last = pick(high)
        here_block = pick(block)
        for i in range(2):
            second = jnp.where(live, jnp.minimum(near + i, last), 0)
            first = jnp.minimum(here_block, second)
            group = modulo(first, groups)
            line = modulo(group, sizes.plane) * sweeps + divide(first, groups)
            apart = jnp.abs(here_block - second)
            place = line * 128 + divide(group, sizes.plane) * sizes.width + apart
            state = jnp.where(live & (near + i <= last), jnp.where(apart == 0, 1, 0), 2)
            code = second + (slot << 12) + (jnp.where(live, slot, slots) << 19) + (state << 26)
            at = 2 * i * chunks + chunk
            list_ref[pl.ds(at, 1), :] = code
            list_ref[pl.ds(at + chunks, 1), :] = jnp.where(live, place, 0)
        return carry

    lax.fori_loop(0, lax.div(band_total + UNIT, 128) + 1, band, 0)
    steps = lax.div(band_total + (UNIT // 2 - 1), UNIT // 2)
    list_ref[4 * chunks : 4 * chunks + 1] = jnp.full((1, 128), steps)


def list_kernel(sizes, pairs_ref, after_ref, list_ref, digits_ref):
    slots, sweeps, groups, chunks = sizes.slots, sizes.sweeps, sizes.groups, sizes.chunks
    family = lax.div(lax.axis_index("row"), sizes.share)
    here = lax.rem(lax.axis_index("row"), sizes.share) * sizes.n_col + lax.axis_index("col")
    lane = lax.broadcasted_iota(jnp.int32, (1, 128), 1)
    slot_row = lax.broadcasted_iota(jnp.int32, (slots, 128), 0)

    half = pairs_ref.shape[2] // 128
    lines = 2 * half
    pairs = pairs_ref[family]
    group = modulo(pairs, groups)
    mine = modulo(group, sizes.plane) == here
    slot = jnp.where(mine, divide(group, sizes.plane) * sweeps + divide(pairs, groups), -1)
    other = pairs

    def cut(value, line):
        side, at = line // half, line % half * 128
        return value[side : side + 1, at : at + 128]

    before = lax.broadcasted_iota(jnp.int32, (128, 256), 0)
    after = lax.broadcasted_iota(jnp.int32, (128, 256), 1)
    count = (before <= after).astype(jnp.float32).astype(jnp.bfloat16)
    running = jnp.zeros((slots, 128), jnp.float32)
    picked = []
    for line in range(lines):
        chosen = (cut(slot, line) == slot_row).astype(jnp.float32)
        counted = jnp.dot(chosen.astype(jnp.bfloat16), count, preferred_element_type=jnp.float32)
        inner = jnp.sum(chosen * (counted[:, :128] - 1.0 + running), axis=0, keepdims=True)
        picked.append((chosen, inner))
        running = running + counted[:, 128:]
    doubled = 2.0 * jnp.floor(0.5 * (running + 1.0))
    base = below(doubled)
    number = jnp.max(base + doubled).astype(jnp.int32)
    digit_row = lax.broadcasted_iota(jnp.int32, (POINT_ROWS, 128), 0)
    ranks = []
    for line in range(lines):
        chosen, inner = picked[line]
        rank = inner + jnp.sum(chosen * base, axis=0, keepdims=True)
        ranks.append(jnp.where(cut(slot, line) >= 0, rank.astype(jnp.int32), -1))
        opposite = (line + half) % lines
        partner = cut(other, opposite)
        digits = jnp.zeros((POINT_ROWS, 128), jnp.int32)
        for place, digit in enumerate(
            (partner & 31, partner >> 5, cut(slot, line), lane, line % half + 0 * lane, 1 + 0 * lane)
        ):
            digits = jnp.where(digit_row == place, digit, digits)
        digits_ref[line] = digits.astype(jnp.float32).astype(jnp.bfloat16)
    spot = lax.broadcasted_iota(jnp.int32, (128, 128), 0)

    def compact(chunk, carry):
        found = jnp.zeros((POINT_ROWS, 128), jnp.float32)
        for line in range(0, lines, 2):
            there = jnp.concatenate(
                [(ranks[line + i] == spot + chunk * 128).astype(jnp.float32).astype(jnp.bfloat16) for i in range(2)],
                axis=1,
            )
            found = found + lax.dot_general(
                jnp.concatenate([digits_ref[line], digits_ref[line + 1]], axis=1),
                there,
                (((1,), (1,)), ((), ())),
                preferred_element_type=jnp.float32,
            )
        found = found.astype(jnp.int32)
        at = found[2:3]
        code = found[0:1] + (found[1:2] << 5) + ((slots + at) << 12) + (at << 19)
        list_ref[pl.ds(chunk, 1), :] = jnp.where(found[5:6] > 0, code, (slots << 19) + (2 << 26))
        list_ref[pl.ds(chunks + chunk, 1), :] = (
            sizes.plane * sweeps * 128 + found[3:4] + found[4:5] * 128
        )
        return carry

    lax.fori_loop(0, lax.div(number + 2 * UNIT - 1, 128) + 1, compact, 0)
    list_ref[2 * chunks : 2 * chunks + 1] = jnp.full((1, 128), number)


def own_kernel(sizes, edges_ref, own_ref, first_ref, marks_ref):
    slots, sweeps, groups = sizes.slots, sizes.sweeps, sizes.groups
    family = lax.div(lax.axis_index("row"), sizes.share)
    here = lax.rem(lax.axis_index("row"), sizes.share) * sizes.n_col + lax.axis_index("col")
    lane = lax.broadcasted_iota(jnp.int32, (1, 128), 1)
    row = lax.broadcasted_iota(jnp.int32, (8, 128), 0)
    labels = edges_ref.shape[1]
    depth = POINT_ROWS + labels

    def mark(group, carry):
        for u in range(sweeps):
            bead = (u * groups + group) * 128 + lane
            inside = (bead >= edges_ref[0]) & (bead < edges_ref[1])
            marks_ref[u * groups + group] = inside.astype(jnp.float32).astype(jnp.bfloat16)
        return carry

    lax.fori_loop(0, groups, mark, 0)

    def fill(turn, carry):
        origin = lax.rem(family + (sizes.structures - turn), sizes.structures)
        for pair in range(sweeps // 2):
            value = own_ref[pl.ds(pl.multiple_of(turn * sweeps * 4 + pair * 8, 8), 8), :]
            for odd in range(2):
                value = pltpu.roll(value, 4, 0) if odd else value
                high = rounded(value)
                low = rounded(value - high)
                shifted = value + 0.5 * CONTACT_SHIFT
                shifted_high = rounded(shifted)
                shifted_low = rounded(shifted - shifted_high)
                both = jnp.where(row < 4, high, pltpu.roll(high, 4, 0))
                near = jnp.where((row & 3) == 3, 1.0, CONTACT_SLOPE * both)
                rest = jnp.where(row == 4, pltpu.roll(shifted_low, 1, 0), 0.0)
                rest = jnp.where(row == 3, shifted_high, rest)
                rest = jnp.where(row < 3, CONTACT_SLOPE * low, rest)
                u = 2 * pair + odd
                bead = (u * groups + origin * sizes.plane + here) * 128 + lane
                inside = (bead >= edges_ref[0]) & (bead < edges_ref[1])
                apart = jnp.where(inside, 0.0, -FAR)
                blank = jnp.zeros((128 - depth, 128), jnp.float32)
                turned = jnp.transpose(jnp.concatenate([near, rest, apart, blank], axis=0))
                slot = origin * sweeps + u
                first_ref[slot] = turned[:, :depth].astype(jnp.bfloat16)
                other = jnp.where(lane < POINT_ROWS, turned, -FAR - turned)
                first_ref[slots + slot] = other[:, :depth].astype(jnp.bfloat16)
        return carry

    lax.fori_loop(0, sizes.structures, fill, 0)


def tile_kernel(sizes, band_ref, list_ref, listed_ref, first_ref, marks_ref, same_ref, across_ref, *refs):
    structures, sweeps, slots, groups = sizes.structures, sizes.sweeps, sizes.slots, sizes.groups
    out_refs = refs[:structures]
    second_ref, counts_ref, held_ref, sums_ref, picks_ref, state_ref, total_ref, gain_ref = refs[structures:]
    row_here = lax.axis_index("row")
    column_here = lax.axis_index("col")
    family = lax.div(row_here, sizes.share)
    chip_here = lax.rem(row_here, sizes.share) * sizes.half + lax.div(column_here, 2)
    core_here = lax.rem(column_here, 2)
    lane = lax.broadcasted_iota(jnp.int32, (1, 128), 1)
    row = lax.broadcasted_iota(jnp.int32, (8, 128), 0)
    ones = jnp.where((row == 3) | (row == 4), 1.0, 0.0)
    narrow = lax.broadcasted_iota(jnp.int32, (1, 2 * POINT_ROWS), 1)

    for core, piece_ref in ((core_here, same_ref), (1 - core_here, across_ref)):
        for k in range(sizes.chips):
            chip = lax.rem(chip_here + (sizes.chips - k), sizes.chips)
            device = chip * 2 + core
            base = k * sizes.rows
            counts_ref[pl.ds(pl.multiple_of(device * sweeps, sweeps), sweeps), :] = piece_ref[
                base + slots * 4 : base + slots * 4 + sweeps
            ]
            for turn in range(structures):
                origin = lax.rem(family + (structures - turn), structures)
                group = origin * sizes.plane + device
                for pair in range(sweeps // 2):
                    start = base + turn * sweeps * 4 + pair * 8
                    value = piece_ref[start : start + 8]
                    high = rounded(value)
                    low = value - high
                    high_turned = pltpu.roll(high, 4, 0)
                    for odd, (top, bottom) in enumerate(
                        ((high, pltpu.roll(low, 4, 0)), (high_turned, low))
                    ):
                        points = jnp.where(row < 4, top, bottom)
                        features = jnp.concatenate([points, jnp.where(row < 3, top, ones)], axis=0)
                        second_ref[(2 * pair + odd) * groups + group] = features.astype(jnp.bfloat16)
    listed_base = sizes.plane * sweeps
    chosen = lax.broadcasted_iota(jnp.int32, (structures, 128), 0) == family
    for k in range(listed_ref.shape[1] // 128):
        line = jnp.where(chosen, listed_ref[:, k * 128 : (k + 1) * 128], 0)
        counts_ref[listed_base + k : listed_base + k + 1] = jnp.sum(line, axis=0, keepdims=True).astype(
            jnp.float32
        )
    chunks, band_chunks = sizes.chunks, sizes.band_chunks

    total_ref[...] = jnp.zeros_like(total_ref)
    spare = 1.0 / (1.0 + jnp.exp(jnp.float32(-CONTACT_SHIFT)))

    def finish(ending):
        unit = len(ending)
        sums = sums_ref[pl.ds(0, unit, stride=8), :]
        for k in range(1, 8):
            sums = sums + sums_ref[pl.ds(k, unit, stride=8), :]
        chance = 64.0 * 128.0 + 0.5 * jnp.sum(sums, axis=1, keepdims=True)
        count = jnp.sum(picks_ref[:unit], axis=1, keepdims=True)
        state = state_ref[:unit]
        chance = jnp.where(state == 1, 0.5 * (chance - 128.0 * spare), chance)
        weight = jnp.where(state == 2, 0.0, 1.0 - count / (BACKGROUND + chance / 128.0))
        for t in range(0, unit, 2):
            left, right = (second_ref[ending[t + i] & 4095] for i in range(2))
            blank = jnp.zeros_like(left)
            both = jnp.concatenate(
                [jnp.concatenate([left, blank], axis=1), jnp.concatenate([blank, right], axis=1)], axis=0
            )
            product = lax.dot_general(
                held_ref[t // 2], both, (((1,), (1,)), ((), ())), preferred_element_type=jnp.float32
            )
            scale = jnp.where(
                narrow < POINT_ROWS,
                weight[t : t + 1, : 2 * POINT_ROWS],
                weight[t + 1 : t + 2, : 2 * POINT_ROWS],
            )
            total_ref[(ending[t] >> 19) & 127] += scale * product

    def begin(beginning):
        for t in range(0, len(beginning), 2):
            seconds = [beginning[t + i][0] & 4095 for i in range(2)]
            logit = jnp.dot(
                first_ref[(beginning[t][0] >> 12) & 127],
                jnp.concatenate(
                    [jnp.concatenate([second_ref[at], marks_ref[at]], axis=0) for at in seconds], axis=1
                ),
                preferred_element_type=jnp.float32,
            )
            bend = jnp.tanh(logit)
            held_ref[t // 2] = (1.0 - bend * bend).astype(jnp.bfloat16)
            for i in range(2):
                part = bend[:, i * 128 : (i + 1) * 128]
                sums_ref[(t + i) * 8 : (t + i + 1) * 8] = jnp.sum(part.reshape(16, 8, 128), axis=0)
                code, place = beginning[t + i]
                picked = counts_ref[pl.ds(place >> 7, 1), :]
                picks_ref[t + i : t + i + 1] = jnp.where(lane == (place & 127), picked, 0.0)
                state_ref[t + i : t + i + 1] = jnp.full((1, 128), code >> 26)
        return tuple(code for code, _ in beginning)

    def band_step(turn, ending):
        line = turn * (UNIT // 2) >> 7
        at = turn * (UNIT // 2) & 127
        beginning = []
        for t in range(UNIT):
            row = line + t % 2 * 2 * band_chunks
            beginning.append((band_ref[row, at + t // 2], band_ref[row + band_chunks, at + t // 2]))
        finish(ending)
        return begin(beginning)

    def listed_step(turn, ending):
        line = turn * SHORT >> 7
        at = turn * SHORT & 127
        beginning = [(list_ref[line, at + t], list_ref[chunks + line, at + t]) for t in range(SHORT)]
        finish(ending)
        return begin(beginning)

    idle = (jnp.int32(slots << 19),) * UNIT
    sums_ref[...] = jnp.zeros_like(sums_ref)
    finish(lax.fori_loop(0, band_ref[4 * band_chunks, 0], band_step, idle))
    listed_steps = lax.div(list_ref[2 * chunks, 0] + SHORT - 1, SHORT)
    finish(lax.fori_loop(0, listed_steps, listed_step, idle[:SHORT]))

    def collect(slot, carry):
        turned = jnp.transpose(total_ref[slot])
        gain_ref[pl.ds(pl.multiple_of(slot * POINT_ROWS, POINT_ROWS), POINT_ROWS), :] = (
            turned[:POINT_ROWS] + turned[POINT_ROWS:]
        )
        return carry

    lax.fori_loop(0, slots, collect, 0, unroll=8)
    scale = -2.0 * CONTACT_SLOPE / 128.0 / 4.0
    for k in range(structures):
        origin = lax.rem(family + k, structures)
        turn = (structures - k) % structures
        first = origin * sweeps * POINT_ROWS
        mass = gain_ref[pl.ds(first + 11, sweeps, stride=POINT_ROWS), :]
        for place in range(3):
            point = same_ref[pl.ds(turn * sweeps * 4 + place, sweeps, stride=4), :]
            high = rounded(point)
            near = high + rounded(point - high)
            pull = (
                gain_ref[pl.ds(first + place, sweeps, stride=POINT_ROWS), :]
                + gain_ref[pl.ds(first + place + 4, sweeps, stride=POINT_ROWS), :]
            )
            out_refs[k][place] = scale * (near * mass - pull)


def place_kernel(sizes, *refs):
    family = lax.div(lax.axis_index("row"), sizes.share)
    for k, ref in enumerate(refs[:-1]):
        refs[-1][lax.rem(family + (sizes.structures - k), sizes.structures)] = ref[...]


def on_device(n_row, n_col, coords, chrom_lengths, band_counts, inter_pairs, inter_counts):
    structures, _, sweeps, block_size = coords.shape
    width = band_counts.shape[3]
    listed = inter_pairs.shape[1]
    sizes = Sizes(n_row, n_col, structures, sweeps, width, listed)
    share, slots, blocks = sizes.share, sizes.slots, sizes.blocks

    messages = pl.pallas_call(
        functools.partial(pack_kernel, sizes),
        out_shape=[jax.ShapeDtypeStruct((5 * sweeps, block_size), jnp.float32)] * structures,
        in_specs=[VMEM, VMEM],
        out_specs=[VMEM] * structures,
        compiler_params=SMALL,
        name="pack",
    )(coords, band_counts)
    deal = [
        [(i, (i // share + k) % structures * share + i % share) for i in range(n_row)]
        for k in range(structures)
    ]
    received = [messages[0]]
    for k in range(1, structures):
        received.append(lax.ppermute(messages[k], "row", deal[k]))
    labels = -(-chrom_lengths.shape[0] // 16) * 16
    band, edges = pl.pallas_call(
        functools.partial(band_kernel, sizes),
        out_shape=[
            jax.ShapeDtypeStruct((4 * sizes.band_chunks + 8, block_size), jnp.int32),
            jax.ShapeDtypeStruct((2, labels, block_size), jnp.int32),
        ],
        in_specs=[SMEM],
        out_specs=[VMEM] * 2,
        compiler_params=SMALL,
        name="band_tiles",
    )(chrom_lengths)

    own_row = pl.pallas_call(
        functools.partial(merge_kernel, 4 * sweeps),
        out_shape=jax.ShapeDtypeStruct((sizes.rows, block_size), jnp.float32),
        in_specs=[ANY] + [VMEM] * structures,
        out_specs=VMEM,
        compiler_params=SMALL,
        name="merge",
    )(band, *received)

    def device(family, chip, core):
        row = family * share + chip // sizes.half
        return row * n_col + chip % sizes.half * 2 + core

    pieces = [own_row]
    for k in range(1, sizes.chips):
        moves = [
            (device(f, i, core), device(f, (i + k) % sizes.chips, core))
            for f in range(structures)
            for i in range(sizes.chips)
            for core in range(2)
        ]
        pieces.append(lax.ppermute(own_row, AXES, moves))
    depth = POINT_ROWS + labels
    own, marks = pl.pallas_call(
        functools.partial(own_kernel, sizes),
        out_shape=[
            jax.ShapeDtypeStruct((2 * slots, block_size, depth), jnp.bfloat16),
            jax.ShapeDtypeStruct((blocks, labels, block_size), jnp.bfloat16),
        ],
        in_specs=[VMEM, VMEM],
        out_specs=[VMEM] * 2,
        compiler_params=pltpu.CompilerParams(vmem_limit_bytes=24 * 1024 * 1024),
        name="own_features",
    )(edges, own_row)

    same = pl.pallas_call(
        join_kernel,
        out_shape=jax.ShapeDtypeStruct((sizes.chips * sizes.rows, block_size), jnp.float32),
        in_specs=[ANY] + [VMEM] * sizes.chips,
        out_specs=VMEM,
        compiler_params=SMALL,
        name="join",
    )(marks, *pieces)
    across = lax.ppermute(same, "col", [(i, i ^ 1) for i in range(n_col)])

    tiles = pl.pallas_call(
        functools.partial(list_kernel, sizes),
        out_shape=jax.ShapeDtypeStruct((2 * sizes.chunks + 8, block_size), jnp.int32),
        in_specs=[VMEM, ANY],
        out_specs=VMEM,
        scratch_shapes=[pltpu.VMEM((2 * listed // block_size, POINT_ROWS, block_size), jnp.bfloat16)],
        cost_estimate=pl.CostEstimate(flops=1 << 28, bytes_accessed=1 << 22, transcendentals=0),
        compiler_params=SMALL,
        name="list_tiles",
    )(jnp.transpose(inter_pairs, (0, 2, 1)), same)

    gains = pl.pallas_call(
        functools.partial(tile_kernel, sizes),
        out_shape=[jax.ShapeDtypeStruct((3, sweeps, block_size), jnp.float32)] * structures,
        in_specs=[SMEM] * 2 + [VMEM] * 5,
        out_specs=[VMEM] * structures,
        scratch_shapes=[
            pltpu.VMEM((blocks, POINT_ROWS, block_size), jnp.bfloat16),
            pltpu.VMEM((sizes.plane * sweeps + listed // block_size, block_size), jnp.float32),
            pltpu.VMEM((UNIT // 2, block_size, 2 * block_size), jnp.bfloat16),
            pltpu.VMEM((UNIT * 8, block_size), jnp.float32),
            pltpu.VMEM((UNIT, block_size), jnp.float32),
            pltpu.VMEM((UNIT, block_size), jnp.int32),
            pltpu.VMEM((slots + 1, block_size, 2 * POINT_ROWS), jnp.float32),
            pltpu.VMEM((slots * POINT_ROWS, block_size), jnp.float32),
        ],
        compiler_params=pltpu.CompilerParams(vmem_limit_bytes=40 * 1024 * 1024),
        name="tiles",
    )(band, tiles, inter_counts, own, marks, same, across)

    arrived = [gains[0]]
    for k in range(1, structures):
        arrived.append(lax.ppermute(gains[k], "row", deal[k]))
    return pl.pallas_call(
        functools.partial(place_kernel, sizes),
        out_shape=jax.ShapeDtypeStruct(coords.shape, jnp.float32),
        in_specs=[VMEM] * structures,
        out_specs=VMEM,
        compiler_params=SMALL,
        name="place",
    )(*arrived)


def solution(mesh):
    placed = (
        P(None, None, None, ("row", "col")),
        P(),
        P(None, None, ("row", "col"), None),
        P(),
        P(),
    )
    return jax.shard_map(
        functools.partial(on_device, mesh.shape["row"], mesh.shape["col"]),
        mesh=mesh,
        in_specs=placed,
        out_specs=P(None, None, None, ("row", "col")),
        check_vma=False,
    )
```

```python
import functools

import jax
import jax.numpy as jnp
from jax import lax
from jax.experimental import pallas as pl
from jax.experimental.pallas import tpu as pltpu
from jax.sharding import PartitionSpec as P

CONTACT_SHIFT = 3.0
CONTACT_SLOPE = 0.5
BACKGROUND = 0.5
FAR = 32.0
UNIT = 32
POINT_ROWS = 16
AXES = ("row", "col")
VMEM = pl.BlockSpec(memory_space=pltpu.VMEM)
SMEM = pl.BlockSpec(memory_space=pltpu.SMEM)
ANY = pl.BlockSpec(memory_space=pl.ANY)
SMALL = pltpu.CompilerParams(vmem_limit_bytes=8 * 1024 * 1024)


def rounded(value):
    return value.astype(jnp.bfloat16).astype(jnp.float32)


def divide(value, by):
    return value >> (by.bit_length() - 1) if by & (by - 1) == 0 else lax.div(value, by)


def modulo(value, by):
    return value & (by - 1) if by & (by - 1) == 0 else lax.rem(value, by)


class Sizes:
    def __init__(self, n_row, n_col, structures, sweeps, width, listed):
        self.n_row, self.n_col, self.structures, self.sweeps = n_row, n_col, structures, sweeps
        self.width = width
        self.share = n_row // structures
        self.plane = self.share * n_col
        self.chips = self.plane // 2
        self.half = n_col // 2
        self.groups = n_row * n_col
        self.blocks = self.groups * sweeps
        self.slots = structures * sweeps
        self.chunks = (2 * listed + self.slots + 2 * UNIT) // 128 + 1
        self.band_chunks = (self.slots * width + UNIT) // 128 + 1
        self.rows = self.slots * 4 + sweeps


def pack_kernel(sizes, coords_ref, counts_ref, *out_refs):
    sweeps, width = sizes.sweeps, sizes.width
    family = lax.div(lax.axis_index("row"), sizes.share)
    lane = lax.broadcasted_iota(jnp.int32, (width, 128), 1)
    place = lax.broadcasted_iota(jnp.int32, (width, 128), 0) + family * width
    spread = (lane == place).astype(jnp.float32)
    for k, out_ref in enumerate(out_refs):
        member = lax.rem(family + k, sizes.structures)
        norm = jnp.zeros((sweeps, 128), jnp.float32)
        for place in range(3):
            point = coords_ref[member, place]
            out_ref[pl.ds(place, sweeps, stride=4), :] = point
            high = rounded(point)
            near = high + rounded(point - high)
            norm = norm - 0.5 * CONTACT_SLOPE * near * near
        out_ref[pl.ds(3, sweeps, stride=4), :] = norm
        counts = counts_ref[member][:, 0, :].astype(jnp.float32)
        out_ref[4 * sweeps : 5 * sweeps] = jnp.dot(counts, spread, preferred_element_type=jnp.float32)


def merge_kernel(points, after_ref, *refs):
    counts = refs[0][points:]
    for k, ref in enumerate(refs[:-1]):
        refs[-1][k * points : (k + 1) * points] = ref[:points]
        counts = counts + ref[points:] if k else counts
    refs[-1][(len(refs) - 1) * points :] = counts


def join_kernel(after_ref, *refs):
    rows = refs[0].shape[0]
    for k, ref in enumerate(refs[:-1]):
        refs[-1][k * rows : (k + 1) * rows] = ref[...]


def below(value):
    rows = value.shape[0]
    row = lax.broadcasted_iota(jnp.int32, (rows, rows), 0)
    lower = (row > lax.broadcasted_iota(jnp.int32, (rows, rows), 1)).astype(jnp.float32)
    return jnp.dot(lower, value, precision=lax.Precision.HIGHEST, preferred_element_type=jnp.float32)


def band_kernel(sizes, lengths_ref, list_ref, edges_ref):
    slots, sweeps, groups = sizes.slots, sizes.sweeps, sizes.groups
    family = lax.div(lax.axis_index("row"), sizes.share)
    here = lax.rem(lax.axis_index("row"), sizes.share) * sizes.n_col + lax.axis_index("col")
    lane = lax.broadcasted_iota(jnp.int32, (1, 128), 1)

    slot_row = lax.broadcasted_iota(jnp.int32, (slots, 128), 0)
    block = modulo(slot_row, sweeps) * groups + divide(slot_row, sweeps) * sizes.plane + here
    first_bead = block * 128
    low = jnp.zeros((slots, 128), jnp.int32)
    high = jnp.full((slots, 128), sizes.blocks * 128)
    edges_ref[...] = jnp.zeros_like(edges_ref)
    end = jnp.int32(0)
    for k in range(lengths_ref.shape[0]):
        start = end
        end = end + lengths_ref[k]
        edges_ref[0, k : k + 1] = jnp.full((1, 128), start)
        edges_ref[1, k : k + 1] = jnp.full((1, 128), end)
        low = jnp.maximum(low, jnp.where(start <= first_bead, start, 0))
        high = jnp.minimum(high, jnp.where(end > first_bead + 127, end, sizes.blocks * 128))
    low = jnp.maximum(low >> 7, block - (sizes.width - 1))
    high = jnp.minimum(jnp.minimum((high - 1) >> 7, block + (sizes.width - 1)), sizes.blocks - 1)
    in_band = (high - low + 2) >> 1
    begin = below(in_band.astype(jnp.float32)).astype(jnp.int32)
    band_total = jnp.max(begin + in_band)
    chunks = sizes.band_chunks

    def band(chunk, carry):
        pair = chunk * 128 + lane
        inside = (begin <= pair) & (pair < begin + in_band)

        def pick(value):
            return jnp.sum(jnp.where(inside, value, 0), axis=0, keepdims=True)

        live = pick(1) > 0
        slot = pick(slot_row)
        near = pick(low - 2 * begin) + 2 * pair
        last = pick(high)
        here_block = pick(block)
        for i in range(2):
            second = jnp.where(live, jnp.minimum(near + i, last), 0)
            first = jnp.minimum(here_block, second)
            group = modulo(first, groups)
            line = modulo(group, sizes.plane) * sweeps + divide(first, groups)
            apart = jnp.abs(here_block - second)
            place = line * 128 + divide(group, sizes.plane) * sizes.width + apart
            state = jnp.where(live & (near + i <= last), jnp.where(apart == 0, 1, 0), 2)
            code = second + (slot << 12) + (jnp.where(live, slot, slots) << 19) + (state << 26)
            at = 2 * i * chunks + chunk
            list_ref[pl.ds(at, 1), :] = code
            list_ref[pl.ds(at + chunks, 1), :] = jnp.where(live, place, 0)
        return carry

    lax.fori_loop(0, lax.div(band_total + UNIT, 128) + 1, band, 0)
    steps = lax.div(band_total + (UNIT // 2 - 1), UNIT // 2)
    list_ref[4 * chunks : 4 * chunks + 1] = jnp.full((1, 128), steps)


def list_kernel(sizes, pairs_ref, after_ref, list_ref, digits_ref):
    slots, sweeps, groups, chunks = sizes.slots, sizes.sweeps, sizes.groups, sizes.chunks
    family = lax.div(lax.axis_index("row"), sizes.share)
    here = lax.rem(lax.axis_index("row"), sizes.share) * sizes.n_col + lax.axis_index("col")
    lane = lax.broadcasted_iota(jnp.int32, (1, 128), 1)
    slot_row = lax.broadcasted_iota(jnp.int32, (slots, 128), 0)

    half = pairs_ref.shape[2] // 128
    lines = 2 * half
    pairs = pairs_ref[family]
    group = modulo(pairs, groups)
    mine = modulo(group, sizes.plane) == here
    slot = jnp.where(mine, divide(group, sizes.plane) * sweeps + divide(pairs, groups), -1)
    other = pairs

    def cut(value, line):
        side, at = line // half, line % half * 128
        return value[side : side + 1, at : at + 128]

    before = lax.broadcasted_iota(jnp.int32, (128, 256), 0)
    after = lax.broadcasted_iota(jnp.int32, (128, 256), 1)
    count = (before <= after).astype(jnp.float32).astype(jnp.bfloat16)
    running = jnp.zeros((slots, 128), jnp.float32)
    picked = []
    for line in range(lines):
        chosen = (cut(slot, line) == slot_row).astype(jnp.float32)
        counted = jnp.dot(chosen.astype(jnp.bfloat16), count, preferred_element_type=jnp.float32)
        inner = jnp.sum(chosen * (counted[:, :128] - 1.0 + running), axis=0, keepdims=True)
        picked.append((chosen, inner))
        running = running + counted[:, 128:]
    doubled = 2.0 * jnp.floor(0.5 * (running + 1.0))
    base = below(doubled)
    number = jnp.max(base + doubled).astype(jnp.int32)
    digit_row = lax.broadcasted_iota(jnp.int32, (POINT_ROWS, 128), 0)
    ranks = []
    for line in range(lines):
        chosen, inner = picked[line]
        rank = inner + jnp.sum(chosen * base, axis=0, keepdims=True)
        ranks.append(jnp.where(cut(slot, line) >= 0, rank.astype(jnp.int32), -1))
        opposite = (line + half) % lines
        partner = cut(other, opposite)
        digits = jnp.zeros((POINT_ROWS, 128), jnp.int32)
        for place, digit in enumerate(
            (partner & 31, partner >> 5, cut(slot, line), lane, line % half + 0 * lane, 1 + 0 * lane)
        ):
            digits = jnp.where(digit_row == place, digit, digits)
        digits_ref[line] = digits.astype(jnp.float32).astype(jnp.bfloat16)
    spot = lax.broadcasted_iota(jnp.int32, (128, 128), 0)

    def compact(chunk, carry):
        found = jnp.zeros((POINT_ROWS, 128), jnp.float32)
        for line in range(0, lines, 2):
            there = jnp.concatenate(
                [(ranks[line + i] == spot + chunk * 128).astype(jnp.float32).astype(jnp.bfloat16) for i in range(2)],
                axis=1,
            )
            found = found + lax.dot_general(
                jnp.concatenate([digits_ref[line], digits_ref[line + 1]], axis=1),
                there,
                (((1,), (1,)), ((), ())),
                preferred_element_type=jnp.float32,
            )
        found = found.astype(jnp.int32)
        at = found[2:3]
        code = found[0:1] + (found[1:2] << 5) + ((slots + at) << 12) + (at << 19)
        list_ref[pl.ds(chunk, 1), :] = jnp.where(found[5:6] > 0, code, (slots << 19) + (2 << 26))
        list_ref[pl.ds(chunks + chunk, 1), :] = (
            sizes.plane * sweeps * 128 + found[3:4] + found[4:5] * 128
        )
        return carry

    lax.fori_loop(0, lax.div(number + 2 * UNIT - 1, 128) + 1, compact, 0)
    list_ref[2 * chunks : 2 * chunks + 1] = jnp.full((1, 128), number)


def own_kernel(sizes, edges_ref, own_ref, first_ref, marks_ref):
    slots, sweeps, groups = sizes.slots, sizes.sweeps, sizes.groups
    family = lax.div(lax.axis_index("row"), sizes.share)
    here = lax.rem(lax.axis_index("row"), sizes.share) * sizes.n_col + lax.axis_index("col")
    lane = lax.broadcasted_iota(jnp.int32, (1, 128), 1)
    row = lax.broadcasted_iota(jnp.int32, (8, 128), 0)
    labels = edges_ref.shape[1]
    depth = POINT_ROWS + labels

    def mark(group, carry):
        for u in range(sweeps):
            bead = (u * groups + group) * 128 + lane
            inside = (bead >= edges_ref[0]) & (bead < edges_ref[1])
            marks_ref[u * groups + group] = inside.astype(jnp.float32).astype(jnp.bfloat16)
        return carry

    lax.fori_loop(0, groups, mark, 0)

    def fill(turn, carry):
        origin = lax.rem(family + (sizes.structures - turn), sizes.structures)
        for pair in range(sweeps // 2):
            value = own_ref[pl.ds(pl.multiple_of(turn * sweeps * 4 + pair * 8, 8), 8), :]
            for odd in range(2):
                value = pltpu.roll(value, 4, 0) if odd else value
                high = rounded(value)
                low = rounded(value - high)
                shifted = value + 0.5 * CONTACT_SHIFT
                shifted_high = rounded(shifted)
                shifted_low = rounded(shifted - shifted_high)
                both = jnp.where(row < 4, high, pltpu.roll(high, 4, 0))
                near = jnp.where((row & 3) == 3, 1.0, CONTACT_SLOPE * both)
                rest = jnp.where(row == 4, pltpu.roll(shifted_low, 1, 0), 0.0)
                rest = jnp.where(row == 3, shifted_high, rest)
                rest = jnp.where(row < 3, CONTACT_SLOPE * low, rest)
                u = 2 * pair + odd
                bead = (u * groups + origin * sizes.plane + here) * 128 + lane
                inside = (bead >= edges_ref[0]) & (bead < edges_ref[1])
                apart = jnp.where(inside, 0.0, -FAR)
                blank = jnp.zeros((128 - depth, 128), jnp.float32)
                turned = jnp.transpose(jnp.concatenate([near, rest, apart, blank], axis=0))
                slot = origin * sweeps + u
                first_ref[slot] = turned[:, :depth].astype(jnp.bfloat16)
                other = jnp.where(lane < POINT_ROWS, turned, -FAR - turned)
                first_ref[slots + slot] = other[:, :depth].astype(jnp.bfloat16)
        return carry

    lax.fori_loop(0, sizes.structures, fill, 0)


def tile_kernel(sizes, band_ref, list_ref, listed_ref, first_ref, marks_ref, same_ref, across_ref, *refs):
    structures, sweeps, slots, groups = sizes.structures, sizes.sweeps, sizes.slots, sizes.groups
    out_refs = refs[:structures]
    second_ref, counts_ref, held_ref, sums_ref, picks_ref, state_ref, total_ref, gain_ref = refs[structures:]
    row_here = lax.axis_index("row")
    column_here = lax.axis_index("col")
    family = lax.div(row_here, sizes.share)
    chip_here = lax.rem(row_here, sizes.share) * sizes.half + lax.div(column_here, 2)
    core_here = lax.rem(column_here, 2)
    lane = lax.broadcasted_iota(jnp.int32, (1, 128), 1)
    row = lax.broadcasted_iota(jnp.int32, (8, 128), 0)
    ones = jnp.where((row == 3) | (row == 4), 1.0, 0.0)
    narrow = lax.broadcasted_iota(jnp.int32, (1, 2 * POINT_ROWS), 1)

    for core, piece_ref in ((core_here, same_ref), (1 - core_here, across_ref)):
        for k in range(sizes.chips):
            chip = lax.rem(chip_here + (sizes.chips - k), sizes.chips)
            device = chip * 2 + core
            base = k * sizes.rows
            counts_ref[pl.ds(pl.multiple_of(device * sweeps, sweeps), sweeps), :] = piece_ref[
                base + slots * 4 : base + slots * 4 + sweeps
            ]
            for turn in range(structures):
                origin = lax.rem(family + (structures - turn), structures)
                group = origin * sizes.plane + device
                for pair in range(sweeps // 2):
                    start = base + turn * sweeps * 4 + pair * 8
                    value = piece_ref[start : start + 8]
                    high = rounded(value)
                    low = value - high
                    high_turned = pltpu.roll(high, 4, 0)
                    for odd, (top, bottom) in enumerate(
                        ((high, pltpu.roll(low, 4, 0)), (high_turned, low))
                    ):
                        points = jnp.where(row < 4, top, bottom)
                        features = jnp.concatenate([points, jnp.where(row < 3, top, ones)], axis=0)
                        second_ref[(2 * pair + odd) * groups + group] = features.astype(jnp.bfloat16)
    listed_base = sizes.plane * sweeps
    chosen = lax.broadcasted_iota(jnp.int32, (structures, 128), 0) == family
    for k in range(listed_ref.shape[1] // 128):
        line = jnp.where(chosen, listed_ref[:, k * 128 : (k + 1) * 128], 0)
        counts_ref[listed_base + k : listed_base + k + 1] = jnp.sum(line, axis=0, keepdims=True).astype(
            jnp.float32
        )
    chunks, band_chunks = sizes.chunks, sizes.band_chunks

    total_ref[...] = jnp.zeros_like(total_ref)
    spare = 1.0 / (1.0 + jnp.exp(jnp.float32(-CONTACT_SHIFT)))

    def step(ending, beginning=None):
        sums = sums_ref[pl.ds(0, UNIT, stride=8), :]
        for k in range(1, 8):
            sums = sums + sums_ref[pl.ds(k, UNIT, stride=8), :]
        chance = 64.0 * 128.0 + 0.5 * jnp.sum(sums, axis=1, keepdims=True)
        count = jnp.sum(picks_ref[...], axis=1, keepdims=True)
        state = state_ref[...]
        chance = jnp.where(state == 1, 0.5 * (chance - 128.0 * spare), chance)
        weight = jnp.where(state == 2, 0.0, 1.0 - count / (BACKGROUND + chance / 128.0))
        for t in range(0, UNIT, 2):
            left, right = (second_ref[ending[t + i] & 4095] for i in range(2))
            blank = jnp.zeros_like(left)
            both = jnp.concatenate(
                [jnp.concatenate([left, blank], axis=1), jnp.concatenate([blank, right], axis=1)], axis=0
            )
            product = lax.dot_general(
                held_ref[t // 2], both, (((1,), (1,)), ((), ())), preferred_element_type=jnp.float32
            )
            scale = jnp.where(
                narrow < POINT_ROWS,
                weight[t : t + 1, : 2 * POINT_ROWS],
                weight[t + 1 : t + 2, : 2 * POINT_ROWS],
            )
            total_ref[(ending[t] >> 19) & 127] += scale * product
            if beginning is None:
                continue
            seconds = [beginning[t + i][0] & 4095 for i in range(2)]
            logit = jnp.dot(
                first_ref[(beginning[t][0] >> 12) & 127],
                jnp.concatenate(
                    [jnp.concatenate([second_ref[at], marks_ref[at]], axis=0) for at in seconds], axis=1
                ),
                preferred_element_type=jnp.float32,
            )
            bend = jnp.tanh(logit)
            held_ref[t // 2] = (1.0 - bend * bend).astype(jnp.bfloat16)
            for i in range(2):
                part = bend[:, i * 128 : (i + 1) * 128]
                sums_ref[(t + i) * 8 : (t + i + 1) * 8] = jnp.sum(part.reshape(16, 8, 128), axis=0)
                code, place = beginning[t + i]
                picked = counts_ref[pl.ds(place >> 7, 1), :]
                picks_ref[t + i : t + i + 1] = jnp.where(lane == (place & 127), picked, 0.0)
                state_ref[t + i : t + i + 1] = jnp.full((1, 128), code >> 26)
        return beginning and tuple(code for code, _ in beginning)

    def band_step(turn, ending):
        line = turn * (UNIT // 2) >> 7
        at = turn * (UNIT // 2) & 127
        beginning = []
        for t in range(UNIT):
            row = line + t % 2 * 2 * band_chunks
            beginning.append((band_ref[row, at + t // 2], band_ref[row + band_chunks, at + t // 2]))
        return step(ending, beginning)

    def listed_step(turn, ending):
        line = turn * UNIT >> 7
        at = turn * UNIT & 127
        beginning = [(list_ref[line, at + t], list_ref[chunks + line, at + t]) for t in range(UNIT)]
        return step(ending, beginning)

    idle = (jnp.int32(slots << 19),) * UNIT
    sums_ref[...] = jnp.zeros_like(sums_ref)
    ending = lax.fori_loop(0, band_ref[4 * band_chunks, 0], band_step, idle)
    listed_steps = lax.div(list_ref[2 * chunks, 0] + UNIT - 1, UNIT)
    step(lax.fori_loop(0, listed_steps, listed_step, ending))

    def collect(slot, carry):
        turned = jnp.transpose(total_ref[slot])
        gain_ref[pl.ds(pl.multiple_of(slot * POINT_ROWS, POINT_ROWS), POINT_ROWS), :] = (
            turned[:POINT_ROWS] + turned[POINT_ROWS:]
        )
        return carry

    lax.fori_loop(0, slots, collect, 0, unroll=8)
    scale = -2.0 * CONTACT_SLOPE / 128.0 / 4.0
    for k in range(structures):
        origin = lax.rem(family + k, structures)
        turn = (structures - k) % structures
        first = origin * sweeps * POINT_ROWS
        mass = gain_ref[pl.ds(first + 11, sweeps, stride=POINT_ROWS), :]
        for place in range(3):
            point = same_ref[pl.ds(turn * sweeps * 4 + place, sweeps, stride=4), :]
            high = rounded(point)
            near = high + rounded(point - high)
            pull = (
                gain_ref[pl.ds(first + place, sweeps, stride=POINT_ROWS), :]
                + gain_ref[pl.ds(first + place + 4, sweeps, stride=POINT_ROWS), :]
            )
            out_refs[k][place] = scale * (near * mass - pull)


def place_kernel(sizes, *refs):
    family = lax.div(lax.axis_index("row"), sizes.share)
    for k, ref in enumerate(refs[:-1]):
        refs[-1][lax.rem(family + (sizes.structures - k), sizes.structures)] = ref[...]


def on_device(n_row, n_col, coords, chrom_lengths, band_counts, inter_pairs, inter_counts):
    structures, _, sweeps, block_size = coords.shape
    width = band_counts.shape[3]
    listed = inter_pairs.shape[1]
    sizes = Sizes(n_row, n_col, structures, sweeps, width, listed)
    share, slots, blocks = sizes.share, sizes.slots, sizes.blocks

    messages = pl.pallas_call(
        functools.partial(pack_kernel, sizes),
        out_shape=[jax.ShapeDtypeStruct((5 * sweeps, block_size), jnp.float32)] * structures,
        in_specs=[VMEM, VMEM],
        out_specs=[VMEM] * structures,
        compiler_params=SMALL,
        name="pack",
    )(coords, band_counts)
    deal = [
        [(i, (i // share + k) % structures * share + i % share) for i in range(n_row)]
        for k in range(structures)
    ]
    received = [messages[0]]
    for k in range(1, structures):
        received.append(lax.ppermute(messages[k], "row", deal[k]))
    labels = -(-chrom_lengths.shape[0] // 16) * 16
    band, edges = pl.pallas_call(
        functools.partial(band_kernel, sizes),
        out_shape=[
            jax.ShapeDtypeStruct((4 * sizes.band_chunks + 8, block_size), jnp.int32),
            jax.ShapeDtypeStruct((2, labels, block_size), jnp.int32),
        ],
        in_specs=[SMEM],
        out_specs=[VMEM] * 2,
        compiler_params=SMALL,
        name="band_tiles",
    )(chrom_lengths)

    own_row = pl.pallas_call(
        functools.partial(merge_kernel, 4 * sweeps),
        out_shape=jax.ShapeDtypeStruct((sizes.rows, block_size), jnp.float32),
        in_specs=[ANY] + [VMEM] * structures,
        out_specs=VMEM,
        compiler_params=SMALL,
        name="merge",
    )(band, *received)

    def device(family, chip, core):
        row = family * share + chip // sizes.half
        return row * n_col + chip % sizes.half * 2 + core

    pieces = [own_row]
    for k in range(1, sizes.chips):
        moves = [
            (device(f, i, core), device(f, (i + k) % sizes.chips, core))
            for f in range(structures)
            for i in range(sizes.chips)
            for core in range(2)
        ]
        pieces.append(lax.ppermute(own_row, AXES, moves))
    depth = POINT_ROWS + labels
    own, marks = pl.pallas_call(
        functools.partial(own_kernel, sizes),
        out_shape=[
            jax.ShapeDtypeStruct((2 * slots, block_size, depth), jnp.bfloat16),
            jax.ShapeDtypeStruct((blocks, labels, block_size), jnp.bfloat16),
        ],
        in_specs=[VMEM, VMEM],
        out_specs=[VMEM] * 2,
        compiler_params=pltpu.CompilerParams(vmem_limit_bytes=24 * 1024 * 1024),
        name="own_features",
    )(edges, own_row)

    same = pl.pallas_call(
        join_kernel,
        out_shape=jax.ShapeDtypeStruct((sizes.chips * sizes.rows, block_size), jnp.float32),
        in_specs=[ANY] + [VMEM] * sizes.chips,
        out_specs=VMEM,
        compiler_params=SMALL,
        name="join",
    )(marks, *pieces)
    across = lax.ppermute(same, "col", [(i, i ^ 1) for i in range(n_col)])

    tiles = pl.pallas_call(
        functools.partial(list_kernel, sizes),
        out_shape=jax.ShapeDtypeStruct((2 * sizes.chunks + 8, block_size), jnp.int32),
        in_specs=[VMEM, ANY],
        out_specs=VMEM,
        scratch_shapes=[pltpu.VMEM((2 * listed // block_size, POINT_ROWS, block_size), jnp.bfloat16)],
        cost_estimate=pl.CostEstimate(flops=1 << 28, bytes_accessed=1 << 22, transcendentals=0),
        compiler_params=SMALL,
        name="list_tiles",
    )(jnp.transpose(inter_pairs, (0, 2, 1)), same)

    gains = pl.pallas_call(
        functools.partial(tile_kernel, sizes),
        out_shape=[jax.ShapeDtypeStruct((3, sweeps, block_size), jnp.float32)] * structures,
        in_specs=[SMEM] * 2 + [VMEM] * 5,
        out_specs=[VMEM] * structures,
        scratch_shapes=[
            pltpu.VMEM((blocks, POINT_ROWS, block_size), jnp.bfloat16),
            pltpu.VMEM((sizes.plane * sweeps + listed // block_size, block_size), jnp.float32),
            pltpu.VMEM((UNIT // 2, block_size, 2 * block_size), jnp.bfloat16),
            pltpu.VMEM((UNIT * 8, block_size), jnp.float32),
            pltpu.VMEM((UNIT, block_size), jnp.float32),
            pltpu.VMEM((UNIT, block_size), jnp.int32),
            pltpu.VMEM((slots + 1, block_size, 2 * POINT_ROWS), jnp.float32),
            pltpu.VMEM((slots * POINT_ROWS, block_size), jnp.float32),
        ],
        compiler_params=pltpu.CompilerParams(vmem_limit_bytes=40 * 1024 * 1024),
        name="tiles",
    )(band, tiles, inter_counts, own, marks, same, across)

    arrived = [gains[0]]
    for k in range(1, structures):
        arrived.append(lax.ppermute(gains[k], "row", deal[k]))
    return pl.pallas_call(
        functools.partial(place_kernel, sizes),
        out_shape=jax.ShapeDtypeStruct(coords.shape, jnp.float32),
        in_specs=[VMEM] * structures,
        out_specs=VMEM,
        compiler_params=SMALL,
        name="place",
    )(*arrived)


def solution(mesh):
    placed = (
        P(None, None, None, ("row", "col")),
        P(),
        P(None, None, ("row", "col"), None),
        P(),
        P(),
    )
    return jax.shard_map(
        functools.partial(on_device, mesh.shape["row"], mesh.shape["col"]),
        mesh=mesh,
        in_specs=placed,
        out_specs=P(None, None, None, ("row", "col")),
        check_vma=False,
    )
```
